32 devices in a mesh: dp: 16 (over z, x, core), shard: 2 (over y).
Axes of the slice: x: 2, y: 2, z: 4, core: 2. Of those that a mesh axis runs over, the one named last changes fastest.
Arguments:
- tokens: bfloat16 [32768, 768], P(('dp', 'shard')), may hold values from -2.5 to 2.5
- cotangent: bfloat16 [32768, 768], P(('dp', 'shard')), may hold values from -2.5 to 2.5
- master_qkv: float32 [768, 2304], P('shard'), may hold values from -0.21875 to 0.21875
- first_qkv: float32 [768, 2304], P('shard'), may hold values from -2.5 to 2.5
- second_qkv: float32 [768, 2304], P('shard'), may hold values from 0.25 to 4
- master_out: float32 [768, 768], P('shard'), may hold values from -0.875 to 0.875
- first_out: float32 [768, 768], P('shard'), may hold values from -2.5 to 2.5
- second_out: float32 [768, 768], P('shard'), may hold values from 0.01 to 0.16
- master_gate_up: float32 [768, 6144], P('shard'), may hold values from -0.21875 to 0.21875
- first_gate_up: float32 [768, 6144], P('shard'), may hold values from -2.5 to 2.5
- second_gate_up: float32 [768, 6144], P('shard'), may hold values from 0.02 to 0.32
- master_down: float32 [3072, 768], P('shard'), may hold values from -0.109375 to 0.109375
- first_down: float32 [3072, 768], P('shard'), may hold values from -2.5 to 2.5
- second_down: float32 [3072, 768], P('shard'), may hold values from 0.25 to 4
- norms: float32 [4, 768], replicated, may hold values from -2.5 to 2.5, as said below
- norm_first: float32 [4, 768], replicated, may hold values from -2.5 to 2.5
- norm_second: float32 [4, 768], replicated, may hold values from 0.25 to 4
Outputs:
- output: bfloat16 [32768, 768], P(('dp', 'shard'))
- input_grad: bfloat16 [32768, 768], P(('dp', 'shard'))
- new_qkv: bfloat16 [768, 2304], replicated
- new_out: bfloat16 [768, 768], replicated
- new_gate_up: bfloat16 [768, 6144], replicated
- new_down: bfloat16 [3072, 768], replicated
- next_first_qkv: float32 [768, 2304], P('shard')
- next_second_qkv: float32 [768, 2304], P('shard')
- next_first_out: float32 [768, 768], P('shard')
- next_second_out: float32 [768, 768], P('shard')
- next_first_gate_up: float32 [768, 6144], P('shard')
- next_second_gate_up: float32 [768, 6144], P('shard')
- next_first_down: float32 [3072, 768], P('shard')
- next_second_down: float32 [3072, 768], P('shard')
- new_norms: float32 [4, 768], replicated
- next_norm_first: float32 [4, 768], replicated
- next_norm_second: float32 [4, 768], replicated
The draws below stay inside these ranges and needn't reach their ends.
Inputs may be any that keep to these rules, and one draw needn't show every extreme that they name: Rows 0 and 2 of norms are gains near 1, rows 1 and 3 biases.
All inputs are finite; a program needn't handle non-finite values.
Results may differ from the reference program's by a relative error of at most 0.018.
Values may be sent and summed in bfloat16 or wider, within the bound.
A program may use at most 320 MiB of HBM per device.

```python
import math
import jax
import jax.numpy as jnp
from jax import lax

D = 768
HEADS = 12
HEAD_DIM = 64
FF = 3072
SEQ_LEN = 1024
STEP = 3
TOKENS = 32768


def draw_norms(key, part):
    key = jax.random.fold_in(key, 11)
    noise = jax.random.normal(key, (4, D), jnp.float32)
    parity = jnp.arange(4)[:, None] % 2
    return jnp.where(parity == 0, 1.0 + 0.1 * noise, 0.3 * noise)


def block_levels(own_key, dims, cuts, least, high):
    loudness, own = 1.0, jax.random.fold_in(own_key, 6)
    for dim, parts in cuts:
        steps = jnp.exp(jax.random.uniform(jax.random.fold_in(own, dim), (parts,), jnp.float32, least / len(cuts), high / len(cuts)))
        loudness = loudness * jnp.repeat(steps, dims[dim] // parts).reshape([-1 if axis == dim else 1 for axis in range(len(dims))])
    return loudness


def normal_values(rng, dims, deviation, limit, pieces=(), kind=jnp.bfloat16):
    entries = deviation * jax.random.normal(rng, dims, jnp.float32)
    if pieces:
        entries = entries * block_levels(rng, dims, pieces, -0.22, 0.18)
    return jnp.clip(entries, -limit, limit).astype(kind)


def setup_inputs(seed: int = 0) -> dict:
    keys = jax.random.split(jax.random.key(seed), 18)
    tokens = normal_values(keys[0], (TOKENS, D), 1.0, 2.5, ((0, 32),))
    cotangent = normal_values(keys[1], (TOKENS, D), 1.0, 2.5, ((0, 32),))
    master_qkv = normal_values(keys[2], (D, 3 * D), D ** -0.5, 0.21875, ((0, 2),), jnp.float32)
    first_qkv = normal_values(keys[3], (D, 3 * D), 1.0, 2.5, ((0, 2),), jnp.float32)
    second_qkv = jnp.clip(jnp.exp(math.log(4.0) - 2.7725887 * jax.random.uniform(keys[4], (D, 3 * D), jnp.float32) ** block_levels(keys[4], (D, 3 * D), ((0, 2),), -0.2, 0.2)), 0.25, 4.0)
    master_out = normal_values(keys[5], (D, D), (D // 16) ** -0.5, 0.875, ((0, 2),), jnp.float32)
    first_out = normal_values(keys[6], (D, D), 1.0, 2.5, ((0, 2),), jnp.float32)
    second_out = jnp.clip(jnp.exp(math.log(0.16) - 2.7725887 * jax.random.uniform(keys[7], (D, D), jnp.float32) ** block_levels(keys[7], (D, D), ((0, 2),), -0.2, 0.2)), 0.01, 0.16)
    master_gate_up = normal_values(keys[8], (D, 2 * FF), D ** -0.5, 0.21875, ((0, 2),), jnp.float32)
    first_gate_up = normal_values(keys[9], (D, 2 * FF), 1.0, 2.5, ((0, 2),), jnp.float32)
    second_gate_up = jnp.clip(jnp.exp(math.log(0.32) - 2.7725887 * jax.random.uniform(keys[10], (D, 2 * FF), jnp.float32) ** block_levels(keys[10], (D, 2 * FF), ((0, 2),), -0.2, 0.2)), 0.02, 0.32)
    master_down = normal_values(keys[11], (FF, D), FF ** -0.5, 0.109375, ((0, 2),), jnp.float32)
    first_down = normal_values(keys[12], (FF, D), 1.0, 2.5, ((0, 2),), jnp.float32)
    second_down = jnp.clip(jnp.exp(math.log(4.0) - 2.7725887 * jax.random.uniform(keys[13], (FF, D), jnp.float32) ** block_levels(keys[13], (FF, D), ((0, 2),), -0.2, 0.2)), 0.25, 4.0)
    norms = draw_norms(jax.random.fold_in(keys[17], 71), 0)
    norm_first = normal_values(keys[15], (4, D), 1.0, 2.5, (), jnp.float32)
    norm_second = jnp.clip(jnp.exp(jax.random.uniform(keys[16], (4, D), jnp.float32, math.log(0.25), math.log(4.0))), 0.25, 4.0)
    return dict(tokens=tokens, cotangent=cotangent, master_qkv=master_qkv, first_qkv=first_qkv, second_qkv=second_qkv, master_out=master_out, first_out=first_out, second_out=second_out, master_gate_up=master_gate_up, first_gate_up=first_gate_up, second_gate_up=second_gate_up, master_down=master_down, first_down=first_down, second_down=second_down, norms=norms, norm_first=norm_first, norm_second=norm_second)


@jax.custom_vjp
def low(v):
    return lax.optimization_barrier(v.astype(jnp.bfloat16)).astype(jnp.float32)

@jax.custom_vjp
def low_back(v):
    return v

def low_keep(v):
    return (low(v), None)

def low_pass(kept, grad):
    return (grad,)

def back_keep(v):
    return (v, None)

def back_low(kept, grad):
    return (low(grad),)
low.defvjp(low_keep, low_pass)
low_back.defvjp(back_keep, back_low)
norm_eps = 1e-12
rope_base = 1000.0
learn_rate = 0.03
norm_rate = 0.3
decay_rate = 0.1
adam_eps = 1e-08
beta_first = 0.5
beta_second = 0.5

def rope_tables(length, head_width):
    half_width = head_width // 2
    frequency = rope_base ** (-(jnp.arange(half_width, dtype=jnp.float32) * (2.0 / head_width)))
    angles = jnp.arange(length, dtype=jnp.float32)[:, None] * frequency[None, :]
    angles = jnp.concatenate([angles, angles], axis=1)
    return (jnp.cos(angles), jnp.sin(angles))

def turn_half(vectors):
    half_width = vectors.shape[-1] // 2
    return jnp.concatenate([-vectors[..., half_width:], vectors[..., :half_width]], axis=-1)

def rotate(vectors, cosine, sine_table):
    return vectors * cosine[:, None, :] + turn_half(vectors) * sine_table[:, None, :]

def layer_norm(values, gain_row, bias_row):
    centred = values - lax.optimization_barrier(jnp.mean(values, axis=-1, keepdims=True))
    inverse = lax.rsqrt(lax.optimization_barrier(jnp.mean(centred * centred, axis=-1, keepdims=True)) + norm_eps)
    return centred * inverse * gain_row + bias_row

def one_sequence(inputs, w_qkv, w_out, w_gate_up, w_down, norm_rows):
    highest = lax.Precision.HIGHEST
    length = inputs.shape[0]
    cosine, sine_table = rope_tables(length, HEAD_DIM)
    joined_rows = low_back(jnp.dot(inputs, w_qkv, precision=highest)).reshape(length, 3, HEADS, HEAD_DIM)
    queries = low(rotate(joined_rows[:, 0], cosine, sine_table) * (1.0 / math.sqrt(HEAD_DIM)))
    key_rows = low(rotate(joined_rows[:, 1], cosine, sine_table))
    value_rows = low(joined_rows[:, 2])
    scores = low_back(jnp.einsum('qhd,khd->hqk', queries, key_rows, precision=highest))
    weights_soft = low(jax.nn.softmax(scores, axis=-1))
    mixed_rows = jnp.einsum('hqk,khd->qhd', weights_soft, value_rows, precision=highest).reshape(length, HEADS * HEAD_DIM)
    mixed_rows = low(low_back(mixed_rows))
    branch_one = low_back(jnp.dot(mixed_rows, w_out, precision=highest))
    hidden = layer_norm(inputs + branch_one, norm_rows[0], norm_rows[1])
    gate_up = low_back(jnp.dot(low(hidden), w_gate_up, precision=highest))
    gate_part = gate_up[:, :FF]
    up_part = gate_up[:, FF:]
    inner_rows = low(jax.nn.silu(gate_part) * up_part)
    branch_two = low_back(jnp.dot(inner_rows, w_down, precision=highest))
    return layer_norm(hidden + branch_two, norm_rows[2], norm_rows[3])

def adam_update(weight, first_moment, second_moment, gradient, rate, decay_on):
    first_new = beta_first * first_moment + (1.0 - beta_first) * gradient
    second_new = beta_second * second_moment + (1.0 - beta_second) * gradient * gradient
    fix_first = 1.0 - beta_first ** STEP
    fix_second = 1.0 - beta_second ** STEP
    direction = first_new / fix_first / (jnp.sqrt(second_new / fix_second) + adam_eps)
    return (weight - rate * (direction + decay_on * weight), first_new, second_new)

def reference(tokens, cotangent, master_qkv, first_qkv, second_qkv, master_out, first_out, second_out, master_gate_up, first_gate_up, second_gate_up, master_down, first_down, second_down, norms, norm_first, norm_second):
    round_qkv = master_qkv.astype(jnp.bfloat16).astype(jnp.float32)
    round_out = master_out.astype(jnp.bfloat16).astype(jnp.float32)
    round_gate_up = master_gate_up.astype(jnp.bfloat16).astype(jnp.float32)
    round_down = master_down.astype(jnp.bfloat16).astype(jnp.float32)
    inputs = tokens.astype(jnp.float32).reshape(TOKENS // SEQ_LEN, SEQ_LEN, D)

    def forward(stacked, w_qkv, w_out, w_gate_up, w_down, norm_rows):

        def sequence_fn(single):
            return one_sequence(single, w_qkv, w_out, w_gate_up, w_down, norm_rows)
        return lax.map(jax.checkpoint(sequence_fn), stacked)
    outputs, pullback = jax.vjp(forward, inputs, round_qkv, round_out, round_gate_up, round_down, norms)
    grads = pullback(cotangent.astype(jnp.float32).reshape(inputs.shape))
    scale_grad = 1.0 / math.sqrt(TOKENS)
    upd_qkv, first_qkv_new, second_qkv_new = adam_update(master_qkv, first_qkv, second_qkv, grads[1] * scale_grad, learn_rate, decay_rate)
    upd_out, first_out_new, second_out_new = adam_update(master_out, first_out, second_out, grads[2] * scale_grad, learn_rate, decay_rate)
    upd_gate_up, first_gate_up_new, second_gate_up_new = adam_update(master_gate_up, first_gate_up, second_gate_up, grads[3] * scale_grad, learn_rate, decay_rate)
    upd_down, first_down_new, second_down_new = adam_update(master_down, first_down, second_down, grads[4] * scale_grad, learn_rate, decay_rate)
    upd_norms, norm_first_new, norm_second_new = adam_update(norms, norm_first, norm_second, grads[5] * scale_grad, norm_rate, 0.0)
    return (outputs.reshape(TOKENS, D).astype(jnp.bfloat16), grads[0].reshape(TOKENS, D).astype(jnp.bfloat16), upd_qkv.astype(jnp.bfloat16), upd_out.astype(jnp.bfloat16), upd_gate_up.astype(jnp.bfloat16), upd_down.astype(jnp.bfloat16), first_qkv_new, second_qkv_new, first_out_new, second_out_new, first_gate_up_new, second_gate_up_new, first_down_new, second_down_new, upd_norms, norm_first_new, norm_second_new)
```

```python
import functools
import math

import jax
import jax.numpy as jnp
import numpy as np
from jax import lax
from jax.experimental import pallas as pl
from jax.experimental.pallas import tpu as pltpu
from jax.sharding import PartitionSpec as P

HEADS = 12
HEAD_DIM = 64
STEP = 3

norm_eps = 1e-12
rope_base = 1000.0
learn_rate = 0.03
norm_rate = 0.3
decay_rate = 0.1
adam_eps = 1e-08
beta_first = 0.5
beta_second = 0.5

f32, bf16 = jnp.float32, jnp.bfloat16
VMEM_BYTES = 56 * 2**20


def contract(left, right, left_dim, right_dim):
    return lax.dot_general(
        left, right, (((left_dim,), (right_dim,)), ((), ())), preferred_element_type=f32
    )


def params(**more):
    return pltpu.CompilerParams(vmem_limit_bytes=VMEM_BYTES, **more)


def cost(flops, moved, transcendentals=0):
    return pl.CostEstimate(
        flops=int(flops), bytes_accessed=int(moved), transcendentals=int(transcendentals)
    )


def whole(*shape):
    return pl.BlockSpec(shape, lambda *_: (0,) * len(shape))


def rope_tables(length):
    half = HEAD_DIM // 2
    frequency = np.float32(rope_base) ** (
        -(np.arange(half, dtype=np.float32) * np.float32(2.0 / HEAD_DIM))
    )
    angles = np.arange(length, dtype=np.float32)[None, :] * frequency[:, None]
    return jnp.asarray(np.cos(angles), f32), jnp.asarray(np.sin(angles), f32)


def qkv_kernel(blocks_rotated, heads_block, tokens, weight, cosine, sine, joined):
    step = pl.program_id(0)
    rows = contract(weight[...], tokens[...], 0, 1)
    half = HEAD_DIM // 2

    @pl.when(step < 2 * blocks_rotated)
    def _():
        scale = jnp.where(step < blocks_rotated, 1.0 / math.sqrt(HEAD_DIM), 1.0)
        cos, sin = cosine[...] * scale, sine[...] * scale
        for head in range(heads_block):
            low = head * HEAD_DIM
            t1, t2 = rows[low : low + half], rows[low + half : low + 2 * half]
            joined[low : low + half] = (t1 * cos - t2 * sin).astype(bf16)
            joined[low + half : low + 2 * half] = (t2 * cos + t1 * sin).astype(bf16)

    @pl.when(step >= 2 * blocks_rotated)
    def _():
        joined[...] = rows.astype(bf16)


def project_qkv(tokens, weight, cosine, sine):
    length, width = tokens.shape
    heads_block = 4
    block = heads_block * HEAD_DIM
    count = weight.shape[1] // block
    return pl.pallas_call(
        functools.partial(qkv_kernel, count // 3, heads_block),
        grid=(count,),
        in_specs=[
            whole(length, width),
            pl.BlockSpec((width, block), lambda i: (0, i)),
            whole(*cosine.shape),
            whole(*sine.shape),
        ],
        out_specs=pl.BlockSpec((block, length), lambda i: (i, 0)),
        out_shape=jax.ShapeDtypeStruct((weight.shape[1], length), bf16),
        compiler_params=params(),
        cost_estimate=cost(2 * length * width * weight.shape[1], 2 * weight.size * 3),
        name="qkv_rope",
    )(tokens, weight, cosine, sine)


def attend_kernel(chunk, queries, key_rows, value_rows, mixed, weights):
    length = queries.shape[1]
    for low in range(0, length, chunk):
        span = pl.ds(low, chunk)
        scores = contract(key_rows[...], queries[:, span], 0, 0)
        highest = jnp.max(scores, axis=0, keepdims=True)
        expanded = jnp.exp(scores - highest)
        totals = jnp.sum(expanded, axis=0, keepdims=True)
        soft = (expanded * (1.0 / totals)).astype(bf16)
        weights[0, :, span] = soft
        mixed[:, span] = contract(value_rows[...], soft, 1, 0).astype(bf16)


def attend_forward(joined):
    length = joined.shape[1]
    head_rows = lambda part: pl.BlockSpec(
        (HEAD_DIM, length), lambda h: (part * HEADS + h, 0)
    )
    return pl.pallas_call(
        functools.partial(attend_kernel, min(256, length)),
        grid=(HEADS,),
        in_specs=[head_rows(0), head_rows(1), head_rows(2)],
        out_specs=[
            pl.BlockSpec((HEAD_DIM, length), lambda h: (h, 0)),
            pl.BlockSpec((1, length, length), lambda h: (h, 0, 0)),
        ],
        out_shape=[
            jax.ShapeDtypeStruct((HEADS * HEAD_DIM, length), bf16),
            jax.ShapeDtypeStruct((HEADS, length, length), bf16),
        ],
        compiler_params=params(),
        cost_estimate=cost(
            16 * HEADS * length * length * HEAD_DIM, 2 * HEADS * length * length, length * length * HEADS
        ),
        name="attend_forward",
    )(joined, joined, joined)


def attend_back_kernel(
    chunk,
    queries,
    key_rows,
    value_rows,
    mixed,
    grad_mixed,
    weights,
    cosine,
    sine,
    query_out,
    key_out,
    value_out,
):
    length = queries.shape[1]
    half = HEAD_DIM // 2
    grad = grad_mixed[...]
    centre = jnp.sum(grad.astype(f32) * mixed[...].astype(f32), axis=0, keepdims=True)
    query_grad = jnp.zeros((HEAD_DIM, length), f32)
    key_parts = []
    for low in range(0, length, chunk):
        span = pl.ds(low, chunk)
        soft = weights[0, span, :]
        weight_grad = contract(value_rows[:, span], grad, 0, 0)
        score_grad = (soft.astype(f32) * (weight_grad - centre)).astype(bf16)
        value_out[:, span] = contract(grad, soft, 1, 1).astype(bf16)
        key_parts.append(contract(queries[...], score_grad, 1, 1))
        query_grad += contract(key_rows[:, span], score_grad, 1, 0)
    key_grad = jnp.concatenate(key_parts, axis=1)
    cos, sin = cosine[...], sine[...]
    scale = 1.0 / math.sqrt(HEAD_DIM)
    for out, grad_rows, factor in ((query_out, query_grad, scale), (key_out, key_grad, 1.0)):
        d1, d2 = grad_rows[:half], grad_rows[half:]
        out[:half] = ((d1 * cos + d2 * sin) * factor).astype(bf16)
        out[half:] = ((d2 * cos - d1 * sin) * factor).astype(bf16)


def attend_backward(joined, mixed, grad_mixed, weights, cosine, sine):
    length = joined.shape[1]
    head_rows = lambda part: pl.BlockSpec(
        (HEAD_DIM, length), lambda h: (part * HEADS + h, 0)
    )
    rows = jax.ShapeDtypeStruct((HEADS * HEAD_DIM, length), bf16)
    return pl.pallas_call(
        functools.partial(attend_back_kernel, min(256, length)),
        grid=(HEADS,),
        in_specs=[
            head_rows(0),
            head_rows(1),
            head_rows(2),
            head_rows(0),
            head_rows(0),
            pl.BlockSpec((1, length, length), lambda h: (h, 0, 0)),
            whole(*cosine.shape),
            whole(*sine.shape),
        ],
        out_specs=[head_rows(0)] * 3,
        out_shape=[rows] * 3,
        compiler_params=params(),
        cost_estimate=cost(
            32 * HEADS * length * length * HEAD_DIM, 2 * HEADS * length * length
        ),
        name="attend_backward",
    )(joined, joined, joined, mixed, grad_mixed, weights, cosine, sine)


def norm_rows(values):
    centred = values - jnp.mean(values, axis=1, keepdims=True)
    inverse = lax.rsqrt(jnp.mean(centred * centred, axis=1, keepdims=True) + norm_eps)
    return centred * inverse, inverse


def norm_back(grad_rows, normed, inverse, gain_row):
    scaled = grad_rows * gain_row
    centred = (
        scaled
        - jnp.mean(scaled, axis=1, keepdims=True)
        - normed * jnp.mean(scaled * normed, axis=1, keepdims=True)
    )
    gain = jnp.sum(grad_rows * normed, axis=0, keepdims=True)
    bias = jnp.sum(grad_rows, axis=0, keepdims=True)
    return centred * inverse, gain, bias


def out_kernel(tokens, mixed, weight, norms, normed, inverse, hidden_low):
    sums = tokens[...].astype(f32) + contract(mixed[...], weight[...], 0, 0)
    rows, scale = norm_rows(sums)
    normed[...] = rows
    inverse[...] = scale
    hidden_low[...] = (rows * norms[0:1, :] + norms[1:2, :]).astype(bf16)


def project_out(tokens, mixed, weight, norms):
    length, width = tokens.shape
    block = min(256, length)
    return pl.pallas_call(
        out_kernel,
        grid=(length // block,),
        in_specs=[
            pl.BlockSpec((block, width), lambda i: (i, 0)),
            pl.BlockSpec((width, block), lambda i: (0, i)),
            whole(width, width),
            whole(*norms.shape),
        ],
        out_specs=[
            pl.BlockSpec((block, width), lambda i: (i, 0)),
            pl.BlockSpec((block, 1), lambda i: (i, 0)),
            pl.BlockSpec((block, width), lambda i: (i, 0)),
        ],
        out_shape=[
            jax.ShapeDtypeStruct((length, width), f32),
            jax.ShapeDtypeStruct((length, 1), f32),
            jax.ShapeDtypeStruct((length, width), bf16),
        ],
        compiler_params=params(),
        cost_estimate=cost(2 * length * width * width, 10 * length * width),
        name="out_norm",
    )(tokens, mixed, weight, norms)


def forward_kernel(
    rows_block,
    hidden_low,
    gate_weight,
    up_weight,
    down_weight,
    normed_one,
    norms,
    cotangent,
    gate,
    up,
    output,
    grad_second,
    grad_low,
    norm_grads,
    total,
):
    step = pl.program_id(0)
    length = hidden_low.shape[0]
    for low in range(0, length, rows_block):
        span = pl.ds(low, rows_block)
        gate_part = contract(hidden_low[span, :], gate_weight[...], 1, 0)
        up_part = contract(hidden_low[span, :], up_weight[...], 1, 0)
        gate[span, :] = gate_part
        up[span, :] = up_part
        inner = (gate_part * jax.nn.sigmoid(gate_part) * up_part).astype(bf16)
        part = contract(inner, down_weight[...], 1, 0)

        @pl.when(step == 0)
        def _():
            total[span, :] = part

        @pl.when(step > 0)
        def _():
            total[span, :] += part

    @pl.when(step == pl.num_programs(0) - 1)
    def _():
        gain_sum = jnp.zeros((1, total.shape[1]), f32)
        bias_sum = jnp.zeros((1, total.shape[1]), f32)
        for low in range(0, length, rows_block):
            span = pl.ds(low, rows_block)
            hidden = normed_one[span, :] * norms[0:1, :] + norms[1:2, :]
            rows, inverse = norm_rows(hidden + total[span, :])
            output[span, :] = (rows * norms[2:3, :] + norms[3:4, :]).astype(bf16)
            back, gain, bias = norm_back(
                cotangent[span, :].astype(f32), rows, inverse, norms[2:3, :]
            )
            grad_second[span, :] = back
            grad_low[span, :] = back.astype(bf16)
            gain_sum += gain
            bias_sum += bias
        norm_grads[0:1, :] = gain_sum
        norm_grads[1:2, :] = bias_sum


def feed_forward(hidden_low, gate_up, down, normed_one, norms, cotangent):
    length, width = hidden_low.shape
    inner = down.shape[0]
    block = min(512, inner)
    count = inner // block
    return pl.pallas_call(
        functools.partial(forward_kernel, min(256, length)),
        grid=(count,),
        in_specs=[
            whole(length, width),
            pl.BlockSpec((width, block), lambda j: (0, j)),
            pl.BlockSpec((width, block), lambda j: (0, count + j)),
            pl.BlockSpec((block, width), lambda j: (j, 0)),
            whole(length, width),
            whole(*norms.shape),
            whole(length, width),
        ],
        out_specs=[
            pl.BlockSpec((length, block), lambda j: (0, j)),
            pl.BlockSpec((length, block), lambda j: (0, j)),
            whole(length, width),
            whole(length, width),
            whole(length, width),
            whole(2, width),
        ],
        out_shape=[
            jax.ShapeDtypeStruct((length, inner), f32),
            jax.ShapeDtypeStruct((length, inner), f32),
            jax.ShapeDtypeStruct((length, width), bf16),
            jax.ShapeDtypeStruct((length, width), f32),
            jax.ShapeDtypeStruct((length, width), bf16),
            jax.ShapeDtypeStruct((2, width), f32),
        ],
        scratch_shapes=[pltpu.VMEM((length, width), f32)],
        compiler_params=params(),
        cost_estimate=cost(6 * length * width * inner, 8 * length * inner),
        name="feed_forward",
    )(hidden_low, gate_up, gate_up, down, normed_one, norms, cotangent)


def backward_kernel(
    rows_block,
    last,
    grad_low,
    hidden_low,
    gate,
    up,
    gate_weight,
    up_weight,
    down_weight,
    before,
    normed,
    inverse,
    norms,
    gate_out,
    up_out,
    down_out,
    *rest,
):
    step = pl.program_id(0)
    length = hidden_low.shape[0]
    if last:
        grad_first, first_low, norm_grads, total, inner, gate_back, up_back = rest
    else:
        grad_hidden, total, inner, gate_back, up_back = rest

    @pl.when(step == 0)
    def _():
        total[...] = before[...]

    for low in range(0, length, rows_block):
        span = pl.ds(low, rows_block)
        inner_grad = contract(grad_low[span, :], down_weight[...], 1, 1)
        gate_part, up_part = gate[span, :], up[span, :]
        sigmoid = jax.nn.sigmoid(gate_part)
        swished = gate_part * sigmoid
        inner[span, :] = (swished * up_part).astype(bf16)
        gate_grad = inner_grad * up_part * sigmoid * (1.0 + gate_part * (1.0 - sigmoid))
        gate_low, up_low = gate_grad.astype(bf16), (inner_grad * swished).astype(bf16)
        gate_back[span, :] = gate_low
        up_back[span, :] = up_low
        total[span, :] += contract(gate_low, gate_weight[...], 1, 1) + contract(
            up_low, up_weight[...], 1, 1
        )
    down_out[...] = contract(inner[...], grad_low[...], 0, 0).astype(bf16)
    gate_out[...] = contract(hidden_low[...], gate_back[...], 0, 0).astype(bf16)
    up_out[...] = contract(hidden_low[...], up_back[...], 0, 0).astype(bf16)

    @pl.when(step == pl.num_programs(0) - 1)
    def _():
        if not last:
            grad_hidden[...] = total[...]
            return
        gain_sum = jnp.zeros((1, total.shape[1]), f32)
        bias_sum = jnp.zeros((1, total.shape[1]), f32)
        for low in range(0, length, rows_block):
            span = pl.ds(low, rows_block)
            back, gain, bias = norm_back(
                total[span, :], normed[span, :], inverse[span, :], norms[0:1, :]
            )
            grad_first[span, :] = back
            first_low[span, :] = back.astype(bf16)
            gain_sum += gain
            bias_sum += bias
        norm_grads[0:1, :] = gain_sum
        norm_grads[1:2, :] = bias_sum


def feed_backward(
    piece,
    pieces,
    groups,
    grad_low,
    hidden_low,
    gate,
    up,
    gate_up,
    down,
    before,
    normed,
    inverse,
    norms,
):
    length, width = hidden_low.shape
    inner = down.shape[0]
    block = 256
    count = inner // block
    run = count // (groups * pieces)
    last = piece == pieces - 1

    def place(j):
        return (j // run) * (count // groups) + piece * run + j % run

    in_cols = lambda shift: pl.BlockSpec((width, block), lambda j: (0, shift + place(j)))
    wide = pl.BlockSpec((length, block), lambda j: (0, place(j)))
    part = inner // pieces
    outs = [
        (pl.BlockSpec((width, block), lambda j: (0, j)), jax.ShapeDtypeStruct((width, part), bf16)),
        (pl.BlockSpec((width, block), lambda j: (0, j)), jax.ShapeDtypeStruct((width, part), bf16)),
        (pl.BlockSpec((block, width), lambda j: (j, 0)), jax.ShapeDtypeStruct((part, width), bf16)),
    ]
    full = whole(length, width)
    if last:
        outs += [
            (full, jax.ShapeDtypeStruct((length, width), f32)),
            (full, jax.ShapeDtypeStruct((length, width), bf16)),
            (whole(2, width), jax.ShapeDtypeStruct((2, width), f32)),
        ]
    else:
        outs += [(full, jax.ShapeDtypeStruct((length, width), f32))]
    return pl.pallas_call(
        functools.partial(backward_kernel, min(256, length), last),
        grid=(groups * run,),
        in_specs=[
            full,
            full,
            wide,
            wide,
            in_cols(0),
            in_cols(count),
            pl.BlockSpec((block, width), lambda j: (place(j), 0)),
            full,
            full,
            whole(length, 1),
            whole(*norms.shape),
        ],
        out_specs=[spec for spec, _ in outs],
        out_shape=[shape for _, shape in outs],
        scratch_shapes=[pltpu.VMEM((length, width), f32)] + [pltpu.VMEM((length, block), bf16)] * 3,
        compiler_params=params(),
        cost_estimate=cost(12 * length * width * part, 8 * length * part),
        name="feed_backward",
    )(grad_low, hidden_low, gate, up, gate_up, gate_up, down, before, normed, inverse, norms)


class Links:
    def __init__(self, mesh):
        self.sizes = {"dp": mesh.shape["dp"], "shard": mesh.shape["shard"]}
        chips = self.sizes["dp"] // 2
        near = 2 if chips % 2 == 0 else 1
        self.core = ("dp", 1, 2)
        self.near = ("dp", 2, near)
        self.far = ("dp", 2 * near, chips // near)
        self.shard = ("shard", 1, self.sizes["shard"])

    def place(self, digit):
        axis, stride, size = digit
        return (lax.axis_index(axis) // stride) % size

    def shift(self, value, digit, step):
        axis, stride, size = digit
        pairs = []
        for i in range(self.sizes[axis]):
            own = (i // stride) % size
            pairs.append((i, i + ((own + step) % size - own) * stride))
        return lax.ppermute(value, axis, pairs)

    def scatter_sum(self, value, digit, dim):
        size = digit[2]
        if size == 1:
            return value
        own = self.place(digit)
        width = value.shape[dim] // size

        def piece(index):
            return lax.dynamic_slice_in_dim(value, index * width, width, dim)

        total = piece(own).astype(f32)
        for step in range(1, size):
            total += self.shift(piece((own + step) % size), digit, step).astype(f32)
        return total.astype(bf16)

    def gather(self, value, digit, dim):
        size = digit[2]
        if size == 1:
            return value
        own = self.place(digit)
        width = value.shape[dim]
        if size == 2:
            other = self.shift(value, digit, 1)
            first = jnp.where(own == 0, value, other)
            second = jnp.where(own == 0, other, value)
            return jnp.concatenate([first, second], axis=dim)
        shape = list(value.shape)
        shape[dim] *= size
        full = lax.dynamic_update_slice_in_dim(
            jnp.zeros(shape, value.dtype), value, own * width, dim
        )
        for step in range(1, size):
            came = self.shift(value, digit, step)
            full = lax.dynamic_update_slice_in_dim(
                full, came, ((own - step) % size) * width, dim
            )
        return full

    def gather_rows(self, value, spread):
        parts = [self.core, self.near] if spread else [self.core]
        piece = value
        for digit in parts:
            width = piece.shape[0] // digit[2]
            piece = lax.dynamic_slice_in_dim(piece, self.place(digit) * width, width, 0)
        size = self.shard[2]
        rows = value.shape[0]
        own = self.place(self.shard)
        full = lax.dynamic_update_slice_in_dim(
            jnp.zeros((size * rows, value.shape[1]), value.dtype), value, own * rows, 0
        )
        for step in range(1, size):
            came = self.shift(piece, self.shard, step)
            for digit in reversed(parts):
                came = self.gather(came, digit, 0)
            full = lax.dynamic_update_slice_in_dim(full, came, ((own - step) % size) * rows, 0)
        return full

    def total(self, grads):
        grads = self.scatter_sum(grads, self.core, 1)
        grads = self.scatter_sum(grads, self.shard, 0)
        grads = self.scatter_sum(grads, self.near, 0)
        grads = self.scatter_sum(grads, self.far, 0)
        grads = self.gather(grads, self.far, 0)
        grads = self.gather(grads, self.near, 0)
        return self.gather(grads, self.core, 1)


def adam_update(weight, first_moment, second_moment, gradient, rate, decay_on):
    first_new = beta_first * first_moment + (1.0 - beta_first) * gradient
    second_new = beta_second * second_moment + (1.0 - beta_second) * gradient * gradient
    fix_first = 1.0 - beta_first**STEP
    fix_second = 1.0 - beta_second**STEP
    direction = first_new / fix_first / (jnp.sqrt(second_new / fix_second) + adam_eps)
    return (weight - rate * (direction + decay_on * weight), first_new, second_new)


class Finish:
    def __init__(self, mesh, shapes, plan, scale):
        self.far_size = mesh.shape["dp"] // 4
        self.scale = scale
        self.shapes = shapes
        self.plan = plan

    @staticmethod
    def fits(mesh, rows):
        far = mesh.shape["dp"] // 4
        return (
            mesh.shape["shard"] == 2
            and mesh.shape["dp"] % 4 == 0
            and all(count % (2 * far * 16) == 0 for count in rows)
        )

    def chunk_scratch(self):
        first, own, second, third, fourth, totals = [], [], [], [], [], []
        for _, _, _, width, _, _, rows in self.plan:
            near, far = rows // 2, rows // 2 // self.far_size
            first.append(pltpu.VMEM((2 * rows, width), bf16))
            own.append(pltpu.VMEM((2 * rows, width), bf16))
            second.append(pltpu.VMEM((rows, width), bf16))
            third.append(pltpu.VMEM((near, width), bf16))
            fourth.append(pltpu.VMEM((max(self.far_size - 1, 1), far, width), bf16))
            totals.append(pltpu.VMEM((2, rows, width), bf16))
        return first + own + second + third + fourth + totals

    def __call__(self, grads, masters, norm_grads, norm_state):
        count, matrices = len(self.plan), len(masters)
        self.block_rows = min(rows for *_, rows in self.plan)
        self.block_cols = max(width for _, _, _, width, *_ in self.plan)
        self.blocks = [
            (k, half, low)
            for k, chunk in enumerate(self.plan)
            for half in range(2)
            for low in range(0, chunk[6], self.block_rows)
        ]
        block = (2, self.block_rows, self.block_cols)
        far = max(self.far_size - 1, 1)
        dma = pltpu.SemaphoreType.DMA
        scratch = self.chunk_scratch() + [
            pltpu.VMEM((3,) + block, f32),
            pltpu.VMEM((2,) + block, f32),
            pltpu.VMEM(block, bf16),
            pltpu.VMEM((3,) + norm_grads.shape, f32),
            pltpu.VMEM((self.far_size,) + norm_grads.shape, f32),
            dma((count,)),
            dma((9, count, 2)),
            dma((2, count, far, 2)),
            dma((4 + 2 * far,)),
            dma((3 + far,)),
            dma((2, 3)),
            dma((2, 4)),
        ]
        anywhere = pl.BlockSpec(memory_space=pl.ANY)
        in_vmem = pl.BlockSpec(memory_space=pltpu.VMEM)
        state = [part for master in masters for part in master]
        outs = []
        for master, _, _ in masters:
            full = (2 * master.shape[0], master.shape[1])
            outs += [
                jax.ShapeDtypeStruct(full, bf16),
                jax.ShapeDtypeStruct(master.shape, f32),
                jax.ShapeDtypeStruct(master.shape, f32),
            ]
        norm_outs = [jax.ShapeDtypeStruct(norm_grads.shape, f32)] * 3
        results = pl.pallas_call(
            functools.partial(self.kernel, len(grads), matrices),
            in_specs=[anywhere] * (len(grads) + len(state)) + [in_vmem] * 4,
            out_specs=[anywhere] * len(outs) + [in_vmem] * 3,
            out_shape=outs + norm_outs,
            scratch_shapes=scratch,
            compiler_params=params(collective_id=1, has_side_effects=True),
            name="finish",
        )(*grads, *state, norm_grads, *norm_state)
        updated = [tuple(results[3 * i : 3 * i + 3]) for i in range(matrices)]
        return updated, tuple(results[3 * matrices :])

    def kernel(self, grad_count, matrices, *refs):
        refs = list(refs)

        def take(number):
            taken = refs[:number]
            del refs[:number]
            return taken

        count = len(self.plan)
        grads, state = take(grad_count), take(3 * matrices)
        norm_in, norms, norm_first, norm_second = take(4)
        outs, norm_outs = take(3 * matrices), take(3)
        first, own, second, third, fourth, totals = [take(count) for _ in range(6)]
        load_buf, store_buf, new_buf, norm_sum, norm_far = take(5)
        own_sem, pair_sem, far_sem, norm_send, norm_recv, load_sem, store_sem = take(7)

        dp, shard = lax.axis_index("dp"), lax.axis_index("shard")
        core, near, far = dp % 2, dp // 2 % 2, dp // 4
        sizes = self.far_size
        core_peer, near_peer, shard_peer = (dp + 1 - 2 * core, shard), (dp + 2 - 4 * near, shard), (dp, 1 - shard)

        def far_peer(step):
            return (dp + ((far + step) % sizes - far) * 4, shard)

        peers = [core_peer, near_peer, shard_peer] + [far_peer(step) for step in range(1, sizes)]
        barrier = pltpu.get_barrier_semaphore()
        for peer in peers:
            pl.semaphore_signal(barrier, inc=1, device_id=peer, device_id_type=pl.DeviceIdType.MESH)
        pl.semaphore_wait(barrier, len(peers))

        pending = []

        def send(source, target, sent, came, peer):
            copy = pltpu.make_async_remote_copy(
                src_ref=source,
                dst_ref=target,
                send_sem=sent,
                recv_sem=came,
                device_id=peer,
                device_id_type=pl.DeviceIdType.MESH,
            )
            copy.start()
            pending.append(copy)
            return copy

        def pair(stage, k, source, target, peer):
            return send(source, target, pair_sem.at[stage, k, 0], pair_sem.at[stage, k, 1], peer)

        def columns(k, half, total):
            _, before, low, width, *_ = self.plan[k]
            return pl.ds(pl.multiple_of(half * (total // 2) + low, 128), width)

        def add_rows(target, sources, rows, step):
            @pl.loop(0, rows // step)
            def _(i):
                span = pl.ds(pl.multiple_of(i * step, step), step)
                value = sources[0][span, :].astype(f32)
                for source in sources[1:]:
                    value += source[span, :].astype(f32)
                target[span, :] = value.astype(bf16)

        copies = {}

        def start_core(k):
            grad, total, _, width, _, _, rows = self.plan[k]
            load = pltpu.make_async_copy(grads[grad].at[:, columns(k, core, total)], own[k], own_sem.at[k])
            load.start()
            copies["own", k] = load
            copies["core", k] = pair(
                0, k, grads[grad].at[:, columns(k, 1 - core, total)], first[k], core_peer
            )

        def start_shard(k):
            rows = self.plan[k][6]
            copies["own", k].wait()
            copies["core", k].wait_recv()
            add_rows(own[k], [own[k], first[k]], 2 * rows, 16)
            copies["shard", k] = pair(
                1, k, own[k].at[pl.ds(pl.multiple_of((1 - shard) * rows, 16), rows)], second[k], shard_peer
            )

        def start_near(k):
            rows = self.plan[k][6]
            half = rows // 2
            copies["shard", k].wait_recv()
            add_rows(
                second[k], [second[k], own[k].at[pl.ds(pl.multiple_of(shard * rows, 16), rows)]], rows, 16
            )
            copies["near", k] = pair(
                2, k, second[k].at[pl.ds(pl.multiple_of((1 - near) * half, 16), half)], third[k], near_peer
            )

        def start_far(k):
            half = self.plan[k][6] // 2
            part = half // sizes
            copies["near", k].wait_recv()
            add_rows(
                third[k], [third[k], second[k].at[pl.ds(pl.multiple_of(near * half, 16), half)]], half, 16
            )
            for step in range(1, sizes):
                place = pl.multiple_of((far + step) % sizes * part, 16)
                copies["far", k, step] = send(
                    third[k].at[pl.ds(place, part)],
                    fourth[k].at[step - 1],
                    far_sem.at[0, k, step - 1, 0],
                    far_sem.at[0, k, step - 1, 1],
                    far_peer(step),
                )

        def own_part(k):
            half = self.plan[k][6] // 2
            part = half // sizes
            return totals[k].at[core, pl.ds(pl.multiple_of(near * half + far * part, 16), part)]

        def start_far_total(k):
            part = self.plan[k][6] // 2 // sizes
            for step in range(1, sizes):
                copies["far", k, step].wait_recv()
            add_rows(
                own_part(k),
                [third[k].at[pl.ds(pl.multiple_of(far * part, 16), part)]]
                + [fourth[k].at[step - 1] for step in range(1, sizes)],
                part,
                16,
            )
            for step in range(1, sizes):
                copies["far total", k, step] = send(
                    own_part(k),
                    own_part(k),
                    far_sem.at[1, k, step - 1, 0],
                    far_sem.at[1, k, step - 1, 1],
                    far_peer(step),
                )

        def start_near_total(k):
            half = self.plan[k][6] // 2
            for step in range(1, sizes):
                copies["far total", k, step].wait_recv()
            rows = totals[k].at[core, pl.ds(pl.multiple_of(near * half, 16), half)]
            copies["near total", k] = pair(3, k, rows, rows, near_peer)

        def start_core_total(k):
            copies["near total", k].wait_recv()
            copies["core total", k] = pair(4, k, totals[k].at[core], totals[k].at[core], core_peer)

        def places(b):
            k, half, low = self.blocks[b]
            _, total, start, width, matrix, before, rows = self.plan[k]
            column = before + half * (total // 2) + start
            return k, half, low, matrix, pl.ds(low, self.block_rows), pl.ds(column, width), width, rows

        def load(b):
            _, _, _, matrix, rows, cols, width, _ = places(b)
            for i in range(3):
                copy = pltpu.make_async_copy(
                    state[3 * matrix + i].at[rows, cols],
                    load_buf.at[i, b % 2, :, pl.ds(0, width)],
                    load_sem.at[b % 2, i],
                )
                copy.start()
                copies["load", b, i] = copy

        def settle(b, first):
            while len(copies["store", b]) > 3 - first:
                copies["store", b].pop(0).wait()

        def update(b):
            k, half, low, matrix, rows, cols, width, shard_rows = places(b)
            slot = b % 2
            for i in range(3):
                copies["load", b, i].wait()
            if b >= 2:
                settle(b - 2, 3)

            step = 16

            @pl.loop(0, self.block_rows // step)
            def _(i):
                span = pl.ds(pl.multiple_of(i * step, step), step)
                lanes = pl.ds(0, width)
                grad = totals[k][half, pl.ds(pl.multiple_of(low + i * step, step), step), :]
                grad = grad.astype(f32) * self.scale
                new, first_new, second_new = adam_update(
                    load_buf[0, slot, span, lanes],
                    load_buf[1, slot, span, lanes],
                    load_buf[2, slot, span, lanes],
                    grad,
                    learn_rate,
                    decay_rate,
                )
                store_buf[0, slot, span, lanes] = first_new
                store_buf[1, slot, span, lanes] = second_new
                new_buf[slot, span, lanes] = new.astype(bf16)

            lanes = pl.ds(0, width)
            stores = []
            for i in range(2):
                stores.append(
                    pltpu.make_async_copy(
                        store_buf.at[i, slot, :, lanes],
                        outs[3 * matrix + 1 + i].at[rows, cols],
                        store_sem.at[slot, i],
                    )
                )
            full_rows = pl.ds(pl.multiple_of(shard * shard_rows + low, 16), self.block_rows)
            stores.append(
                pltpu.make_async_copy(
                    new_buf.at[slot, :, lanes],
                    outs[3 * matrix].at[full_rows, cols],
                    store_sem.at[slot, 2],
                )
            )
            for copy in stores:
                copy.start()
            copies["store", b] = stores[::-1]

        def region(k, half, side, low, rows):
            _, total, start, width, matrix, before, shard_rows = self.plan[k]
            column = before + half * (total // 2) + start
            return outs[3 * matrix].at[
                pl.ds(pl.multiple_of(side * shard_rows + low, 16), rows),
                pl.ds(pl.multiple_of(column, 128), width),
            ]

        def start_new(k):
            half = self.plan[k][6] // 2
            for b, (chunk, _, _) in enumerate(self.blocks):
                if chunk == k:
                    settle(b, 1)
            rows = region(k, core, shard, near * half, half)
            copies["new", k] = pair(5, k, rows, rows, shard_peer)

        def start_new_near(k):
            half = self.plan[k][6] // 2
            copies["new", k].wait_recv()
            rows = region(k, core, 1 - shard, near * half, half)
            copies["new near", k] = pair(6, k, rows, rows, near_peer)

        def start_new_core(k):
            copies["new near", k].wait_recv()
            rows = region(k, core, 1 - shard, 0, self.plan[k][6])
            copies["new core", k] = pair(7, k, rows, rows, core_peer)

        norm_copies = {}

        def norm_send_to(slot, source, peer):
            norm_copies[slot] = send(source, norm_sum.at[slot], norm_send.at[slot], norm_recv.at[slot], peer)

        def norm_stage(stage):
            if stage == 0:
                norm_send_to(0, norm_in, core_peer)
            elif stage == 1:
                norm_copies[0].wait_recv()
                norm_sum[0] += norm_in[...]
                norm_send_to(1, norm_sum.at[0], shard_peer)
            elif stage == 2:
                norm_copies[1].wait_recv()
                norm_sum[1] += norm_sum[0]
                norm_send_to(2, norm_sum.at[1], near_peer)
            elif stage == 3:
                norm_copies[2].wait_recv()
                norm_sum[2] += norm_sum[1]
                norm_far[far] = norm_sum[2]
                for step in range(1, sizes):
                    norm_copies["far", step] = send(
                        norm_sum.at[2],
                        norm_far.at[far],
                        norm_send.at[3 + step],
                        norm_recv.at[2 + step],
                        far_peer(step),
                    )
            elif stage == 4:
                total = None
                for step in range(1, sizes):
                    norm_copies["far", step].wait_recv()
                total = norm_far[0]
                for place in range(1, sizes):
                    total += norm_far[place]
                new, first_new, second_new = adam_update(
                    norms[...], norm_first[...], norm_second[...], total * self.scale, norm_rate, 0.0
                )
                norm_outs[0][...] = new
                norm_outs[1][...] = first_new
                norm_outs[2][...] = second_new

        ahead = 2
        for k in range(min(ahead + 1, count)):
            start_core(k)
        norm_stage(0)
        for k in range(min(ahead, count)):
            start_shard(k)
        load(0)
        load(1)
        done = 0

        def run_update(k):
            nonlocal done
            copies["core total", k].wait_recv()
            while done < len(self.blocks) and self.blocks[done][0] == k:
                update(done)
                if done + 2 < len(self.blocks):
                    load(done + 2)
                done += 1
            start_new(k)

        def on(k, action):
            if 0 <= k < count:
                action(k)

        for t in range(count + 6):
            on(t, start_near)
            if t < count and t + ahead < count:
                if t + ahead + 1 < count:
                    start_core(t + ahead + 1)
                start_shard(t + ahead)
            if 1 + t < 5:
                norm_stage(1 + t)
            on(t - 1, start_far)
            on(t - 2, start_core_total)
            on(t - 4, start_new_near)
            on(t - 1, start_far_total)
            on(t - 2, run_update)
            on(t - 1, start_near_total)
            on(t - 5, start_new_core)
            on(t - 6, lambda k: copies["new core", k].wait_recv())
        for copy in pending:
            copy.wait_send()
        for b in range(len(self.blocks)):
            settle(b, 3)


def shards(
    mesh,
    tokens,
    cotangent,
    master_qkv,
    first_qkv,
    second_qkv,
    master_out,
    first_out,
    second_out,
    master_gate_up,
    first_gate_up,
    second_gate_up,
    master_down,
    first_down,
    second_down,
    norms,
    norm_first,
    norm_second,
):
    links = Links(mesh)
    length, width = tokens.shape
    shard_count = mesh.shape["shard"]
    cosine, sine = rope_tables(length)

    weight_qkv = links.gather_rows(master_qkv.astype(bf16), False)
    weight_out = links.gather_rows(master_out.astype(bf16), False)
    weight_gate_up = links.gather_rows(master_gate_up.astype(bf16), True)
    weight_down = links.gather_rows(master_down.astype(bf16), True)

    joined = project_qkv(tokens, weight_qkv, cosine, sine)
    mixed, weights = attend_forward(joined)
    normed_one, inverse_one, hidden_low = project_out(tokens, mixed, weight_out, norms)
    gate, up, output, grad_second, grad_low, norm_two = feed_forward(
        hidden_low, weight_gate_up, weight_down, normed_one, norms, cotangent
    )

    inner = weight_down.shape[0]
    pieces = 1
    groups = shard_count if pieces > 1 else 1
    carried = grad_second
    for piece in range(pieces):
        gate_grad, up_grad, down_grad, carried, *more = feed_backward(
            piece,
            pieces,
            groups,
            grad_low,
            hidden_low,
            gate,
            up,
            weight_gate_up,
            weight_down,
            carried,
            normed_one,
            inverse_one,
            norms,
        )
    grad_first = carried
    first_low, norm_one = more

    out_grad = contract(mixed, first_low, 1, 0).astype(bf16)
    mixed_grad = contract(weight_out, first_low, 1, 1).astype(bf16)
    query_back, key_back, value_back = attend_backward(
        joined, mixed, mixed_grad, weights, cosine, sine
    )
    joined_back = jnp.concatenate([query_back, key_back, value_back], axis=0)
    qkv_grad = contract(tokens, joined_back, 0, 1).astype(bf16)
    input_grad = (grad_first + contract(joined_back, weight_qkv, 0, 1)).astype(bf16)

    scale_grad = 1.0 / math.sqrt(length * mesh.shape["dp"] * shard_count)
    grads = [gate_grad, up_grad, down_grad, out_grad, qkv_grad]
    masters = [
        (master_gate_up, first_gate_up, second_gate_up),
        (master_down, first_down, second_down),
        (master_out, first_out, second_out),
        (master_qkv, first_qkv, second_qkv),
    ]
    norm_grads = jnp.concatenate([norm_one, norm_two])
    norm_state = (norms, norm_first, norm_second)
    if Finish.fits(mesh, [master.shape[0] for master, _, _ in masters]):
        rows, long_rows = master_out.shape[0], master_down.shape[0]
        plan = [
            (2, width, 0, 256, 1, 0, long_rows),
            (0, inner, 0, 768, 0, 0, rows),
            (1, inner, 0, 768, 0, inner, rows),
            (0, inner, 768, 768, 0, 0, rows),
            (1, inner, 768, 768, 0, inner, rows),
            (2, width, 256, 128, 1, 0, long_rows),
            (4, 3 * width, 0, 768, 3, 0, rows),
            (4, 3 * width, 768, 384, 3, 0, rows),
            (3, width, 0, 384, 2, 0, rows),
        ]
        finish = Finish(mesh, [grad.shape for grad in grads], plan, scale_grad)
        updated, updated_norms = finish(grads, masters, norm_grads, norm_state)
    else:
        totals = [
            jnp.concatenate([links.total(gate_grad), links.total(up_grad)], axis=1),
            links.total(down_grad),
            links.total(out_grad),
            links.total(qkv_grad),
        ]
        updated = []
        for (master, first, second), total in zip(masters, totals, strict=True):
            new, first_new, second_new = adam_update(
                master, first, second, total.astype(f32) * scale_grad, learn_rate, decay_rate
            )
            updated.append((links.gather_rows(new.astype(bf16), True), first_new, second_new))
        norm_total = lax.psum(norm_grads, ("dp", "shard"))
        updated_norms = adam_update(*norm_state, norm_total * scale_grad, norm_rate, 0.0)
    (
        (full_gate_up, first_gate_up_new, second_gate_up_new),
        (full_down, first_down_new, second_down_new),
        (full_out, first_out_new, second_out_new),
        (full_qkv, first_qkv_new, second_qkv_new),
    ) = updated
    upd_norms, norm_first_new, norm_second_new = updated_norms
    return (
        output,
        input_grad,
        full_qkv,
        full_out,
        full_gate_up,
        full_down,
        first_qkv_new,
        second_qkv_new,
        first_out_new,
        second_out_new,
        first_gate_up_new,
        second_gate_up_new,
        first_down_new,
        second_down_new,
        upd_norms,
        norm_first_new,
        norm_second_new,
    )


def solution(mesh):
    rows, split, copied = P(("dp", "shard"), None), P("shard", None), P()
    return jax.shard_map(
        functools.partial(shards, mesh),
        mesh=mesh,
        in_specs=(rows, rows) + (split,) * 12 + (copied,) * 3,
        out_specs=(rows, rows) + (copied,) * 4 + (split,) * 8 + (copied,) * 3,
        check_vma=False,
    )
```

```python
import functools
import math

import jax
import jax.numpy as jnp
import numpy as np
from jax import lax
from jax.experimental import pallas as pl
from jax.experimental.pallas import tpu as pltpu
from jax.sharding import PartitionSpec as P

HEADS = 12
HEAD_DIM = 64
STEP = 3

norm_eps = 1e-12
rope_base = 1000.0
learn_rate = 0.03
norm_rate = 0.3
decay_rate = 0.1
adam_eps = 1e-08
beta_first = 0.5
beta_second = 0.5

f32, bf16 = jnp.float32, jnp.bfloat16
VMEM_BYTES = 56 * 2**20


def contract(left, right, left_dim, right_dim):
    return lax.dot_general(
        left, right, (((left_dim,), (right_dim,)), ((), ())), preferred_element_type=f32
    )


def params(**more):
    return pltpu.CompilerParams(vmem_limit_bytes=VMEM_BYTES, **more)


def cost(flops, moved, transcendentals=0):
    return pl.CostEstimate(
        flops=int(flops), bytes_accessed=int(moved), transcendentals=int(transcendentals)
    )


def whole(*shape):
    return pl.BlockSpec(shape, lambda *_: (0,) * len(shape))


def rope_tables(length):
    half = HEAD_DIM // 2
    frequency = np.float32(rope_base) ** (
        -(np.arange(half, dtype=np.float32) * np.float32(2.0 / HEAD_DIM))
    )
    angles = np.arange(length, dtype=np.float32)[None, :] * frequency[:, None]
    return jnp.asarray(np.cos(angles), f32), jnp.asarray(np.sin(angles), f32)


def qkv_kernel(blocks_rotated, heads_block, tokens, weight, cosine, sine, joined):
    step = pl.program_id(0)
    rows = contract(weight[...], tokens[...], 0, 1)
    half = HEAD_DIM // 2

    @pl.when(step < 2 * blocks_rotated)
    def _():
        scale = jnp.where(step < blocks_rotated, 1.0 / math.sqrt(HEAD_DIM), 1.0)
        cos, sin = cosine[...] * scale, sine[...] * scale
        for head in range(heads_block):
            low = head * HEAD_DIM
            t1, t2 = rows[low : low + half], rows[low + half : low + 2 * half]
            joined[low : low + half] = (t1 * cos - t2 * sin).astype(bf16)
            joined[low + half : low + 2 * half] = (t2 * cos + t1 * sin).astype(bf16)

    @pl.when(step >= 2 * blocks_rotated)
    def _():
        joined[...] = rows.astype(bf16)


def project_qkv(tokens, weight, cosine, sine):
    length, width = tokens.shape
    heads_block = 4
    block = heads_block * HEAD_DIM
    count = weight.shape[1] // block
    return pl.pallas_call(
        functools.partial(qkv_kernel, count // 3, heads_block),
        grid=(count,),
        in_specs=[
            whole(length, width),
            pl.BlockSpec((width, block), lambda i: (0, i)),
            whole(*cosine.shape),
            whole(*sine.shape),
        ],
        out_specs=pl.BlockSpec((block, length), lambda i: (i, 0)),
        out_shape=jax.ShapeDtypeStruct((weight.shape[1], length), bf16),
        compiler_params=params(),
        cost_estimate=cost(2 * length * width * weight.shape[1], 2 * weight.size * 3),
        name="qkv_rope",
    )(tokens, weight, cosine, sine)


def attend_head(queries, key_rows, value_rows, mixed, weights):
    length = queries.shape[1]
    chunk = min(512, length)

    def scores_of(low):
        return contract(key_rows[...], queries[:, pl.ds(low, chunk)], 0, 0)

    scores = scores_of(0)
    for low in range(0, length, chunk):
        span = pl.ds(low, chunk)
        following = scores_of(low + chunk) if low + chunk < length else None
        highest = jnp.max(scores, axis=0, keepdims=True)
        expanded = jnp.exp(scores - highest)
        totals = jnp.sum(expanded, axis=0, keepdims=True)
        soft = (expanded * (1.0 / totals)).astype(bf16)
        weights[0, :, span] = soft
        mixed[:, span] = contract(value_rows[...], soft, 1, 0).astype(bf16)
        scores = following


def attend_forward(joined):
    length = joined.shape[1]
    head_rows = lambda part: pl.BlockSpec(
        (HEAD_DIM, length), lambda h: (part * HEADS + h, 0)
    )
    return pl.pallas_call(
        attend_head,
        grid=(HEADS,),
        in_specs=[head_rows(0), head_rows(1), head_rows(2)],
        out_specs=[
            pl.BlockSpec((HEAD_DIM, length), lambda h: (h, 0)),
            pl.BlockSpec((1, length, length), lambda h: (h, 0, 0)),
        ],
        out_shape=[
            jax.ShapeDtypeStruct((HEADS * HEAD_DIM, length), bf16),
            jax.ShapeDtypeStruct((HEADS, length, length), bf16),
        ],
        compiler_params=params(),
        cost_estimate=cost(
            16 * HEADS * length * length * HEAD_DIM, 2 * HEADS * length * length, length * length * HEADS
        ),
        name="attend_forward",
    )(joined, joined, joined)


def attend_back_kernel(
    chunk,
    queries,
    key_rows,
    value_rows,
    mixed,
    grad_mixed,
    weights,
    cosine,
    sine,
    query_out,
    key_out,
    value_out,
):
    length = queries.shape[1]
    half = HEAD_DIM // 2
    grad = grad_mixed[...]
    centre = jnp.sum(grad.astype(f32) * mixed[...].astype(f32), axis=0, keepdims=True)
    query_grad = jnp.zeros((HEAD_DIM, length), f32)
    key_parts = []
    for low in range(0, length, chunk):
        span = pl.ds(low, chunk)
        soft = weights[0, span, :]
        weight_grad = contract(value_rows[:, span], grad, 0, 0)
        score_grad = (soft.astype(f32) * (weight_grad - centre)).astype(bf16)
        value_out[:, span] = contract(grad, soft, 1, 1).astype(bf16)
        key_parts.append(contract(queries[...], score_grad, 1, 1))
        query_grad += contract(key_rows[:, span], score_grad, 1, 0)
    key_grad = jnp.concatenate(key_parts, axis=1)
    cos, sin = cosine[...], sine[...]
    scale = 1.0 / math.sqrt(HEAD_DIM)
    for out, grad_rows, factor in ((query_out, query_grad, scale), (key_out, key_grad, 1.0)):
        d1, d2 = grad_rows[:half], grad_rows[half:]
        out[:half] = ((d1 * cos + d2 * sin) * factor).astype(bf16)
        out[half:] = ((d2 * cos - d1 * sin) * factor).astype(bf16)


def attend_backward(joined, mixed, grad_mixed, weights, cosine, sine):
    length = joined.shape[1]
    head_rows = lambda part: pl.BlockSpec(
        (HEAD_DIM, length), lambda h: (part * HEADS + h, 0)
    )
    rows = jax.ShapeDtypeStruct((HEADS * HEAD_DIM, length), bf16)
    return pl.pallas_call(
        functools.partial(attend_back_kernel, min(256, length)),
        grid=(HEADS,),
        in_specs=[
            head_rows(0),
            head_rows(1),
            head_rows(2),
            head_rows(0),
            head_rows(0),
            pl.BlockSpec((1, length, length), lambda h: (h, 0, 0)),
            whole(*cosine.shape),
            whole(*sine.shape),
        ],
        out_specs=[head_rows(0)] * 3,
        out_shape=[rows] * 3,
        compiler_params=params(),
        cost_estimate=cost(
            32 * HEADS * length * length * HEAD_DIM, 2 * HEADS * length * length
        ),
        name="attend_backward",
    )(joined, joined, joined, mixed, grad_mixed, weights, cosine, sine)


def norm_rows(values):
    centred = values - jnp.mean(values, axis=1, keepdims=True)
    inverse = lax.rsqrt(jnp.mean(centred * centred, axis=1, keepdims=True) + norm_eps)
    return centred * inverse, inverse


def norm_back(grad_rows, normed, inverse, gain_row):
    scaled = grad_rows * gain_row
    centred = (
        scaled
        - jnp.mean(scaled, axis=1, keepdims=True)
        - normed * jnp.mean(scaled * normed, axis=1, keepdims=True)
    )
    gain = jnp.sum(grad_rows * normed, axis=0, keepdims=True)
    bias = jnp.sum(grad_rows, axis=0, keepdims=True)
    return centred * inverse, gain, bias


def out_kernel(tokens, mixed, weight, norms, normed, inverse, hidden_low):
    sums = tokens[...].astype(f32) + contract(mixed[...], weight[...], 0, 0)
    rows, scale = norm_rows(sums)
    normed[...] = rows
    inverse[...] = scale
    hidden_low[...] = (rows * norms[0:1, :] + norms[1:2, :]).astype(bf16)


def project_out(tokens, mixed, weight, norms):
    length, width = tokens.shape
    block = min(256, length)
    return pl.pallas_call(
        out_kernel,
        grid=(length // block,),
        in_specs=[
            pl.BlockSpec((block, width), lambda i: (i, 0)),
            pl.BlockSpec((width, block), lambda i: (0, i)),
            whole(width, width),
            whole(*norms.shape),
        ],
        out_specs=[
            pl.BlockSpec((block, width), lambda i: (i, 0)),
            pl.BlockSpec((block, 1), lambda i: (i, 0)),
            pl.BlockSpec((block, width), lambda i: (i, 0)),
        ],
        out_shape=[
            jax.ShapeDtypeStruct((length, width), f32),
            jax.ShapeDtypeStruct((length, 1), f32),
            jax.ShapeDtypeStruct((length, width), bf16),
        ],
        compiler_params=params(),
        cost_estimate=cost(2 * length * width * width, 10 * length * width),
        name="out_norm",
    )(tokens, mixed, weight, norms)


def second_norm(
    rows_block, normed_one, norms, cotangent, output, grad_second, grad_low, norm_grads, total
):
    gain_sum = jnp.zeros((1, total.shape[1]), f32)
    bias_sum = jnp.zeros((1, total.shape[1]), f32)
    for low in range(0, total.shape[0], rows_block):
        span = pl.ds(low, rows_block)
        hidden = normed_one[span, :] * norms[0:1, :] + norms[1:2, :]
        rows, inverse = norm_rows(hidden + total[span, :])
        output[span, :] = (rows * norms[2:3, :] + norms[3:4, :]).astype(bf16)
        back, gain, bias = norm_back(cotangent[span, :].astype(f32), rows, inverse, norms[2:3, :])
        grad_second[span, :] = back
        grad_low[span, :] = back.astype(bf16)
        gain_sum += gain
        bias_sum += bias
    norm_grads[0:1, :] = gain_sum
    norm_grads[1:2, :] = bias_sum


def first_norm_back(
    rows_block, normed, inverse, norms, total, grad_first, first_low, norm_grads
):
    gain_sum = jnp.zeros((1, total.shape[1]), f32)
    bias_sum = jnp.zeros((1, total.shape[1]), f32)
    for low in range(0, total.shape[0], rows_block):
        span = pl.ds(low, rows_block)
        back, gain, bias = norm_back(
            total[span, :], normed[span, :], inverse[span, :], norms[0:1, :]
        )
        grad_first[span, :] = back
        first_low[span, :] = back.astype(bf16)
        gain_sum += gain
        bias_sum += bias
    norm_grads[0:1, :] = gain_sum
    norm_grads[1:2, :] = bias_sum


def forward_kernel(
    rows_block,
    hidden_low,
    gate_weight,
    up_weight,
    down_weight,
    normed_one,
    norms,
    cotangent,
    gate,
    up,
    output,
    grad_second,
    grad_low,
    norm_grads,
    total,
):
    step = pl.program_id(0)
    length = hidden_low.shape[0]
    for low in range(0, length, rows_block):
        span = pl.ds(low, rows_block)
        gate_part = contract(hidden_low[span, :], gate_weight[...], 1, 0)
        up_part = contract(hidden_low[span, :], up_weight[...], 1, 0)
        gate[span, :] = gate_part
        up[span, :] = up_part
        inner = (gate_part * jax.nn.sigmoid(gate_part) * up_part).astype(bf16)
        part = contract(inner, down_weight[...], 1, 0)

        @pl.when(step == 0)
        def _():
            total[span, :] = part

        @pl.when(step > 0)
        def _():
            total[span, :] += part

    @pl.when(step == pl.num_programs(0) - 1)
    def _():
        second_norm(
            rows_block, normed_one, norms, cotangent, output, grad_second, grad_low, norm_grads, total
        )


def feed_forward(hidden_low, gate_up, down, normed_one, norms, cotangent):
    length, width = hidden_low.shape
    inner = down.shape[0]
    block = min(512, inner)
    count = inner // block
    return pl.pallas_call(
        functools.partial(forward_kernel, min(256, length)),
        grid=(count,),
        in_specs=[
            whole(length, width),
            pl.BlockSpec((width, block), lambda j: (0, j)),
            pl.BlockSpec((width, block), lambda j: (0, count + j)),
            pl.BlockSpec((block, width), lambda j: (j, 0)),
            whole(length, width),
            whole(*norms.shape),
            whole(length, width),
        ],
        out_specs=[
            pl.BlockSpec((length, block), lambda j: (0, j)),
            pl.BlockSpec((length, block), lambda j: (0, j)),
            whole(length, width),
            whole(length, width),
            whole(length, width),
            whole(2, width),
        ],
        out_shape=[
            jax.ShapeDtypeStruct((length, inner), f32),
            jax.ShapeDtypeStruct((length, inner), f32),
            jax.ShapeDtypeStruct((length, width), bf16),
            jax.ShapeDtypeStruct((length, width), f32),
            jax.ShapeDtypeStruct((length, width), bf16),
            jax.ShapeDtypeStruct((2, width), f32),
        ],
        scratch_shapes=[pltpu.VMEM((length, width), f32)],
        compiler_params=params(),
        cost_estimate=cost(6 * length * width * inner, 8 * length * inner),
        name="feed_forward",
    )(hidden_low, gate_up, gate_up, down, normed_one, norms, cotangent)


def backward_kernel(
    rows_block,
    grad_low,
    hidden_low,
    gate,
    up,
    gate_weight,
    up_weight,
    down_weight,
    before,
    normed,
    inverse,
    norms,
    gate_out,
    up_out,
    down_out,
    grad_first,
    first_low,
    norm_grads,
    total,
    inner,
    gate_back,
    up_back,
):
    step = pl.program_id(0)
    length = hidden_low.shape[0]

    @pl.when(step == 0)
    def _():
        total[...] = before[...]

    for low in range(0, length, rows_block):
        span = pl.ds(low, rows_block)
        inner_grad = contract(grad_low[span, :], down_weight[...], 1, 1)
        gate_part, up_part = gate[span, :], up[span, :]
        sigmoid = jax.nn.sigmoid(gate_part)
        swished = gate_part * sigmoid
        inner[span, :] = (swished * up_part).astype(bf16)
        gate_grad = inner_grad * up_part * sigmoid * (1.0 + gate_part * (1.0 - sigmoid))
        gate_low, up_low = gate_grad.astype(bf16), (inner_grad * swished).astype(bf16)
        gate_back[span, :] = gate_low
        up_back[span, :] = up_low
        total[span, :] += contract(gate_low, gate_weight[...], 1, 1) + contract(
            up_low, up_weight[...], 1, 1
        )
    down_out[...] = contract(inner[...], grad_low[...], 0, 0).astype(bf16)
    gate_out[...] = contract(hidden_low[...], gate_back[...], 0, 0).astype(bf16)
    up_out[...] = contract(hidden_low[...], up_back[...], 0, 0).astype(bf16)

    @pl.when(step == pl.num_programs(0) - 1)
    def _():
        first_norm_back(rows_block, normed, inverse, norms, total, grad_first, first_low, norm_grads)


def feed_backward(
    grad_low, hidden_low, gate, up, gate_up, down, before, normed, inverse, norms
):
    length, width = hidden_low.shape
    inner = down.shape[0]
    block = min(256, inner)
    count = inner // block
    in_cols = lambda shift: pl.BlockSpec((width, block), lambda j: (0, shift + j))
    wide = pl.BlockSpec((length, block), lambda j: (0, j))
    narrow = pl.BlockSpec((block, width), lambda j: (j, 0))
    full = whole(length, width)
    return pl.pallas_call(
        functools.partial(backward_kernel, min(256, length)),
        grid=(count,),
        in_specs=[
            full,
            full,
            wide,
            wide,
            in_cols(0),
            in_cols(count),
            narrow,
            full,
            full,
            whole(length, 1),
            whole(*norms.shape),
        ],
        out_specs=[in_cols(0), in_cols(0), narrow, full, full, whole(2, width)],
        out_shape=[
            jax.ShapeDtypeStruct((width, inner), bf16),
            jax.ShapeDtypeStruct((width, inner), bf16),
            jax.ShapeDtypeStruct((inner, width), bf16),
            jax.ShapeDtypeStruct((length, width), f32),
            jax.ShapeDtypeStruct((length, width), bf16),
            jax.ShapeDtypeStruct((2, width), f32),
        ],
        scratch_shapes=[pltpu.VMEM((length, width), f32)] + [pltpu.VMEM((length, block), bf16)] * 3,
        compiler_params=params(),
        cost_estimate=cost(12 * length * width * inner, 8 * length * inner),
        name="feed_backward",
    )(grad_low, hidden_low, gate, up, gate_up, gate_up, down, before, normed, inverse, norms)


def paired_forward_kernel(
    rows_block,
    hidden_low,
    gate_0,
    gate_1,
    up_0,
    up_1,
    down_0,
    down_1,
    normed_one,
    norms,
    cotangent,
    gate,
    up,
    output,
    grad_second,
    grad_low,
    norm_grads,
    total,
):
    step = pl.program_id(0)
    length = hidden_low.shape[0]
    run = gate.shape[2] // 2
    gate_weight = jnp.concatenate([gate_0[...], gate_1[...]], axis=1)
    up_weight = jnp.concatenate([up_0[...], up_1[...]], axis=1)
    down_weight = jnp.concatenate([down_0[...], down_1[...]], axis=0)

    def keep(target, span, part):
        for i in range(2):
            target[i, span, :run] = part[:, i * run : (i + 1) * run]
            target[i, span, run:] = part[:, (2 + i) * run : (3 + i) * run]

    for low in range(0, length, rows_block):
        span = pl.ds(low, rows_block)
        gate_part = contract(hidden_low[span, :], gate_weight, 1, 0)
        up_part = contract(hidden_low[span, :], up_weight, 1, 0)
        keep(gate, span, gate_part)
        keep(up, span, up_part)
        inner = (gate_part * jax.nn.sigmoid(gate_part) * up_part).astype(bf16)
        part = contract(inner, down_weight, 1, 0)

        @pl.when(step == 0)
        def _():
            total[span, :] = part

        @pl.when(step > 0)
        def _():
            total[span, :] += part

    @pl.when(step == pl.num_programs(0) - 1)
    def _():
        second_norm(
            rows_block, normed_one, norms, cotangent, output, grad_second, grad_low, norm_grads, total
        )


def paired_forward(hidden_low, gate_up, down, normed_one, norms, cotangent):
    length, width = hidden_low.shape
    inner = down.shape[0]
    run = 256
    count = inner // (2 * run)
    cols = lambda shift: pl.BlockSpec((width, run), lambda j: (0, shift * count + j))
    kept = pl.BlockSpec((2, length, run), lambda j: (j, 0, 0))
    kept_shape = jax.ShapeDtypeStruct((2 * count, length, run), f32)
    return pl.pallas_call(
        functools.partial(paired_forward_kernel, min(256, length)),
        grid=(count,),
        in_specs=[
            whole(length, width),
            cols(0),
            cols(1),
            cols(2),
            cols(3),
            pl.BlockSpec((run, width), lambda j: (j, 0)),
            pl.BlockSpec((run, width), lambda j: (count + j, 0)),
            whole(length, width),
            whole(*norms.shape),
            whole(length, width),
        ],
        out_specs=[
            kept,
            kept,
            whole(length, width),
            whole(length, width),
            whole(length, width),
            whole(2, width),
        ],
        out_shape=[
            kept_shape,
            kept_shape,
            jax.ShapeDtypeStruct((length, width), bf16),
            jax.ShapeDtypeStruct((length, width), f32),
            jax.ShapeDtypeStruct((length, width), bf16),
            jax.ShapeDtypeStruct((2, width), f32),
        ],
        scratch_shapes=[pltpu.VMEM((length, width), f32)],
        compiler_params=params(),
        cost_estimate=cost(6 * length * width * inner, 8 * length * inner),
        name="feed_forward",
    )(hidden_low, *[gate_up] * 4, down, down, normed_one, norms, cotangent)


def paired_backward_kernel(
    rows_block,
    grad_low,
    hidden_low,
    gate,
    up,
    gate_0,
    gate_1,
    up_0,
    up_1,
    down_0,
    down_1,
    before,
    normed,
    inverse,
    norms,
    wide_out,
    down_out,
    grad_first,
    first_low,
    norm_grads,
    total,
    inner,
    gate_back,
    up_back,
    wide_part,
    down_part,
    wide_sum,
    down_sum,
    before_sem,
    core_sem,
    out_sem,
):
    step, last = pl.program_id(0), pl.num_programs(0) - 1
    length, width = hidden_low.shape
    run = gate.shape[2] // 2
    dp, shard = lax.axis_index("dp"), lax.axis_index("shard")
    core = dp % 2
    peer = (dp + 1 - 2 * core, shard)
    start_total = pltpu.make_async_copy(before, total, before_sem)

    def sends(j):
        for i, (part, whole_sum) in enumerate(((wide_part, wide_sum), (down_part, down_sum))):
            yield pltpu.make_async_remote_copy(
                src_ref=part.at[j % 2, 1 - core],
                dst_ref=whole_sum.at[j],
                send_sem=core_sem.at[i, j, 0],
                recv_sem=core_sem.at[i, j, 1],
                device_id=peer,
                device_id_type=pl.DeviceIdType.MESH,
            )

    def keeps(j):
        yield pltpu.make_async_copy(wide_sum.at[j], wide_out.at[j], out_sem.at[0, j])
        yield pltpu.make_async_copy(down_sum.at[j], down_out.at[j], out_sem.at[1, j])

    def add_cores(j):
        for copy in sends(j):
            copy.wait_recv()

        @pl.loop(0, width // 64)
        def _(i):
            span = pl.ds(pl.multiple_of(i * 64, 64), 64)
            for k in range(2):
                value = wide_sum[j, k, span, :].astype(f32) + wide_part[j % 2, core, k, span, :].astype(f32)
                wide_sum[j, k, span, :] = value.astype(bf16)

        @pl.loop(0, 2 * run // 32)
        def _(i):
            span = pl.ds(pl.multiple_of(i * 32, 32), 32)
            value = down_sum[j, 0, span, :].astype(f32) + down_part[j % 2, core, 0, span, :].astype(f32)
            down_sum[j, 0, span, :] = value.astype(bf16)

        for copy in keeps(j):
            copy.start()

    @pl.when(step == 0)
    def _():
        start_total.start()
        barrier = pltpu.get_barrier_semaphore()
        pl.semaphore_signal(barrier, inc=1, device_id=peer, device_id_type=pl.DeviceIdType.MESH)
        pl.semaphore_wait(barrier, 1)
        start_total.wait()

    gate_weight = jnp.concatenate([gate_0[...], gate_1[...]], axis=1)
    up_weight = jnp.concatenate([up_0[...], up_1[...]], axis=1)
    down_weight = jnp.concatenate([down_0[...], down_1[...]], axis=0)
    for low in range(0, length, rows_block):
        span = pl.ds(low, rows_block)
        inner_grad = contract(grad_low[span, :], down_weight, 1, 1)
        gate_part, up_part = gate[0, span, :], up[0, span, :]
        sigmoid = jax.nn.sigmoid(gate_part)
        swished = gate_part * sigmoid
        inner[span, :] = (swished * up_part).astype(bf16)
        gate_grad = inner_grad * up_part * sigmoid * (1.0 + gate_part * (1.0 - sigmoid))
        gate_low, up_low = gate_grad.astype(bf16), (inner_grad * swished).astype(bf16)
        gate_back[span, :] = gate_low
        up_back[span, :] = up_low
        total[span, :] += contract(gate_low, gate_weight, 1, 1) + contract(up_low, up_weight, 1, 1)

    @pl.when(step >= 2)
    def _():
        for copy in sends(step - 2):
            copy.wait_send()

    slot, half = step % 2, width // 2
    rows = contract(inner[...], grad_low[...], 0, 0).astype(bf16)
    down_part[slot, 0, 0] = rows[:, :half]
    down_part[slot, 1, 0] = rows[:, half:]
    for i, back in enumerate((gate_back, up_back)):
        columns = contract(hidden_low[...], back[...], 0, 0).astype(bf16)
        wide_part[slot, 0, i] = columns[:, :run]
        wide_part[slot, 1, i] = columns[:, run:]
    for copy in sends(step):
        copy.start()

    @pl.when(step >= 1)
    def _():
        add_cores(step - 1)

    @pl.when(step == last)
    def _():
        first_norm_back(rows_block, normed, inverse, norms, total, grad_first, first_low, norm_grads)
        add_cores(step)
        for copy in [*sends(step - 1), *sends(step)]:
            copy.wait_send()

        @pl.loop(0, last + 1)
        def _(j):
            for copy in keeps(j):
                copy.wait()


def paired_backward(
    grad_low, hidden_low, gate, up, gate_up, down, before, normed, inverse, norms
):
    length, width = hidden_low.shape
    count, _, block = gate.shape
    run = block // 2
    cols = lambda shift: pl.BlockSpec((width, run), lambda j: (0, shift * count + j))
    kept = pl.BlockSpec((1, length, block), lambda j: (j, 0, 0))
    anywhere = pl.BlockSpec(memory_space=pl.ANY)
    full = whole(length, width)
    dma = pltpu.SemaphoreType.DMA
    wide, narrow = (2, width, run), (1, block, width // 2)
    return pl.pallas_call(
        functools.partial(paired_backward_kernel, min(256, length)),
        grid=(count,),
        in_specs=[
            full,
            full,
            kept,
            kept,
            cols(0),
            cols(1),
            cols(2),
            cols(3),
            pl.BlockSpec((run, width), lambda j: (j, 0)),
            pl.BlockSpec((run, width), lambda j: (count + j, 0)),
            anywhere,
            full,
            whole(length, 1),
            whole(*norms.shape),
        ],
        out_specs=[anywhere, anywhere, full, full, whole(2, width)],
        out_shape=[
            jax.ShapeDtypeStruct((count,) + wide, bf16),
            jax.ShapeDtypeStruct((count,) + narrow, bf16),
            jax.ShapeDtypeStruct((length, width), f32),
            jax.ShapeDtypeStruct((length, width), bf16),
            jax.ShapeDtypeStruct((2, width), f32),
        ],
        scratch_shapes=[pltpu.VMEM((length, width), f32)]
        + [pltpu.VMEM((length, block), bf16)] * 3
        + [
            pltpu.VMEM((2, 2) + wide, bf16),
            pltpu.VMEM((2, 2) + narrow, bf16),
            pltpu.VMEM((count,) + wide, bf16),
            pltpu.VMEM((count,) + narrow, bf16),
            dma,
            dma((2, count, 2)),
            dma((2, count)),
        ],
        compiler_params=params(collective_id=3, has_side_effects=True),
        cost_estimate=cost(12 * length * width * down.shape[0], 8 * length * down.shape[0]),
        name="feed_backward",
    )(grad_low, hidden_low, gate, up, *[gate_up] * 4, down, down, before, normed, inverse, norms)


class Links:
    def __init__(self, mesh):
        self.sizes = {"dp": mesh.shape["dp"], "shard": mesh.shape["shard"]}
        chips = self.sizes["dp"] // 2
        near = 2 if chips % 2 == 0 else 1
        self.core = ("dp", 1, 2)
        self.near = ("dp", 2, near)
        self.far = ("dp", 2 * near, chips // near)
        self.shard = ("shard", 1, self.sizes["shard"])

    def place(self, digit):
        axis, stride, size = digit
        return (lax.axis_index(axis) // stride) % size

    def shift(self, value, digit, step):
        axis, stride, size = digit
        pairs = []
        for i in range(self.sizes[axis]):
            own = (i // stride) % size
            pairs.append((i, i + ((own + step) % size - own) * stride))
        return lax.ppermute(value, axis, pairs)

    def scatter_sum(self, value, digit, dim):
        size = digit[2]
        if size == 1:
            return value
        own = self.place(digit)
        width = value.shape[dim] // size

        def piece(index):
            return lax.dynamic_slice_in_dim(value, index * width, width, dim)

        total = piece(own).astype(f32)
        for step in range(1, size):
            total += self.shift(piece((own + step) % size), digit, step).astype(f32)
        return total.astype(bf16)

    def gather(self, value, digit, dim):
        size = digit[2]
        if size == 1:
            return value
        own = self.place(digit)
        width = value.shape[dim]
        if size == 2:
            other = self.shift(value, digit, 1)
            first = jnp.where(own == 0, value, other)
            second = jnp.where(own == 0, other, value)
            return jnp.concatenate([first, second], axis=dim)
        shape = list(value.shape)
        shape[dim] *= size
        full = lax.dynamic_update_slice_in_dim(
            jnp.zeros(shape, value.dtype), value, own * width, dim
        )
        for step in range(1, size):
            came = self.shift(value, digit, step)
            full = lax.dynamic_update_slice_in_dim(
                full, came, ((own - step) % size) * width, dim
            )
        return full

    def gather_rows(self, value, spread):
        parts = [self.core, self.near] if spread else [self.core]
        piece = value
        for digit in parts:
            width = piece.shape[0] // digit[2]
            piece = lax.dynamic_slice_in_dim(piece, self.place(digit) * width, width, 0)
        size = self.shard[2]
        rows = value.shape[0]
        own = self.place(self.shard)
        full = lax.dynamic_update_slice_in_dim(
            jnp.zeros((size * rows, value.shape[1]), value.dtype), value, own * rows, 0
        )
        for step in range(1, size):
            came = self.shift(piece, self.shard, step)
            for digit in reversed(parts):
                came = self.gather(came, digit, 0)
            full = lax.dynamic_update_slice_in_dim(full, came, ((own - step) % size) * rows, 0)
        return full

    def total(self, grads):
        grads = self.scatter_sum(grads, self.core, 1)
        grads = self.scatter_sum(grads, self.shard, 0)
        grads = self.scatter_sum(grads, self.near, 0)
        grads = self.scatter_sum(grads, self.far, 0)
        grads = self.gather(grads, self.far, 0)
        grads = self.gather(grads, self.near, 0)
        return self.gather(grads, self.core, 1)


def adam_update(weight, first_moment, second_moment, gradient, rate, decay_on):
    first_new = beta_first * first_moment + (1.0 - beta_first) * gradient
    second_new = beta_second * second_moment + (1.0 - beta_second) * gradient * gradient
    fix_first = 1.0 - beta_first**STEP
    fix_second = 1.0 - beta_second**STEP
    direction = first_new / fix_first / (jnp.sqrt(second_new / fix_second) + adam_eps)
    return (weight - rate * (direction + decay_on * weight), first_new, second_new)


def fits(mesh, length, rows, long_rows):
    far = mesh.shape["dp"] // 4
    return (
        mesh.shape["shard"] == 2
        and mesh.shape["dp"] == 16
        and length % 512 == 0
        and rows % (32 * far) == 0
        and long_rows % (4 * Back.update_cols) == 0
        and long_rows % (128 * HEADS) == 0
        and 128 % (32 * far) == 0
    )


class Front:
    def __init__(self, mesh, length, width, rows, matrices):
        self.length, self.width, self.rows = length, width, rows
        self.matrices = matrices
        self.units = []
        for i, shape in enumerate(matrices):
            for low in range(0, shape[0], rows):
                for left in range(0, shape[1], width):
                    self.units.append((i, low, left))

    def __call__(self, tokens, masters, cosine, sine):
        length, width, rows = self.length, self.width, self.rows
        dma = pltpu.SemaphoreType.DMA
        anywhere = pl.BlockSpec(memory_space=pl.ANY)
        fulls = [jax.ShapeDtypeStruct((2 * shape[0], shape[1]), bf16) for shape in self.matrices]
        count = 3 + len(self.units)
        return pl.pallas_call(
            self.kernel,
            grid=(HEADS,),
            in_specs=[whole(length, width), whole(*cosine.shape), whole(*sine.shape)] + [anywhere] * 4,
            out_specs=[
                pl.BlockSpec((HEAD_DIM, length), lambda h: (h, 0)),
                pl.BlockSpec((1, length, length), lambda h: (h, 0, 0)),
            ]
            + [anywhere] * 5,
            out_shape=[
                jax.ShapeDtypeStruct((width, length), bf16),
                jax.ShapeDtypeStruct((HEADS, length, length), bf16),
                jax.ShapeDtypeStruct((3 * width, length), bf16),
                jax.ShapeDtypeStruct((width, 3 * width), bf16),
                *fulls,
            ],
            scratch_shapes=[
                pltpu.VMEM((3 * width, length), bf16),
                pltpu.VMEM((3, width, width), bf16),
                pltpu.VMEM((len(self.units), rows, width), bf16),
                pltpu.VMEM((3, rows, width), f32),
                dma((3, count, 2)),
                dma((3,)),
                dma((len(self.units),)),
                dma((4,)),
            ],
            compiler_params=params(collective_id=2, has_side_effects=True),
            name="front",
        )(tokens, cosine, sine, *masters)

    def kernel(
        self,
        tokens,
        cosine,
        sine,
        master_qkv,
        master_out,
        master_gate_up,
        master_down,
        mixed,
        weights,
        joined_out,
        qkv_out,
        full_out,
        full_gate_up,
        full_down,
        joined,
        qkv,
        own_low,
        wide,
        pair_sem,
        load_sem,
        own_sem,
        out_sem,
    ):
        width, rows = self.width, self.rows
        step = pl.program_id(0)
        dp, shard = lax.axis_index("dp"), lax.axis_index("shard")
        core, near = dp % 2, dp // 2 % 2
        peers = [(dp, 1 - shard), (dp + 2 - 4 * near, shard), (dp + 1 - 2 * core, shard)]
        masters, fulls = [master_out, master_gate_up, master_down], [full_out, full_gate_up, full_down]
        count = len(self.units)

        def region(u, stage):
            side = shard if stage == 0 else 1 - shard
            height = rows // 4 if stage < 2 else rows // 2
            low = core * (rows // 2) + (near * (rows // 4) if stage < 2 else 0)
            if u < 3:
                place = pl.ds(pl.multiple_of(side * rows + low, 16), height)
                return qkv.at[u, place], qkv.at[u, place]
            matrix, first, left = self.units[u - 3]
            place = pl.ds(pl.multiple_of(side * self.matrices[matrix][0] + first + low, 16), height)
            full = fulls[matrix].at[place, pl.ds(left, width)]
            if stage == 0:
                return own_low.at[u - 3, pl.ds(pl.multiple_of(low, 16), height)], full
            return full, full

        def copy(u, stage):
            source, target = region(u, stage)
            return pltpu.make_async_remote_copy(
                src_ref=source,
                dst_ref=target,
                send_sem=pair_sem.at[stage, u, 0],
                recv_sem=pair_sem.at[stage, u, 1],
                device_id=peers[stage],
                device_id_type=pl.DeviceIdType.MESH,
            )

        def pass_on(u, stage):
            copy(u, stage - 1).wait_recv()
            copy(u, stage).start()

        def load(u):
            if u < 3:
                source = master_qkv.at[:, pl.ds(u * width, width)]
            else:
                matrix, first, left = self.units[u - 3]
                source = masters[matrix].at[pl.ds(first, rows), pl.ds(left, width)]
            return pltpu.make_async_copy(source, wide.at[u % 3], load_sem.at[u % 3])

        def own_rows(u):
            matrix, first, left = self.units[u - 3]
            place = pl.ds(pl.multiple_of(shard * self.matrices[matrix][0] + first, 16), rows)
            return pltpu.make_async_copy(
                own_low.at[u - 3], fulls[matrix].at[place, pl.ds(left, width)], own_sem.at[u - 3]
            )

        def round_unit(u):
            load(u).wait()
            target = qkv.at[u, pl.ds(pl.multiple_of(shard * rows, 16), rows)] if u < 3 else own_low.at[u - 3]

            @pl.loop(0, rows // 16)
            def _(i):
                span = pl.ds(pl.multiple_of(i * 16, 16), 16)
                target[span, :] = wide[u % 3, span, :].astype(bf16)

            if u + 3 < 3 + count:
                load(u + 3).start()
            if u >= 3:
                own_rows(u).start()

        def project(u):
            block = 4 * HEAD_DIM
            half = HEAD_DIM // 2
            for left in range(0, width, block):
                part = contract(qkv[u, :, left : left + block], tokens[...], 0, 1)
                if u == 2:
                    joined[u * width + left : u * width + left + block] = part.astype(bf16)
                    continue
                scale = 1.0 / math.sqrt(HEAD_DIM) if u == 0 else 1.0
                for low in range(0, block, HEAD_DIM):
                    t1, t2 = part[low : low + half], part[low + half : low + 2 * half]
                    cos, sin = cosine[...] * scale, sine[...] * scale
                    to = u * width + left + low
                    joined[to : to + half] = (t1 * cos - t2 * sin).astype(bf16)
                    joined[to + half : to + 2 * half] = (t2 * cos + t1 * sin).astype(bf16)

        def keep(i):
            if i == 3:
                return pltpu.make_async_copy(joined, joined_out, out_sem.at[3])
            return pltpu.make_async_copy(qkv.at[i], qkv_out.at[:, pl.ds(i * width, width)], out_sem.at[i])

        @pl.when(step == 0)
        def _():
            for u in range(3):
                load(u).start()
            barrier = pltpu.get_barrier_semaphore()
            for peer in peers:
                pl.semaphore_signal(barrier, inc=1, device_id=peer, device_id_type=pl.DeviceIdType.MESH)
            pl.semaphore_wait(barrier, len(peers))
            for u in range(3):
                round_unit(u)
                copy(u, 0).start()
            round_unit(3)
            round_unit(4)
            for u in range(2):
                pass_on(u, 1)
            copy(3, 0).start()
            pass_on(0, 2)
            pass_on(2, 1)
            copy(4, 0).start()
            copy(0, 2).wait_recv()
            project(0)
            pass_on(1, 2)
            pass_on(2, 2)
            copy(1, 2).wait_recv()
            project(1)
            copy(2, 2).wait_recv()
            project(2)
            for i in range(4):
                keep(i).start()

        for s in range(1, HEADS):

            @pl.when(step == s)
            def _(s=s):
                if 4 + s < 3 + count:
                    round_unit(4 + s)
                if 2 + s < 3 + count:
                    pass_on(2 + s, 1)
                if 4 + s < 3 + count:
                    copy(4 + s, 0).start()
                if 3 <= 1 + s < 3 + count:
                    pass_on(1 + s, 2)

        head = lambda part: joined.at[
            pl.ds(pl.multiple_of(part * width + step * HEAD_DIM, HEAD_DIM), HEAD_DIM)
        ]
        attend_head(head(0), head(1), head(2), mixed, weights)

        @pl.when(step == HEADS - 1)
        def _():
            for u in range(4 + HEADS, 3 + count):
                round_unit(u)
                copy(u, 0).start()
            for u in range(2 + HEADS, 3 + count):
                pass_on(u, 1)
            for u in range(1 + HEADS, 3 + count):
                pass_on(u, 2)
            for u in range(3, 3 + count):
                copy(u, 2).wait_recv()
                own_rows(u).wait()
            for u in range(3 + count):
                for stage in range(3):
                    copy(u, stage).wait_send()
            for i in range(4):
                keep(i).wait()


class Back:
    ahead = 3
    steps = ("core", "shard", "near", "low", "high", "high total", "low total", "near total", "core total")
    update_cols = 384

    def __init__(self, mesh, length, width, inner, rows, long_rows, runs):
        self.far_size = mesh.shape["dp"] // 4
        self.length, self.width, self.inner = length, width, inner
        self.rows, self.long_rows, self.runs = rows, long_rows, runs
        self.scale = 1.0 / math.sqrt(length * mesh.shape["dp"] * mesh.shape["shard"])
        self.run = inner // (2 * runs)
        self.units = [[("wide", j), ("down", j)] for j in range(runs)] + [[("square", u)] for u in range(4)]
        self.groups = {
            "wide": (runs, 2, rows, self.run),
            "down": (runs, 1, self.run, width // 2),
            "square": (4, 1, rows, width // 2),
        }
        blocks, side = [], self.update_cols
        for part in range(2):
            for left in range(0, inner, side):
                last = (left % (inner // 2) + side) * 2 * runs // inner - 1
                blocks.append((last, 0, 0, part * inner + left, side, (part, left)))
        for low in range(0, long_rows, rows):
            last = (low + rows) * runs // long_rows - 1
            blocks.append((last, 1, low, 0, width, (0, 0)))
        for u in range(3):
            blocks.append((runs + u, 3, 0, u * width, width, (0, u * width)))
        blocks.append((runs + 3, 2, 0, 0, width, (0, 0)))
        self.blocks = sorted(blocks, key=lambda block: block[0])

    def __call__(
        self,
        joined,
        weights,
        mixed,
        first_low,
        weight_out,
        cosine,
        sine,
        wide,
        down,
        tokens,
        weight_qkv,
        grad_first,
        masters,
        norm_grads,
        norm_state,
    ):
        length, width, rows = self.length, self.width, self.rows
        anywhere = pl.BlockSpec(memory_space=pl.ANY)
        once = lambda array: pl.BlockSpec(
            array.shape, lambda h: (0,) * array.ndim, pipeline_mode=pl.Buffered(1)
        )
        head_rows = lambda part: pl.BlockSpec((HEAD_DIM, length), lambda h: (part * HEADS + h, 0))
        state = [part for master in masters for part in master]
        outs = []
        for master, _, _ in masters:
            full = (2 * master.shape[0], master.shape[1])
            outs += [
                jax.ShapeDtypeStruct(full, bf16),
                jax.ShapeDtypeStruct(master.shape, f32),
                jax.ShapeDtypeStruct(master.shape, f32),
            ]
        totals = [
            jax.ShapeDtypeStruct((2, rows, self.inner), bf16),
            jax.ShapeDtypeStruct((1, self.long_rows, width), bf16),
            jax.ShapeDtypeStruct((1, rows, width), bf16),
            jax.ShapeDtypeStruct((1, rows, 3 * width), bf16),
        ]
        norm_outs = [jax.ShapeDtypeStruct(norm_grads.shape, f32)] * 3
        dma = pltpu.SemaphoreType.DMA
        far = max(self.far_size - 1, 1)
        scratch = [
            pltpu.VMEM((width, length), bf16),
            pltpu.VMEM((3 * width, length), bf16),
            pltpu.VMEM((length, width), bf16),
            pltpu.VMEM((width, 3 * width), bf16),
            pltpu.VMEM((length, width), f32),
            pltpu.VMEM((4, 2, width, width // 2), bf16),
            pltpu.VMEM((4, 1, width, width // 2), bf16),
        ]
        for name, (count, lead, height, columns) in self.groups.items():
            slots = 1 if name == "square" else self.ahead + 1
            heights = [height // 2**i for i in range(4)]
            scratch += [pltpu.VMEM((count, lead, rows_left, columns), bf16) for rows_left in heights]
            scratch += [
                pltpu.VMEM((slots, lead, height if slots > 1 else 16, columns), bf16),
                dma((len(self.steps), count, 2)),
                dma((2, count)),
            ]
        slots = (2, rows, self.update_cols)
        scratch += [
            pltpu.VMEM((3,) + slots, f32),
            pltpu.VMEM(slots, bf16),
            pltpu.VMEM((2,) + slots, f32),
            pltpu.VMEM(slots, bf16),
            pltpu.VMEM((3,) + norm_grads.shape, f32),
            pltpu.VMEM((self.far_size,) + norm_grads.shape, f32),
            dma((3 + far,)),
            dma((3 + far,)),
            dma((2, 4)),
            dma((2, 3)),
            dma((3, len(self.blocks), 2)),
            dma((4,)),
        ]
        results = pl.pallas_call(
            self.kernel,
            grid=(HEADS,),
            in_specs=[
                head_rows(0),
                head_rows(1),
                head_rows(2),
                pl.BlockSpec((1, length, length), lambda h: (h, 0, 0)),
                once(mixed),
                once(first_low),
                once(weight_out),
                once(cosine),
                once(sine),
                *[once(array) for array in (norm_grads, *norm_state)],
            ]
            + [anywhere] * (5 + len(state)),
            out_specs=[anywhere] * (len(outs) + len(totals)) + [whole(*norm_grads.shape)] * 3 + [anywhere],
            out_shape=outs + totals + norm_outs + [jax.ShapeDtypeStruct((length, width), bf16)],
            scratch_shapes=scratch,
            compiler_params=params(collective_id=1, has_side_effects=True),
            name="back",
        )(
            joined,
            joined,
            joined,
            weights,
            mixed,
            first_low,
            weight_out,
            cosine,
            sine,
            norm_grads,
            *norm_state,
            wide,
            down,
            tokens,
            weight_qkv,
            grad_first,
            *state,
        )
        updated = [tuple(results[3 * i : 3 * i + 3]) for i in range(len(masters))]
        return updated, tuple(results[-4:-1]), results[-1]

    def kernel(self, *refs):
        refs = list(refs)

        def take(number):
            taken = refs[:number]
            del refs[:number]
            return taken

        length, width, rows, sizes = self.length, self.width, self.rows, self.far_size
        queries, key_rows, value_rows, weights, mixed, first_low, weight_out, cosine, sine = take(9)
        norm_in, norms, norm_first, norm_second = take(4)
        wide_in, down_in, tokens_in, qkv_in, grad_first_in = take(5)
        state = take(12)
        outs, totals, norm_outs, (input_grad,) = take(12), take(4), take(3), take(1)
        grad_mixed, grad_joined, tokens, weight_qkv, grad_first, square, square_sum = take(7)
        names = ("shard", "near", "low", "high", "keep", "pair_sem", "own_sem")
        groups = {name: dict(zip(names, take(7), strict=True)) for name in self.groups}
        load_buf, grad_buf, store_buf, new_buf, norm_sum, norm_far = take(6)
        norm_send, norm_recv, load_sem, store_sem, new_sem, in_sem = take(6)

        step = pl.program_id(0)
        dp, shard = lax.axis_index("dp"), lax.axis_index("shard")
        core, near, far = dp % 2, dp // 2 % 2, dp // 4
        low_bit, high_bit = far % 2, far // 2
        core_peer, near_peer, shard_peer = (dp + 1 - 2 * core, shard), (dp + 2 - 4 * near, shard), (dp, 1 - shard)

        def far_peer(hop):
            return (dp + ((far + hop) % sizes - far) * 4, shard)

        def remote(source, target, sent, came, peer):
            return pltpu.make_async_remote_copy(
                src_ref=source,
                dst_ref=target,
                send_sem=sent,
                recv_sem=came,
                device_id=peer,
                device_id_type=pl.DeviceIdType.MESH,
            )

        def span(low, height):
            return pl.ds(pl.multiple_of(low, 16), height)

        peers = {
            "core": core_peer,
            "shard": shard_peer,
            "near": near_peer,
            "low": (dp + 4 - 8 * low_bit, shard),
            "high": (dp + 8 - 16 * high_bit, shard),
        }
        bits = {"shard": shard, "near": near, "low": low_bit, "high": high_bit}
        axes = ["shard", "near", "low", "high"]

        class Part:
            def __init__(part, group, index):
                part.group, part.index = group, index
                _, part.lead, part.height, part.columns = self.groups[group]
                part.bufs = groups[group]
                part.held = group == "square"
                part.source = {"wide": wide_in, "down": down_in, "square": square_sum}[group].at[index]
                if part.held:
                    part.keep = part.source.at[:, span(shard * part.height, part.height)]
                else:
                    part.keep = part.bufs["keep"].at[index % (self.ahead + 1)]

            def came(part, axis):
                return part.bufs[axis].at[part.index]

            def rows_after(part, axis):
                low, height = 0, part.height
                for name in axes[1 : axes.index(axis) + 1]:
                    height //= 2
                    low = low + bits[name] * height
                return low, height

            def total(part, axis):
                low, height = part.rows_after(axis)
                index, side = part.index, core
                if part.group == "wide":
                    left = side * (self.inner // 2) + index * part.columns
                    return totals[0].at[:, span(low, height), pl.ds(pl.multiple_of(left, 128), part.columns)]
                left = pl.multiple_of(side * part.columns, 128)
                if part.group == "down":
                    return totals[1].at[:, span(index * part.height + low, height), pl.ds(left, part.columns)]
                if index == 3:
                    return totals[2].at[:, span(low, height), pl.ds(left, part.columns)]
                return totals[3].at[:, span(low, height), pl.ds(index * width + left, part.columns)]

            def copy(part, stage):
                axis, *back = stage.split()
                if back:
                    before = {"high": "high", "low": "low", "near": "near", "core": "shard"}[axis]
                    source = target = part.total(before)
                elif axis == "core":
                    source, target = square.at[part.index, pl.ds(1 - core, 1)], part.source
                else:
                    own = part.source if axis == "shard" else part.came(axes[axes.index(axis) - 1])
                    _, height = part.rows_after(axis)
                    source, target = own.at[:, span((1 - bits[axis]) * height, height)], part.came(axis)
                sem = part.bufs["pair_sem"].at[self.steps.index(stage), part.index]
                return remote(source, target, sem.at[0], sem.at[1], peers[axis])

            def kept(part):
                return pltpu.make_async_copy(
                    part.source.at[:, span(shard * part.height, part.height)],
                    part.keep,
                    part.bufs["own_sem"].at[0, part.index],
                )

            def own_total(part):
                return pltpu.make_async_copy(
                    part.came("high"), part.total("high"), part.bufs["own_sem"].at[1, part.index]
                )

        units = [[Part(group, index) for group, index in unit] for unit in self.units]
        started = []

        def start(k, stage):
            for part in units[k]:
                part.copy(stage).start()
            started.append((k, stage))

        def arrived(k, stage):
            for part in units[k]:
                part.copy(stage).wait_recv()

        def add_rows(target, sources, lead, height):
            tile = next(size for size in (64, 48, 16) if height % size == 0)

            @pl.loop(0, height // tile)
            def _(i):
                place = span(i * tile, tile)
                for k in range(lead):
                    value = sources[0][k, place, :].astype(f32)
                    for source in sources[1:]:
                        value += source[k, place, :].astype(f32)
                    target[k, place, :] = value.astype(bf16)

        def start_shard(k):
            for part in units[k]:
                if part.held:
                    arrived(k, "core")
                    own = square.at[part.index, pl.ds(core, 1)]
                    add_rows(part.source, [part.source, own], 1, 2 * part.height)
                else:
                    part.kept().start()
            start(k, "shard")

        def take_sum(k, axis):
            arrived(k, axis)
            for part in units[k]:
                came = part.came(axis)
                if axis == "shard":
                    if not part.held:
                        part.kept().wait()
                    own = part.keep
                else:
                    _, height = part.rows_after(axis)
                    own = part.came(axes[axes.index(axis) - 1]).at[:, span(bits[axis] * height, height)]
                add_rows(came, [came, own], part.lead, came.shape[1])
            if axis != "high":
                start(k, axes[axes.index(axis) + 1])
                return
            for part in units[k]:
                part.own_total().start()
            for part in units[k]:
                part.own_total().wait()
            start(k, "high total")

        def take_total(k, axis):
            arrived(k, axis + " total")
            start(k, {"high": "low", "low": "near", "near": "core"}[axis] + " total")

        updates = [
            (b, sub) for b, block in enumerate(self.blocks) for sub in range(block[4] // self.update_cols)
        ]

        def update_place(n):
            b, sub = updates[n]
            _, matrix, low, left, _, (part, total_left) = self.blocks[b]
            shift = sub * self.update_cols
            cols = pl.ds(left + shift, self.update_cols)
            return n % 2, matrix, low, cols, part, pl.ds(total_left + shift, self.update_cols)

        def state_loads(n):
            slot, matrix, low, cols, *_ = update_place(n)
            place = pl.ds(low, rows)
            return [
                pltpu.make_async_copy(
                    state[3 * matrix + i].at[place, cols], load_buf.at[i, slot], load_sem.at[slot, i]
                )
                for i in range(3)
            ]

        def grad_load(n):
            slot, matrix, low, _, part, cols = update_place(n)
            grads = totals[matrix].at[part, pl.ds(low, rows), cols]
            return pltpu.make_async_copy(grads, grad_buf.at[slot], load_sem.at[slot, 3])

        def stores_of(n):
            slot, matrix, low, cols, *_ = update_place(n)
            place = pl.ds(low, rows)
            full = span(shard * state[3 * matrix].shape[0] + low, rows)
            return [
                pltpu.make_async_copy(new_buf.at[slot], outs[3 * matrix].at[full, cols], store_sem.at[slot, 2])
            ] + [
                pltpu.make_async_copy(
                    store_buf.at[i, slot], outs[3 * matrix + 1 + i].at[place, cols], store_sem.at[slot, i]
                )
                for i in range(2)
            ]

        waiting = {}

        def load_state(n):
            if n < len(updates):
                for copy in state_loads(n):
                    copy.start()

        def settle(n, left):
            while len(waiting[n]) > left:
                waiting[n].pop(0).wait()

        def update(n):
            slot = n % 2
            for copy in [*state_loads(n), grad_load(n)]:
                copy.wait()
            if n >= 2:
                settle(n - 2, 0)

            @pl.loop(0, rows // 16)
            def _(i):
                place = span(i * 16, 16)
                new, first_new, second_new = adam_update(
                    load_buf[0, slot, place, :],
                    load_buf[1, slot, place, :],
                    load_buf[2, slot, place, :],
                    grad_buf[slot, place, :].astype(f32) * self.scale,
                    learn_rate,
                    decay_rate,
                )
                store_buf[0, slot, place, :] = first_new
                store_buf[1, slot, place, :] = second_new
                new_buf[slot, place, :] = new.astype(bf16)

            waiting[n] = stores_of(n)
            for copy in waiting[n]:
                copy.start()
            load_state(n + 2)

        def new_copy(b, stage):
            _, matrix, first, left, columns, _ = self.blocks[b]
            side = shard if stage == 0 else 1 - shard
            height = rows // 4 if stage < 2 else rows // 2
            by_near = b % 2 == 0
            quarter = near if by_near else low_bit
            low = core * (rows // 2) + (quarter * (rows // 4) if stage < 2 else 0)
            place = outs[3 * matrix].at[
                span(side * state[3 * matrix].shape[0] + first + low, height), pl.ds(left, columns)
            ]
            peer = (shard_peer, near_peer if by_near else peers["low"], core_peer)[stage]
            return remote(place, place, new_sem.at[stage, b, 0], new_sem.at[stage, b, 1], peer)

        def pass_new(b, stage):
            if stage > 0:
                new_copy(b, stage - 1).wait_recv()
            new_copy(b, stage).start()

        def norm_copy(stage, hop=0):
            if stage < 3:
                source = norm_in if stage == 0 else norm_sum.at[stage - 1]
                peer = (core_peer, shard_peer, near_peer)[stage]
                return remote(source, norm_sum.at[stage], norm_send.at[stage], norm_recv.at[stage], peer)
            return remote(
                norm_sum.at[2], norm_far.at[far], norm_send.at[2 + hop], norm_recv.at[2 + hop], far_peer(hop)
            )

        def norm_stage(stage):
            if 1 <= stage <= 3:
                norm_copy(stage - 1).wait_recv()
                before = norm_in[...] if stage == 1 else norm_sum[stage - 2]
                norm_sum[stage - 1] += before
            if stage < 3:
                norm_copy(stage).start()
            elif stage == 3:
                norm_far[far] = norm_sum[2]
                for hop in range(1, sizes):
                    norm_copy(3, hop).start()
            else:
                for hop in range(1, sizes):
                    norm_copy(3, hop).wait_recv()
                total = norm_far[0]
                for place in range(1, sizes):
                    total += norm_far[place]
                new, first_new, second_new = adam_update(
                    norms[...], norm_first[...], norm_second[...], total * self.scale, norm_rate, 0.0
                )
                norm_outs[0][...] = new
                norm_outs[1][...] = first_new
                norm_outs[2][...] = second_new
                for stage in range(3):
                    norm_copy(stage).wait_send()
                for hop in range(1, sizes):
                    norm_copy(3, hop).wait_send()

        count, runs = len(self.units), self.runs
        stages = [functools.partial(take_sum, axis=axis) for axis in axes] + [
            functools.partial(take_total, axis=axis) for axis in ("high", "low", "near")
        ]
        depth = len(stages)
        progress = {"ready": 0, "grad": 0, "update": 0, "near": 0, "core": 0}
        sent_at, near_at = [], []

        def prefetch():
            n = progress["grad"]
            if n < progress["ready"] and n < progress["update"] + 2:
                grad_load(n).start()
                progress["grad"] += 1

        def some_updates(t, most):
            for _ in range(most):
                n = progress["update"]
                if n == progress["ready"]:
                    break
                prefetch()
                prefetch()
                update(n)
                progress["update"] += 1
                b, sub = updates[n]
                if sub == self.blocks[b][4] // self.update_cols - 1:
                    for m in range(n - sub, n + 1):
                        settle(m, 2)
                    pass_new(b, 0)
                    sent_at.append(t)

        def slot(t, most):
            busy = t < count + depth
            for at, lag, stage, name in ((near_at, 2, 2, "core"), (sent_at, 4 if busy else 1, 1, "near")):
                while progress[name] < len(at) and at[progress[name]] <= t - (lag if busy else 1):
                    pass_new(progress[name], stage)
                    progress[name] += 1
                    if stage == 1:
                        near_at.append(t)
            if 0 <= t - depth - 1 < count:
                arrived(t - depth - 1, "core total")
                progress["ready"] = sum(self.blocks[b][0] <= t - depth - 1 for b, _ in updates)
                prefetch()
            for late in range(depth - 1, 0, -1):
                if 0 <= t - late - 1 < count:
                    stages[late](t - late - 1)
            some_updates(t, most)
            if t < count:
                stages[0](t)
                if t + self.ahead < count:
                    start_shard(t + self.ahead)

        inputs = [
            pltpu.make_async_copy(tokens_in, tokens, in_sem.at[0]),
            pltpu.make_async_copy(qkv_in, weight_qkv, in_sem.at[1]),
            pltpu.make_async_copy(grad_first_in, grad_first, in_sem.at[2]),
        ]

        @pl.when(step == 0)
        def _():
            greeted = [core_peer, near_peer, shard_peer] + [far_peer(hop) for hop in range(1, sizes)]
            barrier = pltpu.get_barrier_semaphore()
            for peer in greeted:
                pl.semaphore_signal(barrier, inc=1, device_id=peer, device_id_type=pl.DeviceIdType.MESH)
            pl.semaphore_wait(barrier, len(greeted))
            for k in range(self.ahead):
                start_shard(k)
            norm_stage(0)
            for copy in inputs:
                copy.start()
            load_state(0)
            load_state(1)
            block = 256
            for low in range(0, width, block):
                grad_mixed[low : low + block] = contract(
                    weight_out[low : low + block], first_low[...], 1, 1
                ).astype(bf16)

        head = lambda part: grad_joined.at[
            pl.ds(pl.multiple_of(part * width + step * HEAD_DIM, HEAD_DIM), HEAD_DIM)
        ]
        own_head = pl.ds(pl.multiple_of(step * HEAD_DIM, HEAD_DIM), HEAD_DIM)
        attend_back_kernel(
            min(256, length),
            queries,
            key_rows,
            value_rows,
            mixed.at[own_head],
            grad_mixed.at[own_head],
            weights,
            cosine,
            sine,
            head(0),
            head(1),
            head(2),
        )

        early = {2: 0, 5: 1, 8: 2}
        for at, t in early.items():

            @pl.when(step == at)
            def _(t=t):
                norm_stage(1 + t)
                slot(t, 0)

        @pl.when(step == HEADS - 1)
        def _():
            half = width // 2
            t = len(early)

            def keep_square(u, value):
                square[u, 0] = value[:, :half].astype(bf16)
                square[u, 1] = value[:, half:].astype(bf16)

            def weight_grad(u):
                keep_square(u, contract(tokens[...], grad_joined[u * width : (u + 1) * width], 0, 1))

            def input_rows(low, height):
                for place in range(low, low + height, min(256, length)):
                    block = slice(place, place + min(256, length))
                    rows_sum = contract(grad_joined[:, block], weight_qkv[...], 0, 1)
                    tokens[block] = (grad_first[block] + rows_sum).astype(bf16)

            slot(t, 0)
            inputs[0].wait()
            weight_grad(0)
            weight_grad(1)
            slot(t + 1, 0)
            norm_stage(4)
            weight_grad(2)
            keep_square(3, contract(mixed[...], first_low[...], 1, 0))
            for u in range(4):
                start(runs + u, "core")
            slot(t + 2, 0)
            inputs[1].wait()
            inputs[2].wait()
            input_rows(0, length // 2)
            slot(t + 3, 0)
            input_rows(length // 2, length // 2)
            result = pltpu.make_async_copy(tokens, input_grad, in_sem.at[3])
            result.start()
            later = t + 4
            while later < count + depth + 1 or progress["core"] < len(self.blocks):
                slot(later, 3)
                later += 1
            for b in range(len(self.blocks)):
                new_copy(b, 2).wait_recv()
            for n in range(len(updates)):
                settle(n, 0)
            for k, stage in started:
                for part in units[k]:
                    part.copy(stage).wait_send()
            for b in range(len(self.blocks)):
                for stage in range(3):
                    new_copy(b, stage).wait_send()
            result.wait()


def shards(
    mesh,
    tokens,
    cotangent,
    master_qkv,
    first_qkv,
    second_qkv,
    master_out,
    first_out,
    second_out,
    master_gate_up,
    first_gate_up,
    second_gate_up,
    master_down,
    first_down,
    second_down,
    norms,
    norm_first,
    norm_second,
):
    links = Links(mesh)
    length, width = tokens.shape
    shard_count = mesh.shape["shard"]
    cosine, sine = rope_tables(length)

    scale_grad = 1.0 / math.sqrt(length * mesh.shape["dp"] * shard_count)
    masters = [
        (master_gate_up, first_gate_up, second_gate_up),
        (master_down, first_down, second_down),
        (master_out, first_out, second_out),
        (master_qkv, first_qkv, second_qkv),
    ]
    norm_state = (norms, norm_first, norm_second)
    if fits(mesh, length, master_qkv.shape[0], master_down.shape[0]):
        rows, long_rows = master_qkv.shape[0], master_down.shape[0]
        inner = shard_count * long_rows
        shapes = [master_out.shape, master_gate_up.shape, master_down.shape]
        mixed, weights, joined, weight_qkv, weight_out, weight_gate_up, weight_down = Front(
            mesh, length, width, rows, shapes
        )(tokens, [master_qkv, master_out, master_gate_up, master_down], cosine, sine)
        normed_one, inverse_one, hidden_low = project_out(tokens, mixed, weight_out, norms)
        gate, up, output, grad_second, grad_low, norm_two = paired_forward(
            hidden_low, weight_gate_up, weight_down, normed_one, norms, cotangent
        )
        wide, down, grad_first, first_low, norm_one = paired_backward(
            grad_low,
            hidden_low,
            gate,
            up,
            weight_gate_up,
            weight_down,
            grad_second,
            normed_one,
            inverse_one,
            norms,
        )
        updated, updated_norms, input_grad = Back(
            mesh, length, width, inner, rows, long_rows, gate.shape[0]
        )(
            joined,
            weights,
            mixed,
            first_low,
            weight_out,
            cosine,
            sine,
            wide,
            down,
            tokens,
            weight_qkv,
            grad_first,
            masters,
            jnp.concatenate([norm_one, norm_two]),
            norm_state,
        )
    else:
        weight_qkv = links.gather_rows(master_qkv.astype(bf16), False)
        weight_out = links.gather_rows(master_out.astype(bf16), False)
        weight_gate_up = links.gather_rows(master_gate_up.astype(bf16), True)
        weight_down = links.gather_rows(master_down.astype(bf16), True)
        joined = project_qkv(tokens, weight_qkv, cosine, sine)
        mixed, weights = attend_forward(joined)
        normed_one, inverse_one, hidden_low = project_out(tokens, mixed, weight_out, norms)
        gate, up, output, grad_second, grad_low, norm_two = feed_forward(
            hidden_low, weight_gate_up, weight_down, normed_one, norms, cotangent
        )
        gate_grad, up_grad, down_grad, grad_first, first_low, norm_one = feed_backward(
            grad_low,
            hidden_low,
            gate,
            up,
            weight_gate_up,
            weight_down,
            grad_second,
            normed_one,
            inverse_one,
            norms,
        )
        out_grad = contract(mixed, first_low, 1, 0).astype(bf16)
        mixed_grad = contract(weight_out, first_low, 1, 1).astype(bf16)
        joined_back = attend_backward(joined, mixed, mixed_grad, weights, cosine, sine)
        joined_back = jnp.concatenate(joined_back, axis=0)
        qkv_grad = contract(tokens, joined_back, 0, 1).astype(bf16)
        input_grad = (grad_first + contract(joined_back, weight_qkv, 0, 1)).astype(bf16)
        totals = [
            jnp.concatenate([links.total(gate_grad), links.total(up_grad)], axis=1),
            links.total(down_grad),
            links.total(out_grad),
            links.total(qkv_grad),
        ]
        updated = []
        for (master, first, second), total in zip(masters, totals, strict=True):
            new, first_new, second_new = adam_update(
                master, first, second, total.astype(f32) * scale_grad, learn_rate, decay_rate
            )
            updated.append((links.gather_rows(new.astype(bf16), True), first_new, second_new))
        norm_total = lax.psum(jnp.concatenate([norm_one, norm_two]), ("dp", "shard"))
        updated_norms = adam_update(*norm_state, norm_total * scale_grad, norm_rate, 0.0)
    (
        (full_gate_up, first_gate_up_new, second_gate_up_new),
        (full_down, first_down_new, second_down_new),
        (full_out, first_out_new, second_out_new),
        (full_qkv, first_qkv_new, second_qkv_new),
    ) = updated
    upd_norms, norm_first_new, norm_second_new = updated_norms
    return (
        output,
        input_grad,
        full_qkv,
        full_out,
        full_gate_up,
        full_down,
        first_qkv_new,
        second_qkv_new,
        first_out_new,
        second_out_new,
        first_gate_up_new,
        second_gate_up_new,
        first_down_new,
        second_down_new,
        upd_norms,
        norm_first_new,
        norm_second_new,
    )


def solution(mesh):
    rows, split, copied = P(("dp", "shard"), None), P("shard", None), P()
    return jax.shard_map(
        functools.partial(shards, mesh),
        mesh=mesh,
        in_specs=(rows, rows) + (split,) * 12 + (copied,) * 3,
        out_specs=(rows, rows) + (copied,) * 4 + (split,) * 8 + (copied,) * 3,
        check_vma=False,
    )
```

```python
import functools
import math

import jax
import jax.numpy as jnp
import numpy as np
from jax import lax
from jax.experimental import pallas as pl
from jax.experimental.pallas import tpu as pltpu
from jax.sharding import PartitionSpec as P

HEADS = 12
HEAD_DIM = 64
STEP = 3

norm_eps = 1e-12
rope_base = 1000.0
learn_rate = 0.03
norm_rate = 0.3
decay_rate = 0.1
adam_eps = 1e-08
beta_first = 0.5
beta_second = 0.5

f32, bf16 = jnp.float32, jnp.bfloat16
VMEM_BYTES = 56 * 2**20


def contract(left, right, left_dim, right_dim):
    return lax.dot_general(
        left, right, (((left_dim,), (right_dim,)), ((), ())), preferred_element_type=f32
    )


def params(**more):
    return pltpu.CompilerParams(vmem_limit_bytes=VMEM_BYTES, **more)


def cost(flops, moved, transcendentals=0):
    return pl.CostEstimate(
        flops=int(flops), bytes_accessed=int(moved), transcendentals=int(transcendentals)
    )


def whole(*shape):
    return pl.BlockSpec(shape, lambda *_: (0,) * len(shape))


def rope_tables(length):
    half = HEAD_DIM // 2
    frequency = np.float32(rope_base) ** (
        -(np.arange(half, dtype=np.float32) * np.float32(2.0 / HEAD_DIM))
    )
    angles = np.arange(length, dtype=np.float32)[None, :] * frequency[:, None]
    return jnp.asarray(np.cos(angles), f32), jnp.asarray(np.sin(angles), f32)


def qkv_kernel(blocks_rotated, heads_block, tokens, weight, cosine, sine, joined):
    step = pl.program_id(0)
    rows = contract(weight[...], tokens[...], 0, 1)
    half = HEAD_DIM // 2

    @pl.when(step < 2 * blocks_rotated)
    def _():
        scale = jnp.where(step < blocks_rotated, 1.0 / math.sqrt(HEAD_DIM), 1.0)
        cos, sin = cosine[...] * scale, sine[...] * scale
        for head in range(heads_block):
            low = head * HEAD_DIM
            t1, t2 = rows[low : low + half], rows[low + half : low + 2 * half]
            joined[low : low + half] = (t1 * cos - t2 * sin).astype(bf16)
            joined[low + half : low + 2 * half] = (t2 * cos + t1 * sin).astype(bf16)

    @pl.when(step >= 2 * blocks_rotated)
    def _():
        joined[...] = rows.astype(bf16)


def project_qkv(tokens, weight, cosine, sine):
    length, width = tokens.shape
    heads_block = 4
    block = heads_block * HEAD_DIM
    count = weight.shape[1] // block
    return pl.pallas_call(
        functools.partial(qkv_kernel, count // 3, heads_block),
        grid=(count,),
        in_specs=[
            whole(length, width),
            pl.BlockSpec((width, block), lambda i: (0, i)),
            whole(*cosine.shape),
            whole(*sine.shape),
        ],
        out_specs=pl.BlockSpec((block, length), lambda i: (i, 0)),
        out_shape=jax.ShapeDtypeStruct((weight.shape[1], length), bf16),
        compiler_params=params(),
        cost_estimate=cost(2 * length * width * weight.shape[1], 2 * weight.size * 3),
        name="qkv_rope",
    )(tokens, weight, cosine, sine)


def attend_head(queries, key_rows, value_rows, mixed, weights):
    length = queries.shape[1]
    chunk = min(512, length)

    def scores_of(low):
        return contract(key_rows[...], queries[:, pl.ds(low, chunk)], 0, 0)

    scores = scores_of(0)
    for low in range(0, length, chunk):
        span = pl.ds(low, chunk)
        following = scores_of(low + chunk) if low + chunk < length else None
        highest = jnp.max(scores, axis=0, keepdims=True)
        expanded = jnp.exp(scores - highest)
        totals = jnp.sum(expanded, axis=0, keepdims=True)
        soft = (expanded * (1.0 / totals)).astype(bf16)
        weights[0, :, span] = soft
        mixed[:, span] = contract(value_rows[...], soft, 1, 0).astype(bf16)
        scores = following


def attend_forward(joined):
    length = joined.shape[1]
    head_rows = lambda part: pl.BlockSpec(
        (HEAD_DIM, length), lambda h: (part * HEADS + h, 0)
    )
    return pl.pallas_call(
        attend_head,
        grid=(HEADS,),
        in_specs=[head_rows(0), head_rows(1), head_rows(2)],
        out_specs=[
            pl.BlockSpec((HEAD_DIM, length), lambda h: (h, 0)),
            pl.BlockSpec((1, length, length), lambda h: (h, 0, 0)),
        ],
        out_shape=[
            jax.ShapeDtypeStruct((HEADS * HEAD_DIM, length), bf16),
            jax.ShapeDtypeStruct((HEADS, length, length), bf16),
        ],
        compiler_params=params(),
        cost_estimate=cost(
            16 * HEADS * length * length * HEAD_DIM, 2 * HEADS * length * length, length * length * HEADS
        ),
        name="attend_forward",
    )(joined, joined, joined)


def attend_back_kernel(
    chunk,
    queries,
    key_rows,
    value_rows,
    mixed,
    grad_mixed,
    weights,
    cosine,
    sine,
    query_out,
    key_out,
    value_out,
):
    length = queries.shape[1]
    half = HEAD_DIM // 2
    grad = grad_mixed[...]
    centre = jnp.sum(grad.astype(f32) * mixed[...].astype(f32), axis=0, keepdims=True)
    query_grad = jnp.zeros((HEAD_DIM, length), f32)
    key_parts = []
    for low in range(0, length, chunk):
        span = pl.ds(low, chunk)
        soft = weights[0, span, :]
        weight_grad = contract(value_rows[:, span], grad, 0, 0)
        score_grad = (soft.astype(f32) * (weight_grad - centre)).astype(bf16)
        value_out[:, span] = contract(grad, soft, 1, 1).astype(bf16)
        key_parts.append(contract(queries[...], score_grad, 1, 1))
        query_grad += contract(key_rows[:, span], score_grad, 1, 0)
    key_grad = jnp.concatenate(key_parts, axis=1)
    cos, sin = cosine[...], sine[...]
    scale = 1.0 / math.sqrt(HEAD_DIM)
    for out, grad_rows, factor in ((query_out, query_grad, scale), (key_out, key_grad, 1.0)):
        d1, d2 = grad_rows[:half], grad_rows[half:]
        out[:half] = ((d1 * cos + d2 * sin) * factor).astype(bf16)
        out[half:] = ((d2 * cos - d1 * sin) * factor).astype(bf16)


def attend_backward(joined, mixed, grad_mixed, weights, cosine, sine):
    length = joined.shape[1]
    head_rows = lambda part: pl.BlockSpec(
        (HEAD_DIM, length), lambda h: (part * HEADS + h, 0)
    )
    rows = jax.ShapeDtypeStruct((HEADS * HEAD_DIM, length), bf16)
    return pl.pallas_call(
        functools.partial(attend_back_kernel, min(256, length)),
        grid=(HEADS,),
        in_specs=[
            head_rows(0),
            head_rows(1),
            head_rows(2),
            head_rows(0),
            head_rows(0),
            pl.BlockSpec((1, length, length), lambda h: (h, 0, 0)),
            whole(*cosine.shape),
            whole(*sine.shape),
        ],
        out_specs=[head_rows(0)] * 3,
        out_shape=[rows] * 3,
        compiler_params=params(),
        cost_estimate=cost(
            32 * HEADS * length * length * HEAD_DIM, 2 * HEADS * length * length
        ),
        name="attend_backward",
    )(joined, joined, joined, mixed, grad_mixed, weights, cosine, sine)


def norm_rows(values):
    centred = values - jnp.mean(values, axis=1, keepdims=True)
    inverse = lax.rsqrt(jnp.mean(centred * centred, axis=1, keepdims=True) + norm_eps)
    return centred * inverse, inverse


def norm_back(grad_rows, normed, inverse, gain_row):
    scaled = grad_rows * gain_row
    centred = (
        scaled
        - jnp.mean(scaled, axis=1, keepdims=True)
        - normed * jnp.mean(scaled * normed, axis=1, keepdims=True)
    )
    gain = jnp.sum(grad_rows * normed, axis=0, keepdims=True)
    bias = jnp.sum(grad_rows, axis=0, keepdims=True)
    return centred * inverse, gain, bias


def out_kernel(tokens, mixed, weight, norms, normed, inverse, hidden_low):
    sums = tokens[...].astype(f32) + contract(mixed[...], weight[...], 0, 0)
    rows, scale = norm_rows(sums)
    normed[...] = rows
    inverse[...] = scale
    hidden_low[...] = (rows * norms[0:1, :] + norms[1:2, :]).astype(bf16)


def project_out(tokens, mixed, weight, norms):
    length, width = tokens.shape
    block = min(256, length)
    return pl.pallas_call(
        out_kernel,
        grid=(length // block,),
        in_specs=[
            pl.BlockSpec((block, width), lambda i: (i, 0)),
            pl.BlockSpec((width, block), lambda i: (0, i)),
            whole(width, width),
            whole(*norms.shape),
        ],
        out_specs=[
            pl.BlockSpec((block, width), lambda i: (i, 0)),
            pl.BlockSpec((block, 1), lambda i: (i, 0)),
            pl.BlockSpec((block, width), lambda i: (i, 0)),
        ],
        out_shape=[
            jax.ShapeDtypeStruct((length, width), f32),
            jax.ShapeDtypeStruct((length, 1), f32),
            jax.ShapeDtypeStruct((length, width), bf16),
        ],
        compiler_params=params(),
        cost_estimate=cost(2 * length * width * width, 10 * length * width),
        name="out_norm",
    )(tokens, mixed, weight, norms)


def second_norm(rows_block, norms, cotangent, output, grad_second, grad_low, norm_grads, total):
    gain_sum = jnp.zeros((1, total.shape[1]), f32)
    bias_sum = jnp.zeros((1, total.shape[1]), f32)
    for low in range(0, total.shape[0], rows_block):
        span = pl.ds(low, rows_block)
        rows, inverse = norm_rows(total[span, :])
        output[span, :] = (rows * norms[2:3, :] + norms[3:4, :]).astype(bf16)
        back, gain, bias = norm_back(cotangent[span, :].astype(f32), rows, inverse, norms[2:3, :])
        grad_second[span, :] = back
        grad_low[span, :] = back.astype(bf16)
        gain_sum += gain
        bias_sum += bias
    norm_grads[0:1, :] = gain_sum
    norm_grads[1:2, :] = bias_sum


def first_norm_back(
    rows_block, normed, inverse, norms, total, grad_first, first_low, norm_grads
):
    gain_sum = jnp.zeros((1, total.shape[1]), f32)
    bias_sum = jnp.zeros((1, total.shape[1]), f32)
    for low in range(0, total.shape[0], rows_block):
        span = pl.ds(low, rows_block)
        back, gain, bias = norm_back(
            total[span, :], normed[span, :], inverse[span, :], norms[0:1, :]
        )
        grad_first[span, :] = back
        first_low[span, :] = back.astype(bf16)
        gain_sum += gain
        bias_sum += bias
    norm_grads[0:1, :] = gain_sum
    norm_grads[1:2, :] = bias_sum


def forward_kernel(
    rows_block,
    hidden_low,
    gate_weight,
    up_weight,
    down_weight,
    normed_one,
    norms,
    cotangent,
    gate,
    up,
    output,
    grad_second,
    grad_low,
    norm_grads,
    total,
):
    step = pl.program_id(0)
    length = hidden_low.shape[0]
    for low in range(0, length, rows_block):
        span = pl.ds(low, rows_block)
        gate_part = contract(hidden_low[span, :], gate_weight[...], 1, 0)
        up_part = contract(hidden_low[span, :], up_weight[...], 1, 0)
        gate[span, :] = gate_part
        up[span, :] = up_part
        inner = (gate_part * jax.nn.sigmoid(gate_part) * up_part).astype(bf16)
        part = contract(inner, down_weight[...], 1, 0)

        @pl.when(step == 0)
        def _():
            total[span, :] = part

        @pl.when(step > 0)
        def _():
            total[span, :] += part

    @pl.when(step == pl.num_programs(0) - 1)
    def _():
        total[...] += normed_one[...] * norms[0:1, :] + norms[1:2, :]
        second_norm(rows_block, norms, cotangent, output, grad_second, grad_low, norm_grads, total)


def feed_forward(hidden_low, gate_up, down, normed_one, norms, cotangent):
    length, width = hidden_low.shape
    inner = down.shape[0]
    block = min(512, inner)
    count = inner // block
    return pl.pallas_call(
        functools.partial(forward_kernel, min(256, length)),
        grid=(count,),
        in_specs=[
            whole(length, width),
            pl.BlockSpec((width, block), lambda j: (0, j)),
            pl.BlockSpec((width, block), lambda j: (0, count + j)),
            pl.BlockSpec((block, width), lambda j: (j, 0)),
            whole(length, width),
            whole(*norms.shape),
            whole(length, width),
        ],
        out_specs=[
            pl.BlockSpec((length, block), lambda j: (0, j)),
            pl.BlockSpec((length, block), lambda j: (0, j)),
            whole(length, width),
            whole(length, width),
            whole(length, width),
            whole(2, width),
        ],
        out_shape=[
            jax.ShapeDtypeStruct((length, inner), f32),
            jax.ShapeDtypeStruct((length, inner), f32),
            jax.ShapeDtypeStruct((length, width), bf16),
            jax.ShapeDtypeStruct((length, width), f32),
            jax.ShapeDtypeStruct((length, width), bf16),
            jax.ShapeDtypeStruct((2, width), f32),
        ],
        scratch_shapes=[pltpu.VMEM((length, width), f32)],
        compiler_params=params(),
        cost_estimate=cost(6 * length * width * inner, 8 * length * inner),
        name="feed_forward",
    )(hidden_low, gate_up, gate_up, down, normed_one, norms, cotangent)


def backward_kernel(
    rows_block,
    grad_low,
    hidden_low,
    gate,
    up,
    gate_weight,
    up_weight,
    down_weight,
    before,
    normed,
    inverse,
    norms,
    gate_out,
    up_out,
    down_out,
    grad_first,
    first_low,
    norm_grads,
    total,
    inner,
    gate_back,
    up_back,
):
    step = pl.program_id(0)
    length = hidden_low.shape[0]

    @pl.when(step == 0)
    def _():
        total[...] = before[...]

    for low in range(0, length, rows_block):
        span = pl.ds(low, rows_block)
        inner_grad = contract(grad_low[span, :], down_weight[...], 1, 1)
        gate_part, up_part = gate[span, :], up[span, :]
        sigmoid = jax.nn.sigmoid(gate_part)
        swished = gate_part * sigmoid
        inner[span, :] = (swished * up_part).astype(bf16)
        gate_grad = inner_grad * up_part * sigmoid * (1.0 + gate_part * (1.0 - sigmoid))
        gate_low, up_low = gate_grad.astype(bf16), (inner_grad * swished).astype(bf16)
        gate_back[span, :] = gate_low
        up_back[span, :] = up_low
        total[span, :] += contract(gate_low, gate_weight[...], 1, 1) + contract(
            up_low, up_weight[...], 1, 1
        )
    down_out[...] = contract(inner[...], grad_low[...], 0, 0).astype(bf16)
    gate_out[...] = contract(hidden_low[...], gate_back[...], 0, 0).astype(bf16)
    up_out[...] = contract(hidden_low[...], up_back[...], 0, 0).astype(bf16)

    @pl.when(step == pl.num_programs(0) - 1)
    def _():
        first_norm_back(rows_block, normed, inverse, norms, total, grad_first, first_low, norm_grads)


def feed_backward(
    grad_low, hidden_low, gate, up, gate_up, down, before, normed, inverse, norms
):
    length, width = hidden_low.shape
    inner = down.shape[0]
    block = min(256, inner)
    count = inner // block
    in_cols = lambda shift: pl.BlockSpec((width, block), lambda j: (0, shift + j))
    wide = pl.BlockSpec((length, block), lambda j: (0, j))
    narrow = pl.BlockSpec((block, width), lambda j: (j, 0))
    full = whole(length, width)
    return pl.pallas_call(
        functools.partial(backward_kernel, min(256, length)),
        grid=(count,),
        in_specs=[
            full,
            full,
            wide,
            wide,
            in_cols(0),
            in_cols(count),
            narrow,
            full,
            full,
            whole(length, 1),
            whole(*norms.shape),
        ],
        out_specs=[in_cols(0), in_cols(0), narrow, full, full, whole(2, width)],
        out_shape=[
            jax.ShapeDtypeStruct((width, inner), bf16),
            jax.ShapeDtypeStruct((width, inner), bf16),
            jax.ShapeDtypeStruct((inner, width), bf16),
            jax.ShapeDtypeStruct((length, width), f32),
            jax.ShapeDtypeStruct((length, width), bf16),
            jax.ShapeDtypeStruct((2, width), f32),
        ],
        scratch_shapes=[pltpu.VMEM((length, width), f32)] + [pltpu.VMEM((length, block), bf16)] * 3,
        compiler_params=params(),
        cost_estimate=cost(12 * length * width * inner, 8 * length * inner),
        name="feed_backward",
    )(grad_low, hidden_low, gate, up, gate_up, gate_up, down, before, normed, inverse, norms)


def paired_forward_kernel(
    rows_block,
    hidden_low,
    gate_0,
    gate_1,
    up_0,
    up_1,
    down_0,
    down_1,
    normed_one,
    norms,
    cotangent,
    gate,
    up,
    output,
    grad_second,
    grad_low,
    norm_grads,
    total,
):
    step = pl.program_id(0)
    length = hidden_low.shape[0]
    run = gate.shape[2] // 2
    gate_weight = jnp.concatenate([gate_0[...], gate_1[...]], axis=1)
    up_weight = jnp.concatenate([up_0[...], up_1[...]], axis=1)
    down_weight = jnp.concatenate([down_0[...], down_1[...]], axis=0)

    def keep(target, span, part):
        for i in range(2):
            target[i, span, :run] = part[:, i * run : (i + 1) * run]
            target[i, span, run:] = part[:, (2 + i) * run : (3 + i) * run]

    @pl.when(step == 0)
    def _():
        total[...] = normed_one[...] * norms[0:1, :] + norms[1:2, :]

    def products(low):
        rows = hidden_low[pl.ds(low, rows_block), :]
        return contract(rows, gate_weight, 1, 0), contract(rows, up_weight, 1, 0)

    following = products(0)
    for low in range(0, length, rows_block):
        span = pl.ds(low, rows_block)
        gate_part, up_part = following
        if low + rows_block < length:
            following = products(low + rows_block)
        keep(gate, span, gate_part)
        keep(up, span, up_part)
        inner = (gate_part * jax.nn.sigmoid(gate_part) * up_part).astype(bf16)
        total[span, :] += contract(inner, down_weight, 1, 0)

    @pl.when(step == pl.num_programs(0) - 1)
    def _():
        second_norm(min(256, length), norms, cotangent, output, grad_second, grad_low, norm_grads, total)


def paired_forward(hidden_low, gate_up, down, normed_one, norms, cotangent):
    length, width = hidden_low.shape
    inner = down.shape[0]
    run = 256
    count = inner // (2 * run)
    cols = lambda shift: pl.BlockSpec((width, run), lambda j: (0, shift * count + j))
    kept = pl.BlockSpec((2, length, run), lambda j: (j, 0, 0))
    kept_shape = jax.ShapeDtypeStruct((2 * count, length, run), f32)
    return pl.pallas_call(
        functools.partial(paired_forward_kernel, min(256, length)),
        grid=(count,),
        in_specs=[
            whole(length, width),
            cols(0),
            cols(1),
            cols(2),
            cols(3),
            pl.BlockSpec((run, width), lambda j: (j, 0)),
            pl.BlockSpec((run, width), lambda j: (count + j, 0)),
            whole(length, width),
            whole(*norms.shape),
            whole(length, width),
        ],
        out_specs=[
            kept,
            kept,
            whole(length, width),
            whole(length, width),
            whole(length, width),
            whole(2, width),
        ],
        out_shape=[
            kept_shape,
            kept_shape,
            jax.ShapeDtypeStruct((length, width), bf16),
            jax.ShapeDtypeStruct((length, width), f32),
            jax.ShapeDtypeStruct((length, width), bf16),
            jax.ShapeDtypeStruct((2, width), f32),
        ],
        scratch_shapes=[pltpu.VMEM((length, width), f32)],
        compiler_params=params(),
        cost_estimate=cost(6 * length * width * inner, 8 * length * inner),
        name="feed_forward",
    )(hidden_low, *[gate_up] * 4, down, down, normed_one, norms, cotangent)


EARLY_STEPS = (4, 5, 7, 8, 10, 11, 12)


def paired_backward_kernel(
    rows_block,
    grad_low,
    hidden_low,
    gate,
    up,
    gate_0,
    gate_1,
    up_0,
    up_1,
    down_0,
    down_1,
    before,
    normed,
    inverse,
    norms,
    wide_out,
    down_out,
    wide_shard_out,
    down_shard_out,
    grad_first,
    first_low,
    norm_grads,
    total,
    inner,
    gate_back,
    up_back,
    wide_part,
    down_part,
    wide_sum,
    down_sum,
    wide_shard,
    down_shard,
    before_sem,
    core_sem,
    out_sem,
    shard_sem,
):
    step, last = pl.program_id(0), pl.num_programs(0) - 1
    early = wide_shard.shape[0]
    length, width = hidden_low.shape
    run = gate.shape[2] // 2
    dp, shard = lax.axis_index("dp"), lax.axis_index("shard")
    core = dp % 2
    peer = (dp + 1 - 2 * core, shard)
    start_total = pltpu.make_async_copy(before, total, before_sem)

    def sends(j):
        for i, (part, whole_sum) in enumerate(((wide_part, wide_sum), (down_part, down_sum))):
            yield pltpu.make_async_remote_copy(
                src_ref=part.at[j % 2, 1 - core],
                dst_ref=whole_sum.at[j],
                send_sem=core_sem.at[i, j, 0],
                recv_sem=core_sem.at[i, j, 1],
                device_id=peer,
                device_id_type=pl.DeviceIdType.MESH,
            )

    def keeps(j):
        yield pltpu.make_async_copy(wide_sum.at[j], wide_out.at[j], out_sem.at[0, j])
        yield pltpu.make_async_copy(down_sum.at[j], down_out.at[j], out_sem.at[1, j])

    def shard_keeps(j):
        yield pltpu.make_async_copy(wide_shard.at[j], wide_shard_out.at[j], out_sem.at[0, j])
        yield pltpu.make_async_copy(down_shard.at[j], down_shard_out.at[j], out_sem.at[1, j])

    shard_parts = ((wide_sum, wide_shard), (down_sum, down_shard))

    def shard_sends(j):
        for i, (whole_sum, target) in enumerate(shard_parts):
            height = target.shape[2]
            low = pl.multiple_of((1 - shard) * height, 16)
            yield pltpu.make_async_remote_copy(
                src_ref=whole_sum.at[j, :, pl.ds(low, height)],
                dst_ref=target.at[j],
                send_sem=shard_sem.at[i, j, 0],
                recv_sem=shard_sem.at[i, j, 1],
                device_id=(dp, 1 - shard),
                device_id_type=pl.DeviceIdType.MESH,
            )

    def add_shards(j):
        for copy in shard_sends(j):
            copy.wait_recv()
        for whole_sum, target in shard_parts:
            _, lead, height, _ = target.shape

            @pl.loop(0, height // 64)
            def _(i):
                span = pl.ds(pl.multiple_of(i * 64, 64), 64)
                own = pl.ds(pl.multiple_of(shard * height + i * 64, 64), 64)
                for k in range(lead):
                    value = target[j, k, span, :].astype(f32) + whole_sum[j, k, own, :].astype(f32)
                    target[j, k, span, :] = value.astype(bf16)

        for copy in shard_keeps(j):
            copy.start()

    def add_cores(j):
        for copy in sends(j):
            copy.wait_recv()

        @pl.loop(0, width // 64)
        def _(i):
            span = pl.ds(pl.multiple_of(i * 64, 64), 64)
            for k in range(2):
                value = wide_sum[j, k, span, :].astype(f32) + wide_part[j % 2, core, k, span, :].astype(f32)
                wide_sum[j, k, span, :] = value.astype(bf16)

        @pl.loop(0, 2 * run // 32)
        def _(i):
            span = pl.ds(pl.multiple_of(i * 32, 32), 32)
            value = down_sum[j, 0, span, :].astype(f32) + down_part[j % 2, core, 0, span, :].astype(f32)
            down_sum[j, 0, span, :] = value.astype(bf16)

    @pl.when(step == 0)
    def _():
        start_total.start()
        barrier = pltpu.get_barrier_semaphore()
        for other in (peer, (dp, 1 - shard)):
            pl.semaphore_signal(barrier, inc=1, device_id=other, device_id_type=pl.DeviceIdType.MESH)
        pl.semaphore_wait(barrier, 2)
        start_total.wait()

    gate_weight = jnp.concatenate([gate_0[...], gate_1[...]], axis=1)
    up_weight = jnp.concatenate([up_0[...], up_1[...]], axis=1)
    down_weight = jnp.concatenate([down_0[...], down_1[...]], axis=0)
    def inner_grads(low):
        return contract(grad_low[pl.ds(low, rows_block), :], down_weight, 1, 1)

    following = inner_grads(0)
    for low in range(0, length, rows_block):
        span = pl.ds(low, rows_block)
        inner_grad = following
        if low + rows_block < length:
            following = inner_grads(low + rows_block)
        gate_part, up_part = gate[0, span, :], up[0, span, :]
        sigmoid = jax.nn.sigmoid(gate_part)
        swished = gate_part * sigmoid
        inner[span, :] = (swished * up_part).astype(bf16)
        gate_grad = inner_grad * up_part * sigmoid * (1.0 + gate_part * (1.0 - sigmoid))
        gate_low, up_low = gate_grad.astype(bf16), (inner_grad * swished).astype(bf16)
        gate_back[span, :] = gate_low
        up_back[span, :] = up_low
        total[span, :] += contract(gate_low, gate_weight, 1, 1) + contract(up_low, up_weight, 1, 1)

    @pl.when(step >= 2)
    def _():
        for copy in sends(step - 2):
            copy.wait_send()

    slot, half = step % 2, width // 2
    rows = contract(inner[...], grad_low[...], 0, 0).astype(bf16)
    down_part[slot, 0, 0] = rows[:, :half]
    down_part[slot, 1, 0] = rows[:, half:]
    for i, back in enumerate((gate_back, up_back)):
        columns = contract(hidden_low[...], back[...], 0, 0).astype(bf16)
        wide_part[slot, 0, i] = columns[:, :run]
        wide_part[slot, 1, i] = columns[:, run:]
    for copy in sends(step):
        copy.start()

    @pl.when(step >= 1)
    def _():
        add_cores(step - 1)

    @pl.when((step >= 1) & (step <= early))
    def _():
        for copy in shard_sends(step - 1):
            copy.start()

    @pl.when(step > early)
    def _():
        for copy in keeps(step - 1):
            copy.start()

    for j, at in enumerate(EARLY_STEPS[:-1]):

        @pl.when(step == at)
        def _(j=j):
            add_shards(j)

    @pl.when(step == last)
    def _():
        first_norm_back(min(256, length), normed, inverse, norms, total, grad_first, first_low, norm_grads)
        add_cores(step)
        for copy in keeps(step):
            copy.start()
        add_shards(early - 1)
        for copy in [*sends(step - 1), *sends(step)]:
            copy.wait_send()

        @pl.loop(0, early)
        def _(j):
            for copy in shard_sends(j):
                copy.wait_send()
            for copy in shard_keeps(j):
                copy.wait()

        @pl.loop(early, last + 1)
        def _(j):
            for copy in keeps(j):
                copy.wait()


def paired_backward(
    grad_low, hidden_low, gate, up, gate_up, down, before, normed, inverse, norms
):
    early, rows = len(EARLY_STEPS), hidden_low.shape[1] // 2
    length, width = hidden_low.shape
    count, _, block = gate.shape
    run = block // 2
    cols = lambda shift: pl.BlockSpec((width, run), lambda j: (0, shift * count + j))
    kept = pl.BlockSpec((1, length, block), lambda j: (j, 0, 0))
    anywhere = pl.BlockSpec(memory_space=pl.ANY)
    full = whole(length, width)
    dma = pltpu.SemaphoreType.DMA
    wide, narrow = (2, width, run), (1, block, width // 2)
    return pl.pallas_call(
        functools.partial(paired_backward_kernel, min(256, length)),
        grid=(count,),
        in_specs=[
            full,
            full,
            kept,
            kept,
            cols(0),
            cols(1),
            cols(2),
            cols(3),
            pl.BlockSpec((run, width), lambda j: (j, 0)),
            pl.BlockSpec((run, width), lambda j: (count + j, 0)),
            anywhere,
            full,
            whole(length, 1),
            whole(*norms.shape),
        ],
        out_specs=[anywhere] * 4 + [full, full, whole(2, width)],
        out_shape=[
            jax.ShapeDtypeStruct((count,) + wide, bf16),
            jax.ShapeDtypeStruct((count,) + narrow, bf16),
            jax.ShapeDtypeStruct((early, 2, rows, run), bf16),
            jax.ShapeDtypeStruct((early, 1, run, width // 2), bf16),
            jax.ShapeDtypeStruct((length, width), f32),
            jax.ShapeDtypeStruct((length, width), bf16),
            jax.ShapeDtypeStruct((2, width), f32),
        ],
        scratch_shapes=[pltpu.VMEM((length, width), f32)]
        + [pltpu.VMEM((length, block), bf16)] * 3
        + [
            pltpu.VMEM((2, 2) + wide, bf16),
            pltpu.VMEM((2, 2) + narrow, bf16),
            pltpu.VMEM((count,) + wide, bf16),
            pltpu.VMEM((count,) + narrow, bf16),
            pltpu.VMEM((early, 2, rows, run), bf16),
            pltpu.VMEM((early, 1, run, width // 2), bf16),
            dma,
            dma((2, count, 2)),
            dma((2, count)),
            dma((2, early, 2)),
        ],
        compiler_params=params(collective_id=3, has_side_effects=True),
        cost_estimate=cost(12 * length * width * down.shape[0], 8 * length * down.shape[0]),
        name="feed_backward",
    )(grad_low, hidden_low, gate, up, *[gate_up] * 4, down, down, before, normed, inverse, norms)


class Links:
    def __init__(self, mesh):
        self.sizes = {"dp": mesh.shape["dp"], "shard": mesh.shape["shard"]}
        chips = self.sizes["dp"] // 2
        near = 2 if chips % 2 == 0 else 1
        self.core = ("dp", 1, 2)
        self.near = ("dp", 2, near)
        self.far = ("dp", 2 * near, chips // near)
        self.shard = ("shard", 1, self.sizes["shard"])

    def place(self, digit):
        axis, stride, size = digit
        return (lax.axis_index(axis) // stride) % size

    def shift(self, value, digit, step):
        axis, stride, size = digit
        pairs = []
        for i in range(self.sizes[axis]):
            own = (i // stride) % size
            pairs.append((i, i + ((own + step) % size - own) * stride))
        return lax.ppermute(value, axis, pairs)

    def scatter_sum(self, value, digit, dim):
        size = digit[2]
        if size == 1:
            return value
        own = self.place(digit)
        width = value.shape[dim] // size

        def piece(index):
            return lax.dynamic_slice_in_dim(value, index * width, width, dim)

        total = piece(own).astype(f32)
        for step in range(1, size):
            total += self.shift(piece((own + step) % size), digit, step).astype(f32)
        return total.astype(bf16)

    def gather(self, value, digit, dim):
        size = digit[2]
        if size == 1:
            return value
        own = self.place(digit)
        width = value.shape[dim]
        if size == 2:
            other = self.shift(value, digit, 1)
            first = jnp.where(own == 0, value, other)
            second = jnp.where(own == 0, other, value)
            return jnp.concatenate([first, second], axis=dim)
        shape = list(value.shape)
        shape[dim] *= size
        full = lax.dynamic_update_slice_in_dim(
            jnp.zeros(shape, value.dtype), value, own * width, dim
        )
        for step in range(1, size):
            came = self.shift(value, digit, step)
            full = lax.dynamic_update_slice_in_dim(
                full, came, ((own - step) % size) * width, dim
            )
        return full

    def gather_rows(self, value, spread):
        parts = [self.core, self.near] if spread else [self.core]
        piece = value
        for digit in parts:
            width = piece.shape[0] // digit[2]
            piece = lax.dynamic_slice_in_dim(piece, self.place(digit) * width, width, 0)
        size = self.shard[2]
        rows = value.shape[0]
        own = self.place(self.shard)
        full = lax.dynamic_update_slice_in_dim(
            jnp.zeros((size * rows, value.shape[1]), value.dtype), value, own * rows, 0
        )
        for step in range(1, size):
            came = self.shift(piece, self.shard, step)
            for digit in reversed(parts):
                came = self.gather(came, digit, 0)
            full = lax.dynamic_update_slice_in_dim(full, came, ((own - step) % size) * rows, 0)
        return full

    def total(self, grads):
        grads = self.scatter_sum(grads, self.core, 1)
        grads = self.scatter_sum(grads, self.shard, 0)
        grads = self.scatter_sum(grads, self.near, 0)
        grads = self.scatter_sum(grads, self.far, 0)
        grads = self.gather(grads, self.far, 0)
        grads = self.gather(grads, self.near, 0)
        return self.gather(grads, self.core, 1)


def adam_update(weight, first_moment, second_moment, gradient, rate, decay_on):
    first_new = beta_first * first_moment + (1.0 - beta_first) * gradient
    second_new = beta_second * second_moment + (1.0 - beta_second) * gradient * gradient
    fix_first = 1.0 - beta_first**STEP
    fix_second = 1.0 - beta_second**STEP
    direction = first_new / fix_first / (jnp.sqrt(second_new / fix_second) + adam_eps)
    return (weight - rate * (direction + decay_on * weight), first_new, second_new)


def fits(mesh, length, rows, long_rows):
    far = mesh.shape["dp"] // 4
    return (
        mesh.shape["shard"] == 2
        and mesh.shape["dp"] == 16
        and length % 512 == 0
        and rows % (32 * far) == 0
        and long_rows % (4 * Back.update_cols) == 0
        and long_rows % (128 * HEADS) == 0
        and 128 % (32 * far) == 0
    )


class Front:
    def __init__(self, mesh, length, width, rows, matrices):
        self.length, self.width, self.rows = length, width, rows
        self.matrices = matrices
        self.units = []
        for i, shape in enumerate(matrices):
            for low in range(0, shape[0], rows):
                for left in range(0, shape[1], width):
                    self.units.append((i, low, left))

    def __call__(self, tokens, masters, cosine, sine):
        length, width, rows = self.length, self.width, self.rows
        dma = pltpu.SemaphoreType.DMA
        anywhere = pl.BlockSpec(memory_space=pl.ANY)
        fulls = [jax.ShapeDtypeStruct((2 * shape[0], shape[1]), bf16) for shape in self.matrices]
        count = 3 + len(self.units)
        return pl.pallas_call(
            self.kernel,
            grid=(HEADS,),
            in_specs=[whole(length, width), whole(*cosine.shape), whole(*sine.shape)] + [anywhere] * 4,
            out_specs=[
                pl.BlockSpec((HEAD_DIM, length), lambda h: (h, 0)),
                pl.BlockSpec((1, length, length), lambda h: (h, 0, 0)),
            ]
            + [anywhere] * 5,
            out_shape=[
                jax.ShapeDtypeStruct((width, length), bf16),
                jax.ShapeDtypeStruct((HEADS, length, length), bf16),
                jax.ShapeDtypeStruct((3 * width, length), bf16),
                jax.ShapeDtypeStruct((width, 3 * width), bf16),
                *fulls,
            ],
            scratch_shapes=[
                pltpu.VMEM((3 * width, length), bf16),
                pltpu.VMEM((3, width, width), bf16),
                pltpu.VMEM((len(self.units), rows, width), bf16),
                pltpu.VMEM((3, rows, width), f32),
                dma((4, count, 2)),
                dma((3,)),
                dma((len(self.units),)),
                dma((4,)),
            ],
            compiler_params=params(collective_id=2, has_side_effects=True),
            name="front",
        )(tokens, cosine, sine, *masters)

    def kernel(
        self,
        tokens,
        cosine,
        sine,
        master_qkv,
        master_out,
        master_gate_up,
        master_down,
        mixed,
        weights,
        joined_out,
        qkv_out,
        full_out,
        full_gate_up,
        full_down,
        joined,
        qkv,
        own_low,
        wide,
        pair_sem,
        load_sem,
        own_sem,
        out_sem,
    ):
        width, rows = self.width, self.rows
        step = pl.program_id(0)
        dp, shard = lax.axis_index("dp"), lax.axis_index("shard")
        core, near, low_bit = dp % 2, dp // 2 % 2, dp // 4 % 2
        near_peer, low_peer = (dp + 2 - 4 * near, shard), (dp + 4 - 8 * low_bit, shard)
        shard_peer, core_peer = (dp, 1 - shard), (dp + 1 - 2 * core, shard)
        masters, fulls = [master_out, master_gate_up, master_down], [full_out, full_gate_up, full_down]
        count = len(self.units)

        def region(u, stage):
            first, second = (near, low_bit) if u % 2 == 0 else (low_bit, near)
            side = shard if stage == 0 else 1 - shard
            height = (rows // 8, rows // 8, rows // 4, rows // 2)[stage]
            low = core * (rows // 2)
            if stage < 3:
                low += second * (rows // 4)
            if stage < 2:
                low += first * (rows // 8)
            if u < 3:
                place = pl.ds(pl.multiple_of(side * rows + low, 16), height)
                return qkv.at[u, place], qkv.at[u, place]
            matrix, first, left = self.units[u - 3]
            place = pl.ds(pl.multiple_of(side * self.matrices[matrix][0] + first + low, 16), height)
            full = fulls[matrix].at[place, pl.ds(left, width)]
            if stage == 0:
                return own_low.at[u - 3, pl.ds(pl.multiple_of(low, 16), height)], full
            return full, full

        def copy(u, stage):
            source, target = region(u, stage)
            return pltpu.make_async_remote_copy(
                src_ref=source,
                dst_ref=target,
                send_sem=pair_sem.at[stage, u, 0],
                recv_sem=pair_sem.at[stage, u, 1],
                device_id=peers_of(u)[stage],
                device_id_type=pl.DeviceIdType.MESH,
            )

        def peers_of(u):
            between = [near_peer, low_peer] if u % 2 == 0 else [low_peer, near_peer]
            return [shard_peer, *between, core_peer]

        def pass_on(u, stage):
            copy(u, stage - 1).wait_recv()
            copy(u, stage).start()

        def load(u):
            if u < 3:
                source = master_qkv.at[:, pl.ds(u * width, width)]
            else:
                matrix, first, left = self.units[u - 3]
                source = masters[matrix].at[pl.ds(first, rows), pl.ds(left, width)]
            return pltpu.make_async_copy(source, wide.at[u % 3], load_sem.at[u % 3])

        def own_rows(u):
            matrix, first, left = self.units[u - 3]
            place = pl.ds(pl.multiple_of(shard * self.matrices[matrix][0] + first, 16), rows)
            return pltpu.make_async_copy(
                own_low.at[u - 3], fulls[matrix].at[place, pl.ds(left, width)], own_sem.at[u - 3]
            )

        def round_unit(u):
            load(u).wait()
            target = qkv.at[u, pl.ds(pl.multiple_of(shard * rows, 16), rows)] if u < 3 else own_low.at[u - 3]

            @pl.loop(0, rows // 16)
            def _(i):
                span = pl.ds(pl.multiple_of(i * 16, 16), 16)
                target[span, :] = wide[u % 3, span, :].astype(bf16)

            if u + 3 < 3 + count:
                load(u + 3).start()
            if u >= 3:
                own_rows(u).start()

        def project(u):
            block = 4 * HEAD_DIM
            half = HEAD_DIM // 2
            for left in range(0, width, block):
                part = contract(qkv[u, :, left : left + block], tokens[...], 0, 1)
                if u == 2:
                    joined[u * width + left : u * width + left + block] = part.astype(bf16)
                    continue
                scale = 1.0 / math.sqrt(HEAD_DIM) if u == 0 else 1.0
                for low in range(0, block, HEAD_DIM):
                    t1, t2 = part[low : low + half], part[low + half : low + 2 * half]
                    cos, sin = cosine[...] * scale, sine[...] * scale
                    to = u * width + left + low
                    joined[to : to + half] = (t1 * cos - t2 * sin).astype(bf16)
                    joined[to + half : to + 2 * half] = (t2 * cos + t1 * sin).astype(bf16)

        def keep(i):
            if i == 3:
                return pltpu.make_async_copy(joined, joined_out, out_sem.at[3])
            return pltpu.make_async_copy(qkv.at[i], qkv_out.at[:, pl.ds(i * width, width)], out_sem.at[i])

        first_at = (6, 4, 2, -1)

        @pl.when(step == 0)
        def _():
            for u in range(3):
                load(u).start()
            barrier = pltpu.get_barrier_semaphore()
            for peer in peers_of(0):
                pl.semaphore_signal(barrier, inc=1, device_id=peer, device_id_type=pl.DeviceIdType.MESH)
            pl.semaphore_wait(barrier, len(peers_of(0)))
            for u in range(3):
                round_unit(u)
                copy(u, 0).start()
            for u in range(3, 7):
                round_unit(u)
            for stage in (1, 2):
                for u in range(3):
                    pass_on(u, stage)
                    if u < 2:
                        copy(3 + 2 * (stage - 1) + u, 0).start()
            for u in range(3):
                pass_on(u, 3)
            for u in range(3):
                copy(u, 3).wait_recv()
                project(u)
            for u in range(3, 1 + first_at[1]):
                pass_on(u, 1)
            for i in range(4):
                keep(i).start()

        for s in range(1, HEADS):

            @pl.when(step == s)
            def _(s=s):
                for stage in (3, 2, 1):
                    u = s + first_at[stage]
                    if 3 <= u < 3 + count:
                        pass_on(u, stage)
                if s + first_at[0] < 3 + count:
                    round_unit(s + first_at[0])
                    copy(s + first_at[0], 0).start()

        head = lambda part: joined.at[
            pl.ds(pl.multiple_of(part * width + step * HEAD_DIM, HEAD_DIM), HEAD_DIM)
        ]
        attend_head(head(0), head(1), head(2), mixed, weights)

        @pl.when(step == HEADS - 1)
        def _():
            for u in range(HEADS + first_at[0], 3 + count):
                round_unit(u)
                copy(u, 0).start()
            for stage in (1, 2, 3):
                for u in range(max(3, HEADS + first_at[stage]), 3 + count):
                    pass_on(u, stage)
            for u in range(3, 3 + count):
                copy(u, 3).wait_recv()
                own_rows(u).wait()
            for u in range(3 + count):
                for stage in range(4):
                    copy(u, stage).wait_send()
            for i in range(4):
                keep(i).wait()


def hand_out_kernel(*refs):
    count = len(refs) // 2
    for source, target in zip(refs[:count], refs[count:], strict=True):
        target[...] = source[...]


def hand_out(arrays):
    count = 16
    blocks = [pl.BlockSpec((array.shape[0] // count, array.shape[1]), lambda i: (i, 0)) for array in arrays]
    return pl.pallas_call(
        hand_out_kernel,
        grid=(count,),
        in_specs=blocks,
        out_specs=blocks,
        out_shape=[jax.ShapeDtypeStruct(array.shape, array.dtype) for array in arrays],
        compiler_params=params(),
        name="hand_out",
    )(*arrays)


class Back:
    ahead = 3
    steps = ("core", "shard", "near", "low", "high", "high total", "low total", "near total", "core total")
    update_cols = 384

    def __init__(self, mesh, length, width, inner, rows, long_rows, runs):
        self.far_size = mesh.shape["dp"] // 4
        self.length, self.width, self.inner = length, width, inner
        self.rows, self.long_rows, self.runs = rows, long_rows, runs
        self.scale = 1.0 / math.sqrt(length * mesh.shape["dp"] * mesh.shape["shard"])
        self.run = inner // (2 * runs)
        self.units = [[("wide", j), ("down", j)] for j in range(runs)] + [[("square", u)] for u in range(4)]
        self.groups = {
            "wide": (runs, 2, rows, self.run),
            "down": (runs, 1, self.run, width // 2),
            "square": (4, 1, rows, width // 2),
        }
        self.early = len(EARLY_STEPS)
        self.entry = [0, 0, 1, 2, 2, 3, 4, 2, 3, 5, 6, 7, 8, 9, 10, 11]
        blocks, side = [], self.update_cols
        for part in range(2):
            for left in range(0, inner, side):
                first, last = (at * 2 * runs // inner for at in (left % (inner // 2), left % (inner // 2) + side))
                blocks.append((max(self.entry[first:last]), 0, 0, part * inner + left, side, (part, left)))
        for low in range(0, long_rows, rows):
            first, last = (at * runs // long_rows for at in (low, low + rows))
            blocks.append((max(self.entry[first:last]), 1, low, 0, width, (0, 0)))
        for u in range(3):
            blocks.append((self.entry[runs + u], 3, 0, u * width, width, (0, u * width)))
        blocks.append((self.entry[runs + 3], 2, 0, 0, width, (0, 0)))
        self.blocks = sorted(blocks, key=lambda block: block[0])

    def __call__(
        self,
        joined,
        weights,
        mixed,
        first_low,
        weight_out,
        cosine,
        sine,
        feed_sums,
        tokens,
        weight_qkv,
        grad_first,
        masters,
        norm_grads,
        norm_state,
    ):
        length, width, rows = self.length, self.width, self.rows
        anywhere = pl.BlockSpec(memory_space=pl.ANY)
        once = lambda array: pl.BlockSpec(
            array.shape, lambda h: (0,) * array.ndim, pipeline_mode=pl.Buffered(1)
        )
        head_rows = lambda part: pl.BlockSpec((HEAD_DIM, length), lambda h: (part * HEADS + h, 0))
        state = [part for master in masters for part in master]
        outs = []
        for master, _, _ in masters:
            full = (2 * master.shape[0], master.shape[1])
            outs += [
                jax.ShapeDtypeStruct(full, bf16),
                jax.ShapeDtypeStruct(master.shape, f32),
                jax.ShapeDtypeStruct(master.shape, f32),
            ]
        totals = [
            jax.ShapeDtypeStruct((2, rows, self.inner), bf16),
            jax.ShapeDtypeStruct((1, self.long_rows, width), bf16),
            jax.ShapeDtypeStruct((1, rows, width), bf16),
            jax.ShapeDtypeStruct((1, rows, 3 * width), bf16),
        ]
        norm_outs = [jax.ShapeDtypeStruct(norm_grads.shape, f32)] * 3
        dma = pltpu.SemaphoreType.DMA
        far = max(self.far_size - 1, 1)
        scratch = [
            pltpu.VMEM((width, length), bf16),
            pltpu.VMEM((3 * width, length), bf16),
            pltpu.VMEM((length, width), bf16),
            pltpu.VMEM((width, 3 * width), bf16),
            pltpu.VMEM((length, width), f32),
            pltpu.VMEM((4, 2, width, width // 2), bf16),
            pltpu.VMEM((4, 1, width, width // 2), bf16),
        ]
        for name, (count, lead, height, columns) in self.groups.items():
            slots = 1 if name == "square" else self.ahead + 1
            heights = [height // 2**i for i in range(4)]
            scratch += [pltpu.VMEM((count, lead, rows_left, columns), bf16) for rows_left in heights]
            scratch += [
                pltpu.VMEM((slots, lead, height if slots > 1 else 16, columns), bf16),
                dma((len(self.steps), count, 2)),
                dma((2, count)),
            ]
        slots = (2, rows, self.update_cols)
        scratch += [
            pltpu.VMEM((3,) + slots, f32),
            pltpu.VMEM(slots, bf16),
            pltpu.VMEM((2,) + slots, f32),
            pltpu.VMEM(slots, bf16),
            pltpu.VMEM((3,) + norm_grads.shape, f32),
            pltpu.VMEM((self.far_size,) + norm_grads.shape, f32),
            dma((3 + far,)),
            dma((3 + far,)),
            dma((2, 4)),
            dma((2, 3)),
            dma((3, len(self.blocks), 2)),
            dma((4,)),
        ]
        results = pl.pallas_call(
            self.kernel,
            grid=(HEADS,),
            in_specs=[
                head_rows(0),
                head_rows(1),
                head_rows(2),
                pl.BlockSpec((1, length, length), lambda h: (h, 0, 0)),
                once(mixed),
                once(first_low),
                once(weight_out),
                once(cosine),
                once(sine),
                *[once(array) for array in (norm_grads, *norm_state)],
            ]
            + [anywhere] * (7 + len(state)),
            out_specs=[anywhere] * (len(outs) + len(totals)) + [whole(*norm_grads.shape)] * 3 + [anywhere],
            out_shape=outs + totals + norm_outs + [jax.ShapeDtypeStruct((length, width), bf16)],
            scratch_shapes=scratch,
            compiler_params=params(collective_id=1, has_side_effects=True),
            name="back",
        )(
            joined,
            joined,
            joined,
            weights,
            mixed,
            first_low,
            weight_out,
            cosine,
            sine,
            norm_grads,
            *norm_state,
            *feed_sums,
            tokens,
            weight_qkv,
            grad_first,
            *state,
        )
        copied = hand_out(results[: len(outs)])
        updated = [tuple(copied[3 * i : 3 * i + 3]) for i in range(len(masters))]
        return updated, tuple(results[-4:-1]), results[-1]

    def kernel(self, *refs):
        refs = list(refs)

        def take(number):
            taken = refs[:number]
            del refs[:number]
            return taken

        length, width, rows, sizes = self.length, self.width, self.rows, self.far_size
        queries, key_rows, value_rows, weights, mixed, first_low, weight_out, cosine, sine = take(9)
        norm_in, norms, norm_first, norm_second = take(4)
        wide_in, down_in, wide_shard_in, down_shard_in, tokens_in, qkv_in, grad_first_in = take(7)
        state = take(12)
        outs, totals, norm_outs, (input_grad,) = take(12), take(4), take(3), take(1)
        grad_mixed, grad_joined, tokens, weight_qkv, grad_first, square, square_sum = take(7)
        names = ("shard", "near", "low", "high", "keep", "pair_sem", "own_sem")
        groups = {name: dict(zip(names, take(7), strict=True)) for name in self.groups}
        load_buf, grad_buf, store_buf, new_buf, norm_sum, norm_far = take(6)
        norm_send, norm_recv, load_sem, store_sem, new_sem, in_sem = take(6)

        step = pl.program_id(0)
        dp, shard = lax.axis_index("dp"), lax.axis_index("shard")
        core, near, far = dp % 2, dp // 2 % 2, dp // 4
        low_bit, high_bit = far % 2, far // 2
        core_peer, near_peer, shard_peer = (dp + 1 - 2 * core, shard), (dp + 2 - 4 * near, shard), (dp, 1 - shard)

        def far_peer(hop):
            return (dp + ((far + hop) % sizes - far) * 4, shard)

        def remote(source, target, sent, came, peer):
            return pltpu.make_async_remote_copy(
                src_ref=source,
                dst_ref=target,
                send_sem=sent,
                recv_sem=came,
                device_id=peer,
                device_id_type=pl.DeviceIdType.MESH,
            )

        def span(low, height):
            return pl.ds(pl.multiple_of(low, 16), height)

        peers = {
            "core": core_peer,
            "shard": shard_peer,
            "near": near_peer,
            "low": (dp + 4 - 8 * low_bit, shard),
            "high": (dp + 8 - 16 * high_bit, shard),
        }
        bits = {"shard": shard, "near": near, "low": low_bit, "high": high_bit}
        axes = ["shard", "near", "low", "high"]

        class Part:
            def __init__(part, group, index):
                part.group, part.index = group, index
                _, part.lead, part.height, part.columns = self.groups[group]
                part.bufs = groups[group]
                part.held = group == "square"
                part.source = {"wide": wide_in, "down": down_in, "square": square_sum}[group].at[index]
                if part.held:
                    part.keep = part.source.at[:, span(shard * part.height, part.height)]
                else:
                    part.keep = part.bufs["keep"].at[index % (self.ahead + 1)]

            def came(part, axis):
                return part.bufs[axis].at[part.index]

            def rows_after(part, axis):
                low, height = 0, part.height
                for name in axes[1 : axes.index(axis) + 1]:
                    height //= 2
                    low = low + bits[name] * height
                return low, height

            def total(part, axis):
                low, height = part.rows_after(axis)
                index, side = part.index, core
                if part.group == "wide":
                    left = side * (self.inner // 2) + index * part.columns
                    return totals[0].at[:, span(low, height), pl.ds(pl.multiple_of(left, 128), part.columns)]
                left = pl.multiple_of(side * part.columns, 128)
                if part.group == "down":
                    return totals[1].at[:, span(index * part.height + low, height), pl.ds(left, part.columns)]
                if index == 3:
                    return totals[2].at[:, span(low, height), pl.ds(left, part.columns)]
                return totals[3].at[:, span(low, height), pl.ds(index * width + left, part.columns)]

            def copy(part, stage):
                axis, *back = stage.split()
                if back:
                    before = {"high": "high", "low": "low", "near": "near", "core": "shard"}[axis]
                    source = target = part.total(before)
                elif axis == "core":
                    source, target = square.at[part.index, pl.ds(1 - core, 1)], part.source
                else:
                    own = part.source if axis == "shard" else part.came(axes[axes.index(axis) - 1])
                    _, height = part.rows_after(axis)
                    source, target = own.at[:, span((1 - bits[axis]) * height, height)], part.came(axis)
                sem = part.bufs["pair_sem"].at[self.steps.index(stage), part.index]
                return remote(source, target, sem.at[0], sem.at[1], peers[axis])

            def kept(part):
                return pltpu.make_async_copy(
                    part.source.at[:, span(shard * part.height, part.height)],
                    part.keep,
                    part.bufs["own_sem"].at[0, part.index],
                )

            def shard_sum(part):
                source = {"wide": wide_shard_in, "down": down_shard_in}[part.group].at[part.index]
                return pltpu.make_async_copy(source, part.came("shard"), part.bufs["own_sem"].at[0, part.index])

            def own_total(part):
                return pltpu.make_async_copy(
                    part.came("high"), part.total("high"), part.bufs["own_sem"].at[1, part.index]
                )

        units = [[Part(group, index) for group, index in unit] for unit in self.units]
        started = []

        def start(k, stage):
            for part in units[k]:
                part.copy(stage).start()
            started.append((k, stage))

        def arrived(k, stage):
            for part in units[k]:
                part.copy(stage).wait_recv()

        def add_rows(target, sources, lead, height):
            tile = next(size for size in (64, 48, 16) if height % size == 0)

            @pl.loop(0, height // tile)
            def _(i):
                place = span(i * tile, tile)
                for k in range(lead):
                    value = sources[0][k, place, :].astype(f32)
                    for source in sources[1:]:
                        value += source[k, place, :].astype(f32)
                    target[k, place, :] = value.astype(bf16)

        def start_shard(k):
            for part in units[k]:
                if part.held:
                    arrived(k, "core")
                    own = square.at[part.index, pl.ds(core, 1)]
                    add_rows(part.source, [part.source, own], 1, 2 * part.height)
                else:
                    part.kept().start()
            start(k, "shard")

        def take_sum(k, axis):
            if axis == "shard" and k < self.early:
                for part in units[k]:
                    part.shard_sum().wait()
                start(k, "near")
                return
            arrived(k, axis)
            for part in units[k]:
                came = part.came(axis)
                if axis == "shard":
                    if not part.held:
                        part.kept().wait()
                    own = part.keep
                else:
                    _, height = part.rows_after(axis)
                    own = part.came(axes[axes.index(axis) - 1]).at[:, span(bits[axis] * height, height)]
                add_rows(came, [came, own], part.lead, came.shape[1])
            if axis != "high":
                start(k, axes[axes.index(axis) + 1])
                return
            for part in units[k]:
                part.own_total().start()
            for part in units[k]:
                part.own_total().wait()
            start(k, "high total")

        def take_total(k, axis):
            arrived(k, axis + " total")
            start(k, {"high": "low", "low": "near", "near": "core"}[axis] + " total")

        updates = [
            (b, sub) for b, block in enumerate(self.blocks) for sub in range(block[4] // self.update_cols)
        ]

        def update_place(n):
            b, sub = updates[n]
            _, matrix, low, left, _, (part, total_left) = self.blocks[b]
            shift = sub * self.update_cols
            cols = pl.ds(left + shift, self.update_cols)
            return n % 2, matrix, low, cols, part, pl.ds(total_left + shift, self.update_cols)

        def state_loads(n):
            slot, matrix, low, cols, *_ = update_place(n)
            place = pl.ds(low, rows)
            return [
                pltpu.make_async_copy(
                    state[3 * matrix + i].at[place, cols], load_buf.at[i, slot], load_sem.at[slot, i]
                )
                for i in range(3)
            ]

        def grad_load(n):
            slot, matrix, low, _, part, cols = update_place(n)
            grads = totals[matrix].at[part, pl.ds(low, rows), cols]
            return pltpu.make_async_copy(grads, grad_buf.at[slot], load_sem.at[slot, 3])

        def stores_of(n):
            slot, matrix, low, cols, *_ = update_place(n)
            place = pl.ds(low, rows)
            full = span(shard * state[3 * matrix].shape[0] + low, rows)
            return [
                pltpu.make_async_copy(new_buf.at[slot], outs[3 * matrix].at[full, cols], store_sem.at[slot, 2])
            ] + [
                pltpu.make_async_copy(
                    store_buf.at[i, slot], outs[3 * matrix + 1 + i].at[place, cols], store_sem.at[slot, i]
                )
                for i in range(2)
            ]

        waiting = {}

        def load_state(n):
            if n < len(updates):
                for copy in state_loads(n):
                    copy.start()

        def settle(n, left):
            while len(waiting[n]) > left:
                waiting[n].pop(0).wait()

        def update(n):
            slot = n % 2
            for copy in [*state_loads(n), grad_load(n)]:
                copy.wait()
            if n >= 2:
                settle(n - 2, 0)

            @pl.loop(0, rows // 16)
            def _(i):
                place = span(i * 16, 16)
                new, first_new, second_new = adam_update(
                    load_buf[0, slot, place, :],
                    load_buf[1, slot, place, :],
                    load_buf[2, slot, place, :],
                    grad_buf[slot, place, :].astype(f32) * self.scale,
                    learn_rate,
                    decay_rate,
                )
                store_buf[0, slot, place, :] = first_new
                store_buf[1, slot, place, :] = second_new
                new_buf[slot, place, :] = new.astype(bf16)

            waiting[n] = stores_of(n)
            for copy in waiting[n]:
                copy.start()
            load_state(n + 2)

        def new_copy(b, stage):
            _, matrix, first, left, columns, _ = self.blocks[b]
            side = shard if stage == 0 else 1 - shard
            height = rows // 4 if stage < 2 else rows // 2
            by_near = b % 4 == 0
            quarter = near if by_near else low_bit
            low = core * (rows // 2) + (quarter * (rows // 4) if stage < 2 else 0)
            place = outs[3 * matrix].at[
                span(side * state[3 * matrix].shape[0] + first + low, height), pl.ds(left, columns)
            ]
            peer = (shard_peer, near_peer if by_near else peers["low"], core_peer)[stage]
            return remote(place, place, new_sem.at[stage, b, 0], new_sem.at[stage, b, 1], peer)

        def pass_new(b, stage):
            if stage > 0:
                new_copy(b, stage - 1).wait_recv()
            new_copy(b, stage).start()

        def norm_copy(stage, hop=0):
            if stage < 3:
                source = norm_in if stage == 0 else norm_sum.at[stage - 1]
                peer = (core_peer, shard_peer, near_peer)[stage]
                return remote(source, norm_sum.at[stage], norm_send.at[stage], norm_recv.at[stage], peer)
            return remote(
                norm_sum.at[2], norm_far.at[far], norm_send.at[2 + hop], norm_recv.at[2 + hop], far_peer(hop)
            )

        def norm_stage(stage):
            if 1 <= stage <= 3:
                norm_copy(stage - 1).wait_recv()
                before = norm_in[...] if stage == 1 else norm_sum[stage - 2]
                norm_sum[stage - 1] += before
            if stage < 3:
                norm_copy(stage).start()
            elif stage == 3:
                norm_far[far] = norm_sum[2]
                for hop in range(1, sizes):
                    norm_copy(3, hop).start()
            else:
                for hop in range(1, sizes):
                    norm_copy(3, hop).wait_recv()
                total = norm_far[0]
                for place in range(1, sizes):
                    total += norm_far[place]
                new, first_new, second_new = adam_update(
                    norms[...], norm_first[...], norm_second[...], total * self.scale, norm_rate, 0.0
                )
                norm_outs[0][...] = new
                norm_outs[1][...] = first_new
                norm_outs[2][...] = second_new
                for stage in range(3):
                    norm_copy(stage).wait_send()
                for hop in range(1, sizes):
                    norm_copy(3, hop).wait_send()

        count, runs = len(self.units), self.runs
        stages = [functools.partial(take_sum, axis=axis) for axis in axes] + [
            functools.partial(take_total, axis=axis) for axis in ("high", "low", "near")
        ]
        depth = len(stages)
        progress = {"ready": 0, "grad": 0, "update": 0, "near": 0, "core": 0}
        sent_at, near_at = [], []

        def prefetch():
            n = progress["grad"]
            if n < progress["ready"] and n < progress["update"] + 2:
                grad_load(n).start()
                progress["grad"] += 1

        def some_updates(t, most):
            for _ in range(most):
                n = progress["update"]
                if n == progress["ready"]:
                    break
                prefetch()
                prefetch()
                update(n)
                progress["update"] += 1
                b, sub = updates[n]
                if sub == self.blocks[b][4] // self.update_cols - 1:
                    for m in range(n - sub, n + 1):
                        settle(m, 2)
                    pass_new(b, 0)
                    sent_at.append(t)

        def entering(t):
            return [k for k in range(count) if self.entry[k] == t]

        def sending(t):
            ahead = [self.ahead if k < runs else self.ahead - 1 for k in range(count)]
            return [k for k in range(self.early, count) if self.entry[k] - ahead[k] == t]

        slots = max(self.entry) + 1

        def slot(t, most):
            busy = t < slots + depth
            for at, lag, stage, name in ((near_at, 2, 2, "core"), (sent_at, 3, 1, "near")):
                while progress[name] < len(at) and at[progress[name]] <= t - (lag if busy else 1):
                    pass_new(progress[name], stage)
                    progress[name] += 1
                    if stage == 1:
                        near_at.append(t)
            for k in entering(t - depth - 1):
                arrived(k, "core total")
            progress["ready"] = sum(self.blocks[b][0] <= t - depth - 1 for b, _ in updates)
            prefetch()
            for late in range(depth - 1, 0, -1):
                for k in entering(t - late - 1):
                    stages[late](k)
            some_updates(t, most)
            for k in entering(t):
                stages[0](k)
            for k in sending(t):
                start_shard(k)

        inputs = [
            pltpu.make_async_copy(tokens_in, tokens, in_sem.at[0]),
            pltpu.make_async_copy(qkv_in, weight_qkv, in_sem.at[1]),
            pltpu.make_async_copy(grad_first_in, grad_first, in_sem.at[2]),
        ]

        @pl.when(step == 0)
        def _():
            greeted = [core_peer, near_peer, shard_peer] + [far_peer(hop) for hop in range(1, sizes)]
            barrier = pltpu.get_barrier_semaphore()
            for peer in greeted:
                pl.semaphore_signal(barrier, inc=1, device_id=peer, device_id_type=pl.DeviceIdType.MESH)
            pl.semaphore_wait(barrier, len(greeted))
            for t in range(-self.ahead, 0):
                for k in sending(t):
                    start_shard(k)
            for k in range(self.early):
                for part in units[k]:
                    part.shard_sum().start()
            norm_stage(0)
            for copy in inputs:
                copy.start()
            load_state(0)
            load_state(1)
            block = 256
            for low in range(0, width, block):
                grad_mixed[low : low + block] = contract(
                    weight_out[low : low + block], first_low[...], 1, 1
                ).astype(bf16)

        head = lambda part: grad_joined.at[
            pl.ds(pl.multiple_of(part * width + step * HEAD_DIM, HEAD_DIM), HEAD_DIM)
        ]
        own_head = pl.ds(pl.multiple_of(step * HEAD_DIM, HEAD_DIM), HEAD_DIM)
        attend_back_kernel(
            min(256, length),
            queries,
            key_rows,
            value_rows,
            mixed.at[own_head],
            grad_mixed.at[own_head],
            weights,
            cosine,
            sine,
            head(0),
            head(1),
            head(2),
        )

        early = {1: 0, 3: 1, 5: 2, 7: 3, 9: 4, 11: 5}
        for at, t in early.items():

            @pl.when(step == at)
            def _(t=t):
                if t < 3:
                    norm_stage(1 + t)
                slot(t, 0)

        @pl.when(step == HEADS - 1)
        def _():
            half = width // 2
            t = len(early)

            def keep_square(u, value):
                square[u, 0] = value[:, :half].astype(bf16)
                square[u, 1] = value[:, half:].astype(bf16)

            def weight_grad(u):
                keep_square(u, contract(tokens[...], grad_joined[u * width : (u + 1) * width], 0, 1))

            def input_rows(low, height):
                for place in range(low, low + height, min(256, length)):
                    block = slice(place, place + min(256, length))
                    rows_sum = contract(grad_joined[:, block], weight_qkv[...], 0, 1)
                    tokens[block] = (grad_first[block] + rows_sum).astype(bf16)

            inputs[0].wait()
            for u in range(3):
                weight_grad(u)
            keep_square(3, contract(mixed[...], first_low[...], 1, 0))
            for u in range(4):
                start(runs + u, "core")
            slot(t, 0)
            norm_stage(4)
            inputs[1].wait()
            inputs[2].wait()
            input_rows(0, length // 2)
            slot(t + 1, 0)
            input_rows(length // 2, length // 2)
            result = pltpu.make_async_copy(tokens, input_grad, in_sem.at[3])
            result.start()
            later = t + 2
            while later < slots + depth + 1 or progress["core"] < len(self.blocks):
                slot(later, 3)
                later += 1
            for b in range(len(self.blocks)):
                new_copy(b, 2).wait_recv()
            for n in range(len(updates)):
                settle(n, 0)
            for k, stage in started:
                for part in units[k]:
                    part.copy(stage).wait_send()
            for b in range(len(self.blocks)):
                for stage in range(3):
                    new_copy(b, stage).wait_send()
            result.wait()


def shards(
    mesh,
    tokens,
    cotangent,
    master_qkv,
    first_qkv,
    second_qkv,
    master_out,
    first_out,
    second_out,
    master_gate_up,
    first_gate_up,
    second_gate_up,
    master_down,
    first_down,
    second_down,
    norms,
    norm_first,
    norm_second,
):
    links = Links(mesh)
    length, width = tokens.shape
    shard_count = mesh.shape["shard"]
    cosine, sine = rope_tables(length)

    scale_grad = 1.0 / math.sqrt(length * mesh.shape["dp"] * shard_count)
    masters = [
        (master_gate_up, first_gate_up, second_gate_up),
        (master_down, first_down, second_down),
        (master_out, first_out, second_out),
        (master_qkv, first_qkv, second_qkv),
    ]
    norm_state = (norms, norm_first, norm_second)
    if fits(mesh, length, master_qkv.shape[0], master_down.shape[0]):
        rows, long_rows = master_qkv.shape[0], master_down.shape[0]
        inner = shard_count * long_rows
        shapes = [master_out.shape, master_gate_up.shape, master_down.shape]
        mixed, weights, joined, weight_qkv, weight_out, weight_gate_up, weight_down = Front(
            mesh, length, width, rows, shapes
        )(tokens, [master_qkv, master_out, master_gate_up, master_down], cosine, sine)
        normed_one, inverse_one, hidden_low = project_out(tokens, mixed, weight_out, norms)
        gate, up, output, grad_second, grad_low, norm_two = paired_forward(
            hidden_low, weight_gate_up, weight_down, normed_one, norms, cotangent
        )
        wide, down, wide_shard, down_shard, grad_first, first_low, norm_one = paired_backward(
            grad_low,
            hidden_low,
            gate,
            up,
            weight_gate_up,
            weight_down,
            grad_second,
            normed_one,
            inverse_one,
            norms,
        )
        updated, updated_norms, input_grad = Back(
            mesh, length, width, inner, rows, long_rows, gate.shape[0]
        )(
            joined,
            weights,
            mixed,
            first_low,
            weight_out,
            cosine,
            sine,
            [wide, down, wide_shard, down_shard],
            tokens,
            weight_qkv,
            grad_first,
            masters,
            jnp.concatenate([norm_one, norm_two]),
            norm_state,
        )
    else:
        weight_qkv = links.gather_rows(master_qkv.astype(bf16), False)
        weight_out = links.gather_rows(master_out.astype(bf16), False)
        weight_gate_up = links.gather_rows(master_gate_up.astype(bf16), True)
        weight_down = links.gather_rows(master_down.astype(bf16), True)
        joined = project_qkv(tokens, weight_qkv, cosine, sine)
        mixed, weights = attend_forward(joined)
        normed_one, inverse_one, hidden_low = project_out(tokens, mixed, weight_out, norms)
        gate, up, output, grad_second, grad_low, norm_two = feed_forward(
            hidden_low, weight_gate_up, weight_down, normed_one, norms, cotangent
        )
        gate_grad, up_grad, down_grad, grad_first, first_low, norm_one = feed_backward(
            grad_low,
            hidden_low,
            gate,
            up,
            weight_gate_up,
            weight_down,
            grad_second,
            normed_one,
            inverse_one,
            norms,
        )
        out_grad = contract(mixed, first_low, 1, 0).astype(bf16)
        mixed_grad = contract(weight_out, first_low, 1, 1).astype(bf16)
        joined_back = attend_backward(joined, mixed, mixed_grad, weights, cosine, sine)
        joined_back = jnp.concatenate(joined_back, axis=0)
        qkv_grad = contract(tokens, joined_back, 0, 1).astype(bf16)
        input_grad = (grad_first + contract(joined_back, weight_qkv, 0, 1)).astype(bf16)
        totals = [
            jnp.concatenate([links.total(gate_grad), links.total(up_grad)], axis=1),
            links.total(down_grad),
            links.total(out_grad),
            links.total(qkv_grad),
        ]
        updated = []
        for (master, first, second), total in zip(masters, totals, strict=True):
            new, first_new, second_new = adam_update(
                master, first, second, total.astype(f32) * scale_grad, learn_rate, decay_rate
            )
            updated.append((links.gather_rows(new.astype(bf16), True), first_new, second_new))
        norm_total = lax.psum(jnp.concatenate([norm_one, norm_two]), ("dp", "shard"))
        updated_norms = adam_update(*norm_state, norm_total * scale_grad, norm_rate, 0.0)
    (
        (full_gate_up, first_gate_up_new, second_gate_up_new),
        (full_down, first_down_new, second_down_new),
        (full_out, first_out_new, second_out_new),
        (full_qkv, first_qkv_new, second_qkv_new),
    ) = updated
    upd_norms, norm_first_new, norm_second_new = updated_norms
    return (
        output,
        input_grad,
        full_qkv,
        full_out,
        full_gate_up,
        full_down,
        first_qkv_new,
        second_qkv_new,
        first_out_new,
        second_out_new,
        first_gate_up_new,
        second_gate_up_new,
        first_down_new,
        second_down_new,
        upd_norms,
        norm_first_new,
        norm_second_new,
    )


def solution(mesh):
    rows, split, copied = P(("dp", "shard"), None), P("shard", None), P()
    return jax.shard_map(
        functools.partial(shards, mesh),
        mesh=mesh,
        in_specs=(rows, rows) + (split,) * 12 + (copied,) * 3,
        out_specs=(rows, rows) + (copied,) * 4 + (split,) * 8 + (copied,) * 3,
        check_vma=False,
    )
```

```python
import functools
import math

import jax
import jax.numpy as jnp
import numpy as np
from jax import lax
from jax.experimental import pallas as pl
from jax.experimental.pallas import tpu as pltpu
from jax.sharding import PartitionSpec as P

HEADS = 12
HEAD_DIM = 64
STEP = 3

norm_eps = 1e-12
rope_base = 1000.0
learn_rate = 0.03
norm_rate = 0.3
decay_rate = 0.1
adam_eps = 1e-08
beta_first = 0.5
beta_second = 0.5

f32, bf16 = jnp.float32, jnp.bfloat16
VMEM_BYTES = 56 * 2**20


def contract(left, right, left_dim, right_dim):
    return lax.dot_general(
        left, right, (((left_dim,), (right_dim,)), ((), ())), preferred_element_type=f32
    )


def params(**more):
    return pltpu.CompilerParams(vmem_limit_bytes=VMEM_BYTES, **more)


def cost(flops, moved, transcendentals=0):
    return pl.CostEstimate(
        flops=int(flops), bytes_accessed=int(moved), transcendentals=int(transcendentals)
    )


def whole(*shape):
    return pl.BlockSpec(shape, lambda *_: (0,) * len(shape))


def rope_tables(length):
    half = HEAD_DIM // 2
    frequency = np.float32(rope_base) ** (
        -(np.arange(half, dtype=np.float32) * np.float32(2.0 / HEAD_DIM))
    )
    angles = np.arange(length, dtype=np.float32)[None, :] * frequency[:, None]
    return jnp.asarray(np.cos(angles), f32), jnp.asarray(np.sin(angles), f32)


def qkv_kernel(blocks_rotated, heads_block, tokens, weight, cosine, sine, joined):
    step = pl.program_id(0)
    rows = contract(weight[...], tokens[...], 0, 1)
    half = HEAD_DIM // 2

    @pl.when(step < 2 * blocks_rotated)
    def _():
        scale = jnp.where(step < blocks_rotated, 1.0 / math.sqrt(HEAD_DIM), 1.0)
        cos, sin = cosine[...] * scale, sine[...] * scale
        for head in range(heads_block):
            low = head * HEAD_DIM
            t1, t2 = rows[low : low + half], rows[low + half : low + 2 * half]
            joined[low : low + half] = (t1 * cos - t2 * sin).astype(bf16)
            joined[low + half : low + 2 * half] = (t2 * cos + t1 * sin).astype(bf16)

    @pl.when(step >= 2 * blocks_rotated)
    def _():
        joined[...] = rows.astype(bf16)


def project_qkv(tokens, weight, cosine, sine):
    length, width = tokens.shape
    heads_block = 4
    block = heads_block * HEAD_DIM
    count = weight.shape[1] // block
    return pl.pallas_call(
        functools.partial(qkv_kernel, count // 3, heads_block),
        grid=(count,),
        in_specs=[
            whole(length, width),
            pl.BlockSpec((width, block), lambda i: (0, i)),
            whole(*cosine.shape),
            whole(*sine.shape),
        ],
        out_specs=pl.BlockSpec((block, length), lambda i: (i, 0)),
        out_shape=jax.ShapeDtypeStruct((weight.shape[1], length), bf16),
        compiler_params=params(),
        cost_estimate=cost(2 * length * width * weight.shape[1], 2 * weight.size * 3),
        name="qkv_rope",
    )(tokens, weight, cosine, sine)


def attend_head(queries, key_rows, value_rows, mixed, weights):
    length = queries.shape[1]
    chunk = min(512, length)

    def scores_of(low):
        return contract(key_rows[...], queries[:, pl.ds(low, chunk)], 0, 0)

    scores = scores_of(0)
    for low in range(0, length, chunk):
        span = pl.ds(low, chunk)
        following = scores_of(low + chunk) if low + chunk < length else None
        highest = jnp.max(scores, axis=0, keepdims=True)
        expanded = jnp.exp(scores - highest)
        totals = jnp.sum(expanded, axis=0, keepdims=True)
        soft = (expanded * (1.0 / totals)).astype(bf16)
        weights[0, :, span] = soft
        mixed[:, span] = contract(value_rows[...], soft, 1, 0).astype(bf16)
        scores = following


def attend_forward(joined):
    length = joined.shape[1]
    head_rows = lambda part: pl.BlockSpec(
        (HEAD_DIM, length), lambda h: (part * HEADS + h, 0)
    )
    return pl.pallas_call(
        attend_head,
        grid=(HEADS,),
        in_specs=[head_rows(0), head_rows(1), head_rows(2)],
        out_specs=[
            pl.BlockSpec((HEAD_DIM, length), lambda h: (h, 0)),
            pl.BlockSpec((1, length, length), lambda h: (h, 0, 0)),
        ],
        out_shape=[
            jax.ShapeDtypeStruct((HEADS * HEAD_DIM, length), bf16),
            jax.ShapeDtypeStruct((HEADS, length, length), bf16),
        ],
        compiler_params=params(),
        cost_estimate=cost(
            16 * HEADS * length * length * HEAD_DIM, 2 * HEADS * length * length, length * length * HEADS
        ),
        name="attend_forward",
    )(joined, joined, joined)


def attend_back_kernel(
    chunk,
    queries,
    key_rows,
    value_rows,
    mixed,
    grad_mixed,
    weights,
    cosine,
    sine,
    query_out,
    key_out,
    value_out,
):
    length = queries.shape[1]
    half = HEAD_DIM // 2
    grad = grad_mixed[...]
    centre = jnp.sum(grad.astype(f32) * mixed[...].astype(f32), axis=0, keepdims=True)
    query_grad = jnp.zeros((HEAD_DIM, length), f32)
    key_parts = []
    for low in range(0, length, chunk):
        span = pl.ds(low, chunk)
        soft = weights[0, span, :]
        weight_grad = contract(value_rows[:, span], grad, 0, 0)
        score_grad = (soft.astype(f32) * (weight_grad - centre)).astype(bf16)
        value_out[:, span] = contract(grad, soft, 1, 1).astype(bf16)
        key_parts.append(contract(queries[...], score_grad, 1, 1))
        query_grad += contract(key_rows[:, span], score_grad, 1, 0)
    key_grad = jnp.concatenate(key_parts, axis=1)
    cos, sin = cosine[...], sine[...]
    scale = 1.0 / math.sqrt(HEAD_DIM)
    for out, grad_rows, factor in ((query_out, query_grad, scale), (key_out, key_grad, 1.0)):
        d1, d2 = grad_rows[:half], grad_rows[half:]
        out[:half] = ((d1 * cos + d2 * sin) * factor).astype(bf16)
        out[half:] = ((d2 * cos - d1 * sin) * factor).astype(bf16)


def attend_backward(joined, mixed, grad_mixed, weights, cosine, sine):
    length = joined.shape[1]
    head_rows = lambda part: pl.BlockSpec(
        (HEAD_DIM, length), lambda h: (part * HEADS + h, 0)
    )
    rows = jax.ShapeDtypeStruct((HEADS * HEAD_DIM, length), bf16)
    return pl.pallas_call(
        functools.partial(attend_back_kernel, min(256, length)),
        grid=(HEADS,),
        in_specs=[
            head_rows(0),
            head_rows(1),
            head_rows(2),
            head_rows(0),
            head_rows(0),
            pl.BlockSpec((1, length, length), lambda h: (h, 0, 0)),
            whole(*cosine.shape),
            whole(*sine.shape),
        ],
        out_specs=[head_rows(0)] * 3,
        out_shape=[rows] * 3,
        compiler_params=params(),
        cost_estimate=cost(
            32 * HEADS * length * length * HEAD_DIM, 2 * HEADS * length * length
        ),
        name="attend_backward",
    )(joined, joined, joined, mixed, grad_mixed, weights, cosine, sine)


def norm_rows(values):
    centred = values - jnp.mean(values, axis=1, keepdims=True)
    inverse = lax.rsqrt(jnp.mean(centred * centred, axis=1, keepdims=True) + norm_eps)
    return centred * inverse, inverse


def norm_back(grad_rows, normed, inverse, gain_row):
    scaled = grad_rows * gain_row
    centred = (
        scaled
        - jnp.mean(scaled, axis=1, keepdims=True)
        - normed * jnp.mean(scaled * normed, axis=1, keepdims=True)
    )
    gain = jnp.sum(grad_rows * normed, axis=0, keepdims=True)
    bias = jnp.sum(grad_rows, axis=0, keepdims=True)
    return centred * inverse, gain, bias


def out_kernel(tokens, mixed, weight, norms, normed, inverse, hidden_low):
    sums = tokens[...].astype(f32) + contract(mixed[...], weight[...], 0, 0)
    rows, scale = norm_rows(sums)
    normed[...] = rows
    inverse[...] = scale
    hidden_low[...] = (rows * norms[0:1, :] + norms[1:2, :]).astype(bf16)


def project_out(tokens, mixed, weight, norms):
    length, width = tokens.shape
    block = min(256, length)
    return pl.pallas_call(
        out_kernel,
        grid=(length // block,),
        in_specs=[
            pl.BlockSpec((block, width), lambda i: (i, 0)),
            pl.BlockSpec((width, block), lambda i: (0, i)),
            whole(width, width),
            whole(*norms.shape),
        ],
        out_specs=[
            pl.BlockSpec((block, width), lambda i: (i, 0)),
            pl.BlockSpec((block, 1), lambda i: (i, 0)),
            pl.BlockSpec((block, width), lambda i: (i, 0)),
        ],
        out_shape=[
            jax.ShapeDtypeStruct((length, width), f32),
            jax.ShapeDtypeStruct((length, 1), f32),
            jax.ShapeDtypeStruct((length, width), bf16),
        ],
        compiler_params=params(),
        cost_estimate=cost(2 * length * width * width, 10 * length * width),
        name="out_norm",
    )(tokens, mixed, weight, norms)


def second_norm(rows_block, norms, cotangent, output, grad_second, grad_low, norm_grads, total):
    gain_sum = jnp.zeros((1, total.shape[1]), f32)
    bias_sum = jnp.zeros((1, total.shape[1]), f32)
    for low in range(0, total.shape[0], rows_block):
        span = pl.ds(low, rows_block)
        rows, inverse = norm_rows(total[span, :])
        output[span, :] = (rows * norms[2:3, :] + norms[3:4, :]).astype(bf16)
        back, gain, bias = norm_back(cotangent[span, :].astype(f32), rows, inverse, norms[2:3, :])
        grad_second[span, :] = back
        grad_low[span, :] = back.astype(bf16)
        gain_sum += gain
        bias_sum += bias
    norm_grads[0:1, :] = gain_sum
    norm_grads[1:2, :] = bias_sum


def first_norm_back(
    rows_block, normed, inverse, norms, total, grad_first, first_low, norm_grads
):
    gain_sum = jnp.zeros((1, total.shape[1]), f32)
    bias_sum = jnp.zeros((1, total.shape[1]), f32)
    for low in range(0, total.shape[0], rows_block):
        span = pl.ds(low, rows_block)
        back, gain, bias = norm_back(
            total[span, :], normed[span, :], inverse[span, :], norms[0:1, :]
        )
        grad_first[span, :] = back
        first_low[span, :] = back.astype(bf16)
        gain_sum += gain
        bias_sum += bias
    norm_grads[0:1, :] = gain_sum
    norm_grads[1:2, :] = bias_sum


def forward_kernel(
    rows_block,
    hidden_low,
    gate_weight,
    up_weight,
    down_weight,
    normed_one,
    norms,
    cotangent,
    gate,
    up,
    output,
    grad_second,
    grad_low,
    norm_grads,
    total,
):
    step = pl.program_id(0)
    length = hidden_low.shape[0]
    for low in range(0, length, rows_block):
        span = pl.ds(low, rows_block)
        gate_part = contract(hidden_low[span, :], gate_weight[...], 1, 0)
        up_part = contract(hidden_low[span, :], up_weight[...], 1, 0)
        gate[span, :] = gate_part
        up[span, :] = up_part
        inner = (gate_part * jax.nn.sigmoid(gate_part) * up_part).astype(bf16)
        part = contract(inner, down_weight[...], 1, 0)

        @pl.when(step == 0)
        def _():
            total[span, :] = part

        @pl.when(step > 0)
        def _():
            total[span, :] += part

    @pl.when(step == pl.num_programs(0) - 1)
    def _():
        total[...] += normed_one[...] * norms[0:1, :] + norms[1:2, :]
        second_norm(rows_block, norms, cotangent, output, grad_second, grad_low, norm_grads, total)


def feed_forward(hidden_low, gate_up, down, normed_one, norms, cotangent):
    length, width = hidden_low.shape
    inner = down.shape[0]
    block = min(512, inner)
    count = inner // block
    return pl.pallas_call(
        functools.partial(forward_kernel, min(256, length)),
        grid=(count,),
        in_specs=[
            whole(length, width),
            pl.BlockSpec((width, block), lambda j: (0, j)),
            pl.BlockSpec((width, block), lambda j: (0, count + j)),
            pl.BlockSpec((block, width), lambda j: (j, 0)),
            whole(length, width),
            whole(*norms.shape),
            whole(length, width),
        ],
        out_specs=[
            pl.BlockSpec((length, block), lambda j: (0, j)),
            pl.BlockSpec((length, block), lambda j: (0, j)),
            whole(length, width),
            whole(length, width),
            whole(length, width),
            whole(2, width),
        ],
        out_shape=[
            jax.ShapeDtypeStruct((length, inner), f32),
            jax.ShapeDtypeStruct((length, inner), f32),
            jax.ShapeDtypeStruct((length, width), bf16),
            jax.ShapeDtypeStruct((length, width), f32),
            jax.ShapeDtypeStruct((length, width), bf16),
            jax.ShapeDtypeStruct((2, width), f32),
        ],
        scratch_shapes=[pltpu.VMEM((length, width), f32)],
        compiler_params=params(),
        cost_estimate=cost(6 * length * width * inner, 8 * length * inner),
        name="feed_forward",
    )(hidden_low, gate_up, gate_up, down, normed_one, norms, cotangent)


def backward_kernel(
    rows_block,
    grad_low,
    hidden_low,
    gate,
    up,
    gate_weight,
    up_weight,
    down_weight,
    before,
    normed,
    inverse,
    norms,
    gate_out,
    up_out,
    down_out,
    grad_first,
    first_low,
    norm_grads,
    total,
    inner,
    gate_back,
    up_back,
):
    step = pl.program_id(0)
    length = hidden_low.shape[0]

    @pl.when(step == 0)
    def _():
        total[...] = before[...]

    for low in range(0, length, rows_block):
        span = pl.ds(low, rows_block)
        inner_grad = contract(grad_low[span, :], down_weight[...], 1, 1)
        gate_part, up_part = gate[span, :], up[span, :]
        sigmoid = jax.nn.sigmoid(gate_part)
        swished = gate_part * sigmoid
        inner[span, :] = (swished * up_part).astype(bf16)
        gate_grad = inner_grad * up_part * sigmoid * (1.0 + gate_part * (1.0 - sigmoid))
        gate_low, up_low = gate_grad.astype(bf16), (inner_grad * swished).astype(bf16)
        gate_back[span, :] = gate_low
        up_back[span, :] = up_low
        total[span, :] += contract(gate_low, gate_weight[...], 1, 1) + contract(
            up_low, up_weight[...], 1, 1
        )
    down_out[...] = contract(inner[...], grad_low[...], 0, 0).astype(bf16)
    gate_out[...] = contract(hidden_low[...], gate_back[...], 0, 0).astype(bf16)
    up_out[...] = contract(hidden_low[...], up_back[...], 0, 0).astype(bf16)

    @pl.when(step == pl.num_programs(0) - 1)
    def _():
        first_norm_back(rows_block, normed, inverse, norms, total, grad_first, first_low, norm_grads)


def feed_backward(
    grad_low, hidden_low, gate, up, gate_up, down, before, normed, inverse, norms
):
    length, width = hidden_low.shape
    inner = down.shape[0]
    block = min(256, inner)
    count = inner // block
    in_cols = lambda shift: pl.BlockSpec((width, block), lambda j: (0, shift + j))
    wide = pl.BlockSpec((length, block), lambda j: (0, j))
    narrow = pl.BlockSpec((block, width), lambda j: (j, 0))
    full = whole(length, width)
    return pl.pallas_call(
        functools.partial(backward_kernel, min(256, length)),
        grid=(count,),
        in_specs=[
            full,
            full,
            wide,
            wide,
            in_cols(0),
            in_cols(count),
            narrow,
            full,
            full,
            whole(length, 1),
            whole(*norms.shape),
        ],
        out_specs=[in_cols(0), in_cols(0), narrow, full, full, whole(2, width)],
        out_shape=[
            jax.ShapeDtypeStruct((width, inner), bf16),
            jax.ShapeDtypeStruct((width, inner), bf16),
            jax.ShapeDtypeStruct((inner, width), bf16),
            jax.ShapeDtypeStruct((length, width), f32),
            jax.ShapeDtypeStruct((length, width), bf16),
            jax.ShapeDtypeStruct((2, width), f32),
        ],
        scratch_shapes=[pltpu.VMEM((length, width), f32)] + [pltpu.VMEM((length, block), bf16)] * 3,
        compiler_params=params(),
        cost_estimate=cost(12 * length * width * inner, 8 * length * inner),
        name="feed_backward",
    )(grad_low, hidden_low, gate, up, gate_up, gate_up, down, before, normed, inverse, norms)


def paired_forward_kernel(
    rows_block,
    hidden_low,
    gate_0,
    gate_1,
    up_0,
    up_1,
    down_0,
    down_1,
    normed_one,
    norms,
    cotangent,
    gate,
    up,
    output,
    grad_second,
    grad_low,
    norm_grads,
    total,
):
    step = pl.program_id(0)
    length = hidden_low.shape[0]
    run = gate.shape[2] // 2
    gate_weight = jnp.concatenate([gate_0[...], gate_1[...]], axis=1)
    up_weight = jnp.concatenate([up_0[...], up_1[...]], axis=1)
    down_weight = jnp.concatenate([down_0[...], down_1[...]], axis=0)

    def keep(target, span, part):
        for i in range(2):
            target[i, span, :run] = part[:, i * run : (i + 1) * run]
            target[i, span, run:] = part[:, (2 + i) * run : (3 + i) * run]

    @pl.when(step == 0)
    def _():
        total[...] = normed_one[...] * norms[0:1, :] + norms[1:2, :]

    def products(low):
        rows = hidden_low[pl.ds(low, rows_block), :]
        return contract(rows, gate_weight, 1, 0), contract(rows, up_weight, 1, 0)

    following = products(0)
    for low in range(0, length, rows_block):
        span = pl.ds(low, rows_block)
        gate_part, up_part = following
        if low + rows_block < length:
            following = products(low + rows_block)
        keep(gate, span, gate_part)
        keep(up, span, up_part)
        inner = (gate_part * jax.nn.sigmoid(gate_part) * up_part).astype(bf16)
        total[span, :] += contract(inner, down_weight, 1, 0)

    @pl.when(step == pl.num_programs(0) - 1)
    def _():
        second_norm(min(256, length), norms, cotangent, output, grad_second, grad_low, norm_grads, total)


def paired_forward(hidden_low, gate_up, down, normed_one, norms, cotangent):
    length, width = hidden_low.shape
    inner = down.shape[0]
    run = 256
    count = inner // (2 * run)
    cols = lambda shift: pl.BlockSpec((width, run), lambda j: (0, shift * count + j))
    kept = pl.BlockSpec((2, length, run), lambda j: (j, 0, 0))
    kept_shape = jax.ShapeDtypeStruct((2 * count, length, run), f32)
    return pl.pallas_call(
        functools.partial(paired_forward_kernel, min(256, length)),
        grid=(count,),
        in_specs=[
            whole(length, width),
            cols(0),
            cols(1),
            cols(2),
            cols(3),
            pl.BlockSpec((run, width), lambda j: (j, 0)),
            pl.BlockSpec((run, width), lambda j: (count + j, 0)),
            whole(length, width),
            whole(*norms.shape),
            whole(length, width),
        ],
        out_specs=[
            kept,
            kept,
            whole(length, width),
            whole(length, width),
            whole(length, width),
            whole(2, width),
        ],
        out_shape=[
            kept_shape,
            kept_shape,
            jax.ShapeDtypeStruct((length, width), bf16),
            jax.ShapeDtypeStruct((length, width), f32),
            jax.ShapeDtypeStruct((length, width), bf16),
            jax.ShapeDtypeStruct((2, width), f32),
        ],
        scratch_shapes=[pltpu.VMEM((length, width), f32)],
        compiler_params=params(),
        cost_estimate=cost(6 * length * width * inner, 8 * length * inner),
        name="feed_forward",
    )(hidden_low, *[gate_up] * 4, down, down, normed_one, norms, cotangent)


EARLY_STEPS = (5, 7, 8, 10, 11, 12)


def paired_backward_kernel(
    rows_block,
    grad_low,
    hidden_low,
    gate,
    up,
    gate_0,
    gate_1,
    up_0,
    up_1,
    down_0,
    down_1,
    before,
    normed,
    inverse,
    norms,
    wide_out,
    down_out,
    wide_shard_out,
    down_shard_out,
    grad_first,
    first_low,
    norm_grads,
    total,
    inner,
    gate_back,
    up_back,
    wide_part,
    down_part,
    wide_sum,
    down_sum,
    wide_shard,
    down_shard,
    before_sem,
    core_sem,
    out_sem,
    shard_sem,
):
    step, last = pl.program_id(0), pl.num_programs(0) - 1
    early = wide_shard.shape[0]
    length, width = hidden_low.shape
    run = gate.shape[2] // 2
    dp, shard = lax.axis_index("dp"), lax.axis_index("shard")
    core = dp % 2
    peer = (dp + 1 - 2 * core, shard)
    start_total = pltpu.make_async_copy(before, total, before_sem)

    def sends(j):
        for i, (part, whole_sum) in enumerate(((wide_part, wide_sum), (down_part, down_sum))):
            yield pltpu.make_async_remote_copy(
                src_ref=part.at[j % 2, 1 - core],
                dst_ref=whole_sum.at[j],
                send_sem=core_sem.at[i, j, 0],
                recv_sem=core_sem.at[i, j, 1],
                device_id=peer,
                device_id_type=pl.DeviceIdType.MESH,
            )

    def keeps(j):
        yield pltpu.make_async_copy(wide_sum.at[j], wide_out.at[j], out_sem.at[0, j])
        yield pltpu.make_async_copy(down_sum.at[j], down_out.at[j], out_sem.at[1, j])

    def shard_keeps(j):
        yield pltpu.make_async_copy(wide_shard.at[j], wide_shard_out.at[j], out_sem.at[0, j])
        yield pltpu.make_async_copy(down_shard.at[j], down_shard_out.at[j], out_sem.at[1, j])

    shard_parts = ((wide_sum, wide_shard), (down_sum, down_shard))

    def shard_sends(j):
        for i, (whole_sum, target) in enumerate(shard_parts):
            height = target.shape[2]
            low = pl.multiple_of((1 - shard) * height, 16)
            yield pltpu.make_async_remote_copy(
                src_ref=whole_sum.at[j, :, pl.ds(low, height)],
                dst_ref=target.at[j],
                send_sem=shard_sem.at[i, j, 0],
                recv_sem=shard_sem.at[i, j, 1],
                device_id=(dp, 1 - shard),
                device_id_type=pl.DeviceIdType.MESH,
            )

    def add_shards(j):
        for copy in shard_sends(j):
            copy.wait_recv()
        for whole_sum, target in shard_parts:
            _, lead, height, _ = target.shape

            @pl.loop(0, height // 64)
            def _(i):
                span = pl.ds(pl.multiple_of(i * 64, 64), 64)
                own = pl.ds(pl.multiple_of(shard * height + i * 64, 64), 64)
                for k in range(lead):
                    value = target[j, k, span, :].astype(f32) + whole_sum[j, k, own, :].astype(f32)
                    target[j, k, span, :] = value.astype(bf16)

        for copy in shard_keeps(j):
            copy.start()

    def add_cores(j):
        for copy in sends(j):
            copy.wait_recv()

        @pl.loop(0, width // 64)
        def _(i):
            span = pl.ds(pl.multiple_of(i * 64, 64), 64)
            for k in range(2):
                value = wide_sum[j, k, span, :].astype(f32) + wide_part[j % 2, core, k, span, :].astype(f32)
                wide_sum[j, k, span, :] = value.astype(bf16)

        @pl.loop(0, 2 * run // 32)
        def _(i):
            span = pl.ds(pl.multiple_of(i * 32, 32), 32)
            value = down_sum[j, 0, span, :].astype(f32) + down_part[j % 2, core, 0, span, :].astype(f32)
            down_sum[j, 0, span, :] = value.astype(bf16)

    @pl.when(step == 0)
    def _():
        start_total.start()
        barrier = pltpu.get_barrier_semaphore()
        for other in (peer, (dp, 1 - shard)):
            pl.semaphore_signal(barrier, inc=1, device_id=other, device_id_type=pl.DeviceIdType.MESH)
        pl.semaphore_wait(barrier, 2)
        start_total.wait()

    gate_weight = jnp.concatenate([gate_0[...], gate_1[...]], axis=1)
    up_weight = jnp.concatenate([up_0[...], up_1[...]], axis=1)
    down_weight = jnp.concatenate([down_0[...], down_1[...]], axis=0)
    def inner_grads(low):
        return contract(grad_low[pl.ds(low, rows_block), :], down_weight, 1, 1)

    following = inner_grads(0)
    for low in range(0, length, rows_block):
        span = pl.ds(low, rows_block)
        inner_grad = following
        if low + rows_block < length:
            following = inner_grads(low + rows_block)
        gate_part, up_part = gate[0, span, :], up[0, span, :]
        sigmoid = jax.nn.sigmoid(gate_part)
        swished = gate_part * sigmoid
        inner[span, :] = (swished * up_part).astype(bf16)
        gate_grad = inner_grad * up_part * sigmoid * (1.0 + gate_part * (1.0 - sigmoid))
        gate_low, up_low = gate_grad.astype(bf16), (inner_grad * swished).astype(bf16)
        gate_back[span, :] = gate_low
        up_back[span, :] = up_low
        total[span, :] += contract(gate_low, gate_weight, 1, 1) + contract(up_low, up_weight, 1, 1)

    @pl.when(step >= 2)
    def _():
        for copy in sends(step - 2):
            copy.wait_send()

    slot, half = step % 2, width // 2
    rows = contract(inner[...], grad_low[...], 0, 0).astype(bf16)
    down_part[slot, 0, 0] = rows[:, :half]
    down_part[slot, 1, 0] = rows[:, half:]
    for i, back in enumerate((gate_back, up_back)):
        columns = contract(hidden_low[...], back[...], 0, 0).astype(bf16)
        wide_part[slot, 0, i] = columns[:, :run]
        wide_part[slot, 1, i] = columns[:, run:]
    for copy in sends(step):
        copy.start()

    @pl.when(step >= 1)
    def _():
        add_cores(step - 1)

    @pl.when((step >= 1) & (step <= early))
    def _():
        for copy in shard_sends(step - 1):
            copy.start()

    @pl.when(step > early)
    def _():
        for copy in keeps(step - 1):
            copy.start()

    for j, at in enumerate(EARLY_STEPS[:-1]):

        @pl.when(step == at)
        def _(j=j):
            add_shards(j)

    @pl.when(step == last)
    def _():
        first_norm_back(min(256, length), normed, inverse, norms, total, grad_first, first_low, norm_grads)
        add_cores(step)
        for copy in keeps(step):
            copy.start()
        add_shards(early - 1)
        for copy in [*sends(step - 1), *sends(step)]:
            copy.wait_send()

        @pl.loop(0, early)
        def _(j):
            for copy in shard_sends(j):
                copy.wait_send()
            for copy in shard_keeps(j):
                copy.wait()

        @pl.loop(early, last + 1)
        def _(j):
            for copy in keeps(j):
                copy.wait()


def paired_backward(
    grad_low, hidden_low, gate, up, gate_up, down, before, normed, inverse, norms
):
    early, rows = len(EARLY_STEPS), hidden_low.shape[1] // 2
    length, width = hidden_low.shape
    count, _, block = gate.shape
    run = block // 2
    cols = lambda shift: pl.BlockSpec((width, run), lambda j: (0, shift * count + j))
    kept = pl.BlockSpec((1, length, block), lambda j: (j, 0, 0))
    anywhere = pl.BlockSpec(memory_space=pl.ANY)
    full = whole(length, width)
    dma = pltpu.SemaphoreType.DMA
    wide, narrow = (2, width, run), (1, block, width // 2)
    return pl.pallas_call(
        functools.partial(paired_backward_kernel, min(256, length)),
        grid=(count,),
        in_specs=[
            full,
            full,
            kept,
            kept,
            cols(0),
            cols(1),
            cols(2),
            cols(3),
            pl.BlockSpec((run, width), lambda j: (j, 0)),
            pl.BlockSpec((run, width), lambda j: (count + j, 0)),
            anywhere,
            full,
            whole(length, 1),
            whole(*norms.shape),
        ],
        out_specs=[anywhere] * 4 + [full, full, whole(2, width)],
        out_shape=[
            jax.ShapeDtypeStruct((count,) + wide, bf16),
            jax.ShapeDtypeStruct((count,) + narrow, bf16),
            jax.ShapeDtypeStruct((early, 2, rows, run), bf16),
            jax.ShapeDtypeStruct((early, 1, run, width // 2), bf16),
            jax.ShapeDtypeStruct((length, width), f32),
            jax.ShapeDtypeStruct((length, width), bf16),
            jax.ShapeDtypeStruct((2, width), f32),
        ],
        scratch_shapes=[pltpu.VMEM((length, width), f32)]
        + [pltpu.VMEM((length, block), bf16)] * 3
        + [
            pltpu.VMEM((2, 2) + wide, bf16),
            pltpu.VMEM((2, 2) + narrow, bf16),
            pltpu.VMEM((count,) + wide, bf16),
            pltpu.VMEM((count,) + narrow, bf16),
            pltpu.VMEM((early, 2, rows, run), bf16),
            pltpu.VMEM((early, 1, run, width // 2), bf16),
            dma,
            dma((2, count, 2)),
            dma((2, count)),
            dma((2, early, 2)),
        ],
        compiler_params=params(collective_id=3, has_side_effects=True),
        cost_estimate=cost(12 * length * width * down.shape[0], 8 * length * down.shape[0]),
        name="feed_backward",
    )(grad_low, hidden_low, gate, up, *[gate_up] * 4, down, down, before, normed, inverse, norms)


class Links:
    def __init__(self, mesh):
        self.sizes = {"dp": mesh.shape["dp"], "shard": mesh.shape["shard"]}
        chips = self.sizes["dp"] // 2
        near = 2 if chips % 2 == 0 else 1
        self.core = ("dp", 1, 2)
        self.near = ("dp", 2, near)
        self.far = ("dp", 2 * near, chips // near)
        self.shard = ("shard", 1, self.sizes["shard"])

    def place(self, digit):
        axis, stride, size = digit
        return (lax.axis_index(axis) // stride) % size

    def shift(self, value, digit, step):
        axis, stride, size = digit
        pairs = []
        for i in range(self.sizes[axis]):
            own = (i // stride) % size
            pairs.append((i, i + ((own + step) % size - own) * stride))
        return lax.ppermute(value, axis, pairs)

    def scatter_sum(self, value, digit, dim):
        size = digit[2]
        if size == 1:
            return value
        own = self.place(digit)
        width = value.shape[dim] // size

        def piece(index):
            return lax.dynamic_slice_in_dim(value, index * width, width, dim)

        total = piece(own).astype(f32)
        for step in range(1, size):
            total += self.shift(piece((own + step) % size), digit, step).astype(f32)
        return total.astype(bf16)

    def gather(self, value, digit, dim):
        size = digit[2]
        if size == 1:
            return value
        own = self.place(digit)
        width = value.shape[dim]
        if size == 2:
            other = self.shift(value, digit, 1)
            first = jnp.where(own == 0, value, other)
            second = jnp.where(own == 0, other, value)
            return jnp.concatenate([first, second], axis=dim)
        shape = list(value.shape)
        shape[dim] *= size
        full = lax.dynamic_update_slice_in_dim(
            jnp.zeros(shape, value.dtype), value, own * width, dim
        )
        for step in range(1, size):
            came = self.shift(value, digit, step)
            full = lax.dynamic_update_slice_in_dim(
                full, came, ((own - step) % size) * width, dim
            )
        return full

    def gather_rows(self, value, spread):
        parts = [self.core, self.near] if spread else [self.core]
        piece = value
        for digit in parts:
            width = piece.shape[0] // digit[2]
            piece = lax.dynamic_slice_in_dim(piece, self.place(digit) * width, width, 0)
        size = self.shard[2]
        rows = value.shape[0]
        own = self.place(self.shard)
        full = lax.dynamic_update_slice_in_dim(
            jnp.zeros((size * rows, value.shape[1]), value.dtype), value, own * rows, 0
        )
        for step in range(1, size):
            came = self.shift(piece, self.shard, step)
            for digit in reversed(parts):
                came = self.gather(came, digit, 0)
            full = lax.dynamic_update_slice_in_dim(full, came, ((own - step) % size) * rows, 0)
        return full

    def total(self, grads):
        grads = self.scatter_sum(grads, self.core, 1)
        grads = self.scatter_sum(grads, self.shard, 0)
        grads = self.scatter_sum(grads, self.near, 0)
        grads = self.scatter_sum(grads, self.far, 0)
        grads = self.gather(grads, self.far, 0)
        grads = self.gather(grads, self.near, 0)
        return self.gather(grads, self.core, 1)


def adam_update(weight, first_moment, second_moment, gradient, rate, decay_on):
    first_new = beta_first * first_moment + (1.0 - beta_first) * gradient
    second_new = beta_second * second_moment + (1.0 - beta_second) * gradient * gradient
    fix_first = 1.0 - beta_first**STEP
    fix_second = 1.0 - beta_second**STEP
    direction = first_new / fix_first / (jnp.sqrt(second_new / fix_second) + adam_eps)
    return (weight - rate * (direction + decay_on * weight), first_new, second_new)


def fits(mesh, length, rows, long_rows):
    far = mesh.shape["dp"] // 4
    return (
        mesh.shape["shard"] == 2
        and mesh.shape["dp"] == 16
        and length % 512 == 0
        and rows % (32 * far) == 0
        and long_rows % (4 * Back.update_cols) == 0
        and long_rows % (128 * HEADS) == 0
        and 128 % (32 * far) == 0
    )


class Front:
    def __init__(self, mesh, length, width, rows, matrices):
        self.length, self.width, self.rows = length, width, rows
        self.matrices = matrices
        self.units = []
        for i, shape in enumerate(matrices):
            for low in range(0, shape[0], rows):
                for left in range(0, shape[1], width):
                    self.units.append((i, low, left))

    def __call__(self, tokens, masters, cosine, sine):
        length, width, rows = self.length, self.width, self.rows
        dma = pltpu.SemaphoreType.DMA
        anywhere = pl.BlockSpec(memory_space=pl.ANY)
        fulls = [jax.ShapeDtypeStruct((2 * shape[0], shape[1]), bf16) for shape in self.matrices]
        count = 3 + len(self.units)
        return pl.pallas_call(
            self.kernel,
            grid=(HEADS,),
            in_specs=[whole(length, width), whole(*cosine.shape), whole(*sine.shape)] + [anywhere] * 4,
            out_specs=[
                pl.BlockSpec((HEAD_DIM, length), lambda h: (h, 0)),
                pl.BlockSpec((1, length, length), lambda h: (h, 0, 0)),
            ]
            + [anywhere] * 5,
            out_shape=[
                jax.ShapeDtypeStruct((width, length), bf16),
                jax.ShapeDtypeStruct((HEADS, length, length), bf16),
                jax.ShapeDtypeStruct((3 * width, length), bf16),
                jax.ShapeDtypeStruct((width, 3 * width), bf16),
                *fulls,
            ],
            scratch_shapes=[
                pltpu.VMEM((3 * width, length), bf16),
                pltpu.VMEM((3, width, width), bf16),
                pltpu.VMEM((len(self.units), rows, width), bf16),
                pltpu.VMEM((3, rows, width), f32),
                dma((4, count, 2)),
                dma((3,)),
                dma((len(self.units),)),
                dma((4,)),
            ],
            compiler_params=params(collective_id=2, has_side_effects=True),
            name="front",
        )(tokens, cosine, sine, *masters)

    def kernel(
        self,
        tokens,
        cosine,
        sine,
        master_qkv,
        master_out,
        master_gate_up,
        master_down,
        mixed,
        weights,
        joined_out,
        qkv_out,
        full_out,
        full_gate_up,
        full_down,
        joined,
        qkv,
        own_low,
        wide,
        pair_sem,
        load_sem,
        own_sem,
        out_sem,
    ):
        width, rows = self.width, self.rows
        step = pl.program_id(0)
        dp, shard = lax.axis_index("dp"), lax.axis_index("shard")
        core, near, low_bit = dp % 2, dp // 2 % 2, dp // 4 % 2
        near_peer, low_peer = (dp + 2 - 4 * near, shard), (dp + 4 - 8 * low_bit, shard)
        shard_peer, core_peer = (dp, 1 - shard), (dp + 1 - 2 * core, shard)
        masters, fulls = [master_out, master_gate_up, master_down], [full_out, full_gate_up, full_down]
        count = len(self.units)

        def region(u, stage):
            first, second = (near, low_bit) if u % 2 == 0 else (low_bit, near)
            side = shard if stage == 0 else 1 - shard
            height = (rows // 8, rows // 8, rows // 4, rows // 2)[stage]
            low = core * (rows // 2)
            if stage < 3:
                low += second * (rows // 4)
            if stage < 2:
                low += first * (rows // 8)
            if u < 3:
                place = pl.ds(pl.multiple_of(side * rows + low, 16), height)
                return qkv.at[u, place], qkv.at[u, place]
            matrix, first, left = self.units[u - 3]
            place = pl.ds(pl.multiple_of(side * self.matrices[matrix][0] + first + low, 16), height)
            full = fulls[matrix].at[place, pl.ds(left, width)]
            if stage == 0:
                return own_low.at[u - 3, pl.ds(pl.multiple_of(low, 16), height)], full
            return full, full

        def copy(u, stage):
            source, target = region(u, stage)
            return pltpu.make_async_remote_copy(
                src_ref=source,
                dst_ref=target,
                send_sem=pair_sem.at[stage, u, 0],
                recv_sem=pair_sem.at[stage, u, 1],
                device_id=peers_of(u)[stage],
                device_id_type=pl.DeviceIdType.MESH,
            )

        def peers_of(u):
            between = [near_peer, low_peer] if u % 2 == 0 else [low_peer, near_peer]
            return [shard_peer, *between, core_peer]

        def pass_on(u, stage):
            copy(u, stage - 1).wait_recv()
            copy(u, stage).start()

        def load(u):
            if u < 3:
                source = master_qkv.at[:, pl.ds(u * width, width)]
            else:
                matrix, first, left = self.units[u - 3]
                source = masters[matrix].at[pl.ds(first, rows), pl.ds(left, width)]
            return pltpu.make_async_copy(source, wide.at[u % 3], load_sem.at[u % 3])

        def own_rows(u):
            matrix, first, left = self.units[u - 3]
            place = pl.ds(pl.multiple_of(shard * self.matrices[matrix][0] + first, 16), rows)
            return pltpu.make_async_copy(
                own_low.at[u - 3], fulls[matrix].at[place, pl.ds(left, width)], own_sem.at[u - 3]
            )

        def round_unit(u):
            load(u).wait()
            target = qkv.at[u, pl.ds(pl.multiple_of(shard * rows, 16), rows)] if u < 3 else own_low.at[u - 3]

            @pl.loop(0, rows // 16)
            def _(i):
                span = pl.ds(pl.multiple_of(i * 16, 16), 16)
                target[span, :] = wide[u % 3, span, :].astype(bf16)

            if u + 3 < 3 + count:
                load(u + 3).start()
            if u >= 3:
                own_rows(u).start()

        def project(u):
            block = 4 * HEAD_DIM
            half = HEAD_DIM // 2
            for left in range(0, width, block):
                part = contract(qkv[u, :, left : left + block], tokens[...], 0, 1)
                if u == 2:
                    joined[u * width + left : u * width + left + block] = part.astype(bf16)
                    continue
                scale = 1.0 / math.sqrt(HEAD_DIM) if u == 0 else 1.0
                for low in range(0, block, HEAD_DIM):
                    t1, t2 = part[low : low + half], part[low + half : low + 2 * half]
                    cos, sin = cosine[...] * scale, sine[...] * scale
                    to = u * width + left + low
                    joined[to : to + half] = (t1 * cos - t2 * sin).astype(bf16)
                    joined[to + half : to + 2 * half] = (t2 * cos + t1 * sin).astype(bf16)

        def keep(i):
            if i == 3:
                return pltpu.make_async_copy(joined, joined_out, out_sem.at[3])
            return pltpu.make_async_copy(qkv.at[i], qkv_out.at[:, pl.ds(i * width, width)], out_sem.at[i])

        first_at = (6, 4, 2, -1)

        @pl.when(step == 0)
        def _():
            for u in range(3):
                load(u).start()
            barrier = pltpu.get_barrier_semaphore()
            for peer in peers_of(0):
                pl.semaphore_signal(barrier, inc=1, device_id=peer, device_id_type=pl.DeviceIdType.MESH)
            pl.semaphore_wait(barrier, len(peers_of(0)))
            for u in range(3):
                round_unit(u)
                copy(u, 0).start()
            for u in range(3, 7):
                round_unit(u)
            for stage in (1, 2):
                for u in range(3):
                    pass_on(u, stage)
                    if u < 2:
                        copy(3 + 2 * (stage - 1) + u, 0).start()
            for u in range(3):
                pass_on(u, 3)
            for u in range(3):
                copy(u, 3).wait_recv()
                project(u)
            for u in range(3, 1 + first_at[1]):
                pass_on(u, 1)
            for i in range(4):
                keep(i).start()

        for s in range(1, HEADS):

            @pl.when(step == s)
            def _(s=s):
                for stage in (3, 2, 1):
                    u = s + first_at[stage]
                    if 3 <= u < 3 + count:
                        pass_on(u, stage)
                if s + first_at[0] < 3 + count:
                    round_unit(s + first_at[0])
                    copy(s + first_at[0], 0).start()

        head = lambda part: joined.at[
            pl.ds(pl.multiple_of(part * width + step * HEAD_DIM, HEAD_DIM), HEAD_DIM)
        ]
        attend_head(head(0), head(1), head(2), mixed, weights)

        @pl.when(step == HEADS - 1)
        def _():
            for u in range(HEADS + first_at[0], 3 + count):
                round_unit(u)
                copy(u, 0).start()
            for stage in (1, 2, 3):
                for u in range(max(3, HEADS + first_at[stage]), 3 + count):
                    pass_on(u, stage)
            for u in range(3, 3 + count):
                copy(u, 3).wait_recv()
                own_rows(u).wait()
            for u in range(3 + count):
                for stage in range(4):
                    copy(u, stage).wait_send()
            for i in range(4):
                keep(i).wait()


def hand_out_kernel(*refs):
    count = len(refs) // 2
    for source, target in zip(refs[:count], refs[count:], strict=True):
        target[...] = source[...]


def hand_out(arrays):
    count = 16
    blocks = [pl.BlockSpec((array.shape[0] // count, array.shape[1]), lambda i: (i, 0)) for array in arrays]
    return pl.pallas_call(
        hand_out_kernel,
        grid=(count,),
        in_specs=blocks,
        out_specs=blocks,
        out_shape=[jax.ShapeDtypeStruct(array.shape, array.dtype) for array in arrays],
        compiler_params=params(),
        name="hand_out",
    )(*arrays)


class Back:
    ahead = 3
    steps = ("core", "shard", "near", "low", "high", "high total", "low total", "near total", "core total")
    update_cols = 384
    update_slots = 2

    def __init__(self, mesh, length, width, inner, rows, long_rows, runs):
        self.far_size = mesh.shape["dp"] // 4
        self.length, self.width, self.inner = length, width, inner
        self.rows, self.long_rows, self.runs = rows, long_rows, runs
        self.scale = 1.0 / math.sqrt(length * mesh.shape["dp"] * mesh.shape["shard"])
        self.run = inner // (2 * runs)
        self.units = [[("wide", j), ("down", j)] for j in range(runs)] + [[("square", u)] for u in range(4)]
        self.groups = {
            "wide": (runs, 2, rows, self.run),
            "down": (runs, 1, self.run, width // 2),
            "square": (4, 1, rows, width // 2),
        }
        self.early = len(EARLY_STEPS)
        self.entry = [0, 0, 1, 2, 2, 3, 1, 2, 4, 5, 6, 7, 8, 9, 10, 11]
        blocks, side = [], self.update_cols
        for part in range(2):
            for left in range(0, inner, side):
                first, last = (at * 2 * runs // inner for at in (left % (inner // 2), left % (inner // 2) + side))
                blocks.append((max(self.entry[first:last]), 0, 0, part * inner + left, side, (part, left)))
        for low in range(0, long_rows, rows):
            first, last = (at * runs // long_rows for at in (low, low + rows))
            blocks.append((max(self.entry[first:last]), 1, low, 0, width, (0, 0)))
        for u in range(3):
            blocks.append((self.entry[runs + u], 3, 0, u * width, width, (0, u * width)))
        blocks.append((self.entry[runs + 3], 2, 0, 0, width, (0, 0)))
        self.blocks = sorted(blocks, key=lambda block: block[0])

    def __call__(
        self,
        joined,
        weights,
        mixed,
        first_low,
        weight_out,
        cosine,
        sine,
        feed_sums,
        tokens,
        weight_qkv,
        grad_first,
        masters,
        norm_grads,
        norm_state,
    ):
        length, width, rows = self.length, self.width, self.rows
        anywhere = pl.BlockSpec(memory_space=pl.ANY)
        once = lambda array: pl.BlockSpec(
            array.shape, lambda h: (0,) * array.ndim, pipeline_mode=pl.Buffered(1)
        )
        head_rows = lambda part: pl.BlockSpec((HEAD_DIM, length), lambda h: (part * HEADS + h, 0))
        state = [part for master in masters for part in master]
        outs = []
        for master, _, _ in masters:
            full = (2 * master.shape[0], master.shape[1])
            outs += [
                jax.ShapeDtypeStruct(full, bf16),
                jax.ShapeDtypeStruct(master.shape, f32),
                jax.ShapeDtypeStruct(master.shape, f32),
            ]
        totals = [
            jax.ShapeDtypeStruct((2, rows, self.inner), bf16),
            jax.ShapeDtypeStruct((1, self.long_rows, width), bf16),
            jax.ShapeDtypeStruct((1, rows, width), bf16),
            jax.ShapeDtypeStruct((1, rows, 3 * width), bf16),
        ]
        norm_outs = [jax.ShapeDtypeStruct(norm_grads.shape, f32)] * 3
        dma = pltpu.SemaphoreType.DMA
        far = max(self.far_size - 1, 1)
        scratch = [
            pltpu.VMEM((width, length), bf16),
            pltpu.VMEM((3 * width, length), bf16),
            pltpu.VMEM((length, width), bf16),
            pltpu.VMEM((width, 3 * width), bf16),
            pltpu.VMEM((length, width), f32),
            pltpu.VMEM((4, 2, width, width // 2), bf16),
            pltpu.VMEM((4, 1, width, width // 2), bf16),
        ]
        for name, (count, lead, height, columns) in self.groups.items():
            slots = 1 if name == "square" else self.ahead + 1
            heights = [height // 2**i for i in range(4)]
            scratch += [pltpu.VMEM((count, lead, rows_left, columns), bf16) for rows_left in heights]
            scratch += [
                pltpu.VMEM((slots, lead, height if slots > 1 else 16, columns), bf16),
                dma((len(self.steps), count, 2)),
                dma((2, count)),
            ]
        slots = (self.update_slots, rows, self.update_cols)
        scratch += [
            pltpu.VMEM((3,) + slots, f32),
            pltpu.VMEM(slots, bf16),
            pltpu.VMEM((2,) + slots, f32),
            pltpu.VMEM(slots, bf16),
            pltpu.VMEM((3,) + norm_grads.shape, f32),
            pltpu.VMEM((self.far_size,) + norm_grads.shape, f32),
            dma((3 + far,)),
            dma((3 + far,)),
            dma((self.update_slots, 4)),
            dma((self.update_slots, 3)),
            dma((3, len(self.blocks), 2)),
            dma((4,)),
        ]
        results = pl.pallas_call(
            self.kernel,
            grid=(HEADS,),
            in_specs=[
                head_rows(0),
                head_rows(1),
                head_rows(2),
                pl.BlockSpec((1, length, length), lambda h: (h, 0, 0)),
                once(mixed),
                once(first_low),
                once(weight_out),
                once(cosine),
                once(sine),
                *[once(array) for array in (norm_grads, *norm_state)],
            ]
            + [anywhere] * (7 + len(state)),
            out_specs=[anywhere] * (len(outs) + len(totals)) + [whole(*norm_grads.shape)] * 3 + [anywhere],
            out_shape=outs + totals + norm_outs + [jax.ShapeDtypeStruct((length, width), bf16)],
            scratch_shapes=scratch,
            compiler_params=params(collective_id=1, has_side_effects=True),
            name="back",
        )(
            joined,
            joined,
            joined,
            weights,
            mixed,
            first_low,
            weight_out,
            cosine,
            sine,
            norm_grads,
            *norm_state,
            *feed_sums,
            tokens,
            weight_qkv,
            grad_first,
            *state,
        )
        copied = hand_out(results[: len(outs)])
        updated = [tuple(copied[3 * i : 3 * i + 3]) for i in range(len(masters))]
        return updated, tuple(results[-4:-1]), results[-1]

    def kernel(self, *refs):
        refs = list(refs)

        def take(number):
            taken = refs[:number]
            del refs[:number]
            return taken

        length, width, rows, sizes = self.length, self.width, self.rows, self.far_size
        queries, key_rows, value_rows, weights, mixed, first_low, weight_out, cosine, sine = take(9)
        norm_in, norms, norm_first, norm_second = take(4)
        wide_in, down_in, wide_shard_in, down_shard_in, tokens_in, qkv_in, grad_first_in = take(7)
        state = take(12)
        outs, totals, norm_outs, (input_grad,) = take(12), take(4), take(3), take(1)
        grad_mixed, grad_joined, tokens, weight_qkv, grad_first, square, square_sum = take(7)
        names = ("shard", "near", "low", "high", "keep", "pair_sem", "own_sem")
        groups = {name: dict(zip(names, take(7), strict=True)) for name in self.groups}
        load_buf, grad_buf, store_buf, new_buf, norm_sum, norm_far = take(6)
        norm_send, norm_recv, load_sem, store_sem, new_sem, in_sem = take(6)

        step = pl.program_id(0)
        dp, shard = lax.axis_index("dp"), lax.axis_index("shard")
        core, near, far = dp % 2, dp // 2 % 2, dp // 4
        low_bit, high_bit = far % 2, far // 2
        core_peer, near_peer, shard_peer = (dp + 1 - 2 * core, shard), (dp + 2 - 4 * near, shard), (dp, 1 - shard)

        def far_peer(hop):
            return (dp + ((far + hop) % sizes - far) * 4, shard)

        def remote(source, target, sent, came, peer):
            return pltpu.make_async_remote_copy(
                src_ref=source,
                dst_ref=target,
                send_sem=sent,
                recv_sem=came,
                device_id=peer,
                device_id_type=pl.DeviceIdType.MESH,
            )

        def span(low, height):
            return pl.ds(pl.multiple_of(low, 16), height)

        peers = {
            "core": core_peer,
            "shard": shard_peer,
            "near": near_peer,
            "low": (dp + 4 - 8 * low_bit, shard),
            "high": (dp + 8 - 16 * high_bit, shard),
        }
        bits = {"shard": shard, "near": near, "low": low_bit, "high": high_bit}
        axes = ["shard", "near", "low", "high"]

        class Part:
            def __init__(part, group, index):
                part.group, part.index = group, index
                _, part.lead, part.height, part.columns = self.groups[group]
                part.bufs = groups[group]
                part.held = group == "square"
                part.source = {"wide": wide_in, "down": down_in, "square": square_sum}[group].at[index]
                if part.held:
                    part.keep = part.source.at[:, span(shard * part.height, part.height)]
                else:
                    part.keep = part.bufs["keep"].at[index % (self.ahead + 1)]

            def came(part, axis):
                return part.bufs[axis].at[part.index]

            def rows_after(part, axis):
                low, height = 0, part.height
                for name in axes[1 : axes.index(axis) + 1]:
                    height //= 2
                    low = low + bits[name] * height
                return low, height

            def total(part, axis):
                low, height = part.rows_after(axis)
                index, side = part.index, core
                if part.group == "wide":
                    left = side * (self.inner // 2) + index * part.columns
                    return totals[0].at[:, span(low, height), pl.ds(pl.multiple_of(left, 128), part.columns)]
                left = pl.multiple_of(side * part.columns, 128)
                if part.group == "down":
                    return totals[1].at[:, span(index * part.height + low, height), pl.ds(left, part.columns)]
                if index == 3:
                    return totals[2].at[:, span(low, height), pl.ds(left, part.columns)]
                return totals[3].at[:, span(low, height), pl.ds(index * width + left, part.columns)]

            def copy(part, stage):
                axis, *back = stage.split()
                if back:
                    before = {"high": "high", "low": "low", "near": "near", "core": "shard"}[axis]
                    source = target = part.total(before)
                elif axis == "core":
                    source, target = square.at[part.index, pl.ds(1 - core, 1)], part.source
                else:
                    own = part.source if axis == "shard" else part.came(axes[axes.index(axis) - 1])
                    _, height = part.rows_after(axis)
                    source, target = own.at[:, span((1 - bits[axis]) * height, height)], part.came(axis)
                sem = part.bufs["pair_sem"].at[self.steps.index(stage), part.index]
                return remote(source, target, sem.at[0], sem.at[1], peers[axis])

            def kept(part):
                return pltpu.make_async_copy(
                    part.source.at[:, span(shard * part.height, part.height)],
                    part.keep,
                    part.bufs["own_sem"].at[0, part.index],
                )

            def shard_sum(part):
                source = {"wide": wide_shard_in, "down": down_shard_in}[part.group].at[part.index]
                return pltpu.make_async_copy(source, part.came("shard"), part.bufs["own_sem"].at[0, part.index])

            def own_total(part):
                return pltpu.make_async_copy(
                    part.came("high"), part.total("high"), part.bufs["own_sem"].at[1, part.index]
                )

        units = [[Part(group, index) for group, index in unit] for unit in self.units]
        started = []

        def start(k, stage):
            for part in units[k]:
                part.copy(stage).start()
            started.append((k, stage))

        def arrived(k, stage):
            for part in units[k]:
                part.copy(stage).wait_recv()

        def add_rows(target, sources, lead, height):
            tile = next(size for size in (64, 48, 16) if height % size == 0)

            @pl.loop(0, height // tile)
            def _(i):
                place = span(i * tile, tile)
                for k in range(lead):
                    value = sources[0][k, place, :].astype(f32)
                    for source in sources[1:]:
                        value += source[k, place, :].astype(f32)
                    target[k, place, :] = value.astype(bf16)

        def start_shard(k):
            for part in units[k]:
                if part.held:
                    arrived(k, "core")
                    own = square.at[part.index, pl.ds(core, 1)]
                    add_rows(part.source, [part.source, own], 1, 2 * part.height)
                else:
                    part.kept().start()
            start(k, "shard")

        def take_sum(k, axis):
            if axis == "shard" and k < self.early:
                for part in units[k]:
                    part.shard_sum().wait()
                start(k, "near")
                return
            arrived(k, axis)
            for part in units[k]:
                came = part.came(axis)
                if axis == "shard":
                    if not part.held:
                        part.kept().wait()
                    own = part.keep
                else:
                    _, height = part.rows_after(axis)
                    own = part.came(axes[axes.index(axis) - 1]).at[:, span(bits[axis] * height, height)]
                add_rows(came, [came, own], part.lead, came.shape[1])
            if axis != "high":
                start(k, axes[axes.index(axis) + 1])
                return
            for part in units[k]:
                part.own_total().start()
            for part in units[k]:
                part.own_total().wait()
            start(k, "high total")

        def take_total(k, axis):
            arrived(k, axis + " total")
            start(k, {"high": "low", "low": "near", "near": "core"}[axis] + " total")

        updates = [
            (b, sub) for b, block in enumerate(self.blocks) for sub in range(block[4] // self.update_cols)
        ]

        def update_place(n):
            b, sub = updates[n]
            _, matrix, low, left, _, (part, total_left) = self.blocks[b]
            shift = sub * self.update_cols
            cols = pl.ds(left + shift, self.update_cols)
            return n % self.update_slots, matrix, low, cols, part, pl.ds(total_left + shift, self.update_cols)

        def state_loads(n):
            slot, matrix, low, cols, *_ = update_place(n)
            place = pl.ds(low, rows)
            return [
                pltpu.make_async_copy(
                    state[3 * matrix + i].at[place, cols], load_buf.at[i, slot], load_sem.at[slot, i]
                )
                for i in range(3)
            ]

        def grad_load(n):
            slot, matrix, low, _, part, cols = update_place(n)
            grads = totals[matrix].at[part, pl.ds(low, rows), cols]
            return pltpu.make_async_copy(grads, grad_buf.at[slot], load_sem.at[slot, 3])

        def stores_of(n):
            slot, matrix, low, cols, *_ = update_place(n)
            place = pl.ds(low, rows)
            full = span(shard * state[3 * matrix].shape[0] + low, rows)
            return [
                pltpu.make_async_copy(new_buf.at[slot], outs[3 * matrix].at[full, cols], store_sem.at[slot, 2])
            ] + [
                pltpu.make_async_copy(
                    store_buf.at[i, slot], outs[3 * matrix + 1 + i].at[place, cols], store_sem.at[slot, i]
                )
                for i in range(2)
            ]

        waiting = {}

        def load_state(n):
            if n < len(updates):
                for copy in state_loads(n):
                    copy.start()

        def settle(n, left):
            while len(waiting[n]) > left:
                waiting[n].pop(0).wait()

        def update(n):
            slot = n % self.update_slots
            for copy in [*state_loads(n), grad_load(n)]:
                copy.wait()
            if n >= self.update_slots:
                settle(n - self.update_slots, 0)

            @pl.loop(0, rows // 16)
            def _(i):
                place = span(i * 16, 16)
                new, first_new, second_new = adam_update(
                    load_buf[0, slot, place, :],
                    load_buf[1, slot, place, :],
                    load_buf[2, slot, place, :],
                    grad_buf[slot, place, :].astype(f32) * self.scale,
                    learn_rate,
                    decay_rate,
                )
                store_buf[0, slot, place, :] = first_new
                store_buf[1, slot, place, :] = second_new
                new_buf[slot, place, :] = new.astype(bf16)

            waiting[n] = stores_of(n)
            for copy in waiting[n]:
                copy.start()
            load_state(n + self.update_slots)

        def new_copy(b, stage):
            _, matrix, first, left, columns, _ = self.blocks[b]
            side = shard if stage == 0 else 1 - shard
            height = rows // 4 if stage < 2 else rows // 2
            by_near = b % 4 == 0
            quarter = near if by_near else low_bit
            low = core * (rows // 2) + (quarter * (rows // 4) if stage < 2 else 0)
            place = outs[3 * matrix].at[
                span(side * state[3 * matrix].shape[0] + first + low, height), pl.ds(left, columns)
            ]
            peer = (shard_peer, near_peer if by_near else peers["low"], core_peer)[stage]
            return remote(place, place, new_sem.at[stage, b, 0], new_sem.at[stage, b, 1], peer)

        def pass_new(b, stage):
            if stage > 0:
                new_copy(b, stage - 1).wait_recv()
            new_copy(b, stage).start()

        def norm_copy(stage, hop=0):
            if stage < 3:
                source = norm_in if stage == 0 else norm_sum.at[stage - 1]
                peer = (core_peer, shard_peer, near_peer)[stage]
                return remote(source, norm_sum.at[stage], norm_send.at[stage], norm_recv.at[stage], peer)
            return remote(
                norm_sum.at[2], norm_far.at[far], norm_send.at[2 + hop], norm_recv.at[2 + hop], far_peer(hop)
            )

        def norm_stage(stage):
            if 1 <= stage <= 3:
                norm_copy(stage - 1).wait_recv()
                before = norm_in[...] if stage == 1 else norm_sum[stage - 2]
                norm_sum[stage - 1] += before
            if stage < 3:
                norm_copy(stage).start()
            elif stage == 3:
                norm_far[far] = norm_sum[2]
                for hop in range(1, sizes):
                    norm_copy(3, hop).start()
            else:
                for hop in range(1, sizes):
                    norm_copy(3, hop).wait_recv()
                total = norm_far[0]
                for place in range(1, sizes):
                    total += norm_far[place]
                new, first_new, second_new = adam_update(
                    norms[...], norm_first[...], norm_second[...], total * self.scale, norm_rate, 0.0
                )
                norm_outs[0][...] = new
                norm_outs[1][...] = first_new
                norm_outs[2][...] = second_new
                for stage in range(3):
                    norm_copy(stage).wait_send()
                for hop in range(1, sizes):
                    norm_copy(3, hop).wait_send()

        count, runs = len(self.units), self.runs
        stages = [functools.partial(take_sum, axis=axis) for axis in axes] + [
            functools.partial(take_total, axis=axis) for axis in ("high", "low", "near")
        ]
        depth = len(stages)
        progress = {"ready": 0, "grad": 0, "update": 0, "near": 0, "core": 0}
        sent_at, near_at = [], []

        def prefetch():
            n = progress["grad"]
            if n < progress["ready"] and n < progress["update"] + self.update_slots:
                grad_load(n).start()
                progress["grad"] += 1

        def some_updates(t, most):
            for _ in range(most):
                n = progress["update"]
                if n == progress["ready"]:
                    break
                for _ in range(self.update_slots):
                    prefetch()
                update(n)
                progress["update"] += 1
                b, sub = updates[n]
                if sub == self.blocks[b][4] // self.update_cols - 1:
                    for m in range(n - sub, n + 1):
                        settle(m, 2)
                    pass_new(b, 0)
                    sent_at.append(t)

        def entering(t):
            return [k for k in range(count) if self.entry[k] == t]

        def sending(t):
            ahead = [self.ahead if k < runs else self.ahead - 1 for k in range(count)]
            return [k for k in range(self.early, count) if self.entry[k] - ahead[k] == t]

        slots = max(self.entry) + 1

        def slot(t, most):
            busy = t < slots + depth
            for at, lag, stage, name in ((near_at, 2, 2, "core"), (sent_at, 3, 1, "near")):
                while progress[name] < len(at) and at[progress[name]] <= t - (lag if busy else 1):
                    pass_new(progress[name], stage)
                    progress[name] += 1
                    if stage == 1:
                        near_at.append(t)
            for k in entering(t - depth - 1):
                arrived(k, "core total")
            progress["ready"] = sum(self.blocks[b][0] <= t - depth - 1 for b, _ in updates)
            prefetch()
            for late in range(depth - 1, 0, -1):
                for k in entering(t - late - 1):
                    stages[late](k)
            some_updates(t, most)
            for k in entering(t):
                stages[0](k)
            for k in sending(t):
                start_shard(k)

        inputs = [
            pltpu.make_async_copy(tokens_in, tokens, in_sem.at[0]),
            pltpu.make_async_copy(qkv_in, weight_qkv, in_sem.at[1]),
            pltpu.make_async_copy(grad_first_in, grad_first, in_sem.at[2]),
        ]

        @pl.when(step == 0)
        def _():
            greeted = [core_peer, near_peer, shard_peer] + [far_peer(hop) for hop in range(1, sizes)]
            barrier = pltpu.get_barrier_semaphore()
            for peer in greeted:
                pl.semaphore_signal(barrier, inc=1, device_id=peer, device_id_type=pl.DeviceIdType.MESH)
            pl.semaphore_wait(barrier, len(greeted))
            for t in range(-self.ahead, 0):
                for k in sending(t):
                    start_shard(k)
            for k in range(self.early):
                for part in units[k]:
                    part.shard_sum().start()
            norm_stage(0)
            for copy in inputs:
                copy.start()
            for n in range(self.update_slots):
                load_state(n)
            block = 256
            for low in range(0, width, block):
                grad_mixed[low : low + block] = contract(
                    weight_out[low : low + block], first_low[...], 1, 1
                ).astype(bf16)

        head = lambda part: grad_joined.at[
            pl.ds(pl.multiple_of(part * width + step * HEAD_DIM, HEAD_DIM), HEAD_DIM)
        ]
        own_head = pl.ds(pl.multiple_of(step * HEAD_DIM, HEAD_DIM), HEAD_DIM)
        attend_back_kernel(
            min(256, length),
            queries,
            key_rows,
            value_rows,
            mixed.at[own_head],
            grad_mixed.at[own_head],
            weights,
            cosine,
            sine,
            head(0),
            head(1),
            head(2),
        )

        early = {1: 0, 3: 1, 5: 2, 7: 3, 9: 4, 11: 5}
        for at, t in early.items():

            @pl.when(step == at)
            def _(t=t):
                if t < 3:
                    norm_stage(1 + t)
                slot(t, 0)

        @pl.when(step == HEADS - 1)
        def _():
            half = width // 2
            t = len(early)

            def keep_square(u, value):
                square[u, 0] = value[:, :half].astype(bf16)
                square[u, 1] = value[:, half:].astype(bf16)

            def weight_grad(u):
                keep_square(u, contract(tokens[...], grad_joined[u * width : (u + 1) * width], 0, 1))

            def input_rows(low, height):
                for place in range(low, low + height, min(256, length)):
                    block = slice(place, place + min(256, length))
                    rows_sum = contract(grad_joined[:, block], weight_qkv[...], 0, 1)
                    tokens[block] = (grad_first[block] + rows_sum).astype(bf16)

            inputs[0].wait()
            for u in range(3):
                weight_grad(u)
            keep_square(3, contract(mixed[...], first_low[...], 1, 0))
            for u in range(4):
                start(runs + u, "core")
            slot(t, 0)
            norm_stage(4)
            inputs[1].wait()
            inputs[2].wait()
            input_rows(0, length // 2)
            slot(t + 1, 0)
            input_rows(length // 2, length // 2)
            result = pltpu.make_async_copy(tokens, input_grad, in_sem.at[3])
            result.start()
            later = t + 2
            while later < slots + depth + 1 or progress["core"] < len(self.blocks):
                slot(later, 3)
                later += 1
            for b in range(len(self.blocks)):
                new_copy(b, 2).wait_recv()
            for n in range(len(updates)):
                settle(n, 0)
            for k, stage in started:
                for part in units[k]:
                    part.copy(stage).wait_send()
            for b in range(len(self.blocks)):
                for stage in range(3):
                    new_copy(b, stage).wait_send()
            result.wait()


def shards(
    mesh,
    tokens,
    cotangent,
    master_qkv,
    first_qkv,
    second_qkv,
    master_out,
    first_out,
    second_out,
    master_gate_up,
    first_gate_up,
    second_gate_up,
    master_down,
    first_down,
    second_down,
    norms,
    norm_first,
    norm_second,
):
    links = Links(mesh)
    length, width = tokens.shape
    shard_count = mesh.shape["shard"]
    cosine, sine = rope_tables(length)

    scale_grad = 1.0 / math.sqrt(length * mesh.shape["dp"] * shard_count)
    masters = [
        (master_gate_up, first_gate_up, second_gate_up),
        (master_down, first_down, second_down),
        (master_out, first_out, second_out),
        (master_qkv, first_qkv, second_qkv),
    ]
    norm_state = (norms, norm_first, norm_second)
    if fits(mesh, length, master_qkv.shape[0], master_down.shape[0]):
        rows, long_rows = master_qkv.shape[0], master_down.shape[0]
        inner = shard_count * long_rows
        shapes = [master_out.shape, master_gate_up.shape, master_down.shape]
        mixed, weights, joined, weight_qkv, weight_out, weight_gate_up, weight_down = Front(
            mesh, length, width, rows, shapes
        )(tokens, [master_qkv, master_out, master_gate_up, master_down], cosine, sine)
        normed_one, inverse_one, hidden_low = project_out(tokens, mixed, weight_out, norms)
        gate, up, output, grad_second, grad_low, norm_two = paired_forward(
            hidden_low, weight_gate_up, weight_down, normed_one, norms, cotangent
        )
        wide, down, wide_shard, down_shard, grad_first, first_low, norm_one = paired_backward(
            grad_low,
            hidden_low,
            gate,
            up,
            weight_gate_up,
            weight_down,
            grad_second,
            normed_one,
            inverse_one,
            norms,
        )
        updated, updated_norms, input_grad = Back(
            mesh, length, width, inner, rows, long_rows, gate.shape[0]
        )(
            joined,
            weights,
            mixed,
            first_low,
            weight_out,
            cosine,
            sine,
            [wide, down, wide_shard, down_shard],
            tokens,
            weight_qkv,
            grad_first,
            masters,
            jnp.concatenate([norm_one, norm_two]),
            norm_state,
        )
    else:
        weight_qkv = links.gather_rows(master_qkv.astype(bf16), False)
        weight_out = links.gather_rows(master_out.astype(bf16), False)
        weight_gate_up = links.gather_rows(master_gate_up.astype(bf16), True)
        weight_down = links.gather_rows(master_down.astype(bf16), True)
        joined = project_qkv(tokens, weight_qkv, cosine, sine)
        mixed, weights = attend_forward(joined)
        normed_one, inverse_one, hidden_low = project_out(tokens, mixed, weight_out, norms)
        gate, up, output, grad_second, grad_low, norm_two = feed_forward(
            hidden_low, weight_gate_up, weight_down, normed_one, norms, cotangent
        )
        gate_grad, up_grad, down_grad, grad_first, first_low, norm_one = feed_backward(
            grad_low,
            hidden_low,
            gate,
            up,
            weight_gate_up,
            weight_down,
            grad_second,
            normed_one,
            inverse_one,
            norms,
        )
        out_grad = contract(mixed, first_low, 1, 0).astype(bf16)
        mixed_grad = contract(weight_out, first_low, 1, 1).astype(bf16)
        joined_back = attend_backward(joined, mixed, mixed_grad, weights, cosine, sine)
        joined_back = jnp.concatenate(joined_back, axis=0)
        qkv_grad = contract(tokens, joined_back, 0, 1).astype(bf16)
        input_grad = (grad_first + contract(joined_back, weight_qkv, 0, 1)).astype(bf16)
        totals = [
            jnp.concatenate([links.total(gate_grad), links.total(up_grad)], axis=1),
            links.total(down_grad),
            links.total(out_grad),
            links.total(qkv_grad),
        ]
        updated = []
        for (master, first, second), total in zip(masters, totals, strict=True):
            new, first_new, second_new = adam_update(
                master, first, second, total.astype(f32) * scale_grad, learn_rate, decay_rate
            )
            updated.append((links.gather_rows(new.astype(bf16), True), first_new, second_new))
        norm_total = lax.psum(jnp.concatenate([norm_one, norm_two]), ("dp", "shard"))
        updated_norms = adam_update(*norm_state, norm_total * scale_grad, norm_rate, 0.0)
    (
        (full_gate_up, first_gate_up_new, second_gate_up_new),
        (full_down, first_down_new, second_down_new),
        (full_out, first_out_new, second_out_new),
        (full_qkv, first_qkv_new, second_qkv_new),
    ) = updated
    upd_norms, norm_first_new, norm_second_new = updated_norms
    return (
        output,
        input_grad,
        full_qkv,
        full_out,
        full_gate_up,
        full_down,
        first_qkv_new,
        second_qkv_new,
        first_out_new,
        second_out_new,
        first_gate_up_new,
        second_gate_up_new,
        first_down_new,
        second_down_new,
        upd_norms,
        norm_first_new,
        norm_second_new,
    )


def solution(mesh):
    rows, split, copied = P(("dp", "shard"), None), P("shard", None), P()
    return jax.shard_map(
        functools.partial(shards, mesh),
        mesh=mesh,
        in_specs=(rows, rows) + (split,) * 12 + (copied,) * 3,
        out_specs=(rows, rows) + (copied,) * 4 + (split,) * 8 + (copied,) * 3,
        check_vma=False,
    )
```
